32 devices in a mesh: seq: 4 (over x, core), shard: 8 (over z, y).
Axes of the slice: x: 2, y: 2, z: 4, core: 2. Of those that a mesh axis runs over, the one named last changes fastest.
Arguments:
- inputs: bfloat16 [8, 512, 2048], P('shard', 'seq'), may hold values from -6 to 6
- seq_ids: int32 [8, 512], P('shard', 'seq'), may hold values from 0 to 2, as said below
- routes: int32 [8, 512, 8], P('shard', 'seq'), may hold values from 0 to 31, all different within a row; in each aligned block of 128 rows (0 to 127, 128 to 255, ..., all dimensions but the last counted through in order) at most 40 rows name the same one
- norm1_gain: bfloat16 [2048], P('shard'), may hold values from 0.5 to 1.5
- w_query: bfloat16 [2048, 4096], P('shard'), may hold values from -0.125 to 0.125
- key_weight: bfloat16 [2048, 512], P('shard'), may hold values from -0.125 to 0.125
- value_weight: bfloat16 [2048, 512], P('shard'), may hold values from -0.125 to 0.125
- q_gain: bfloat16 [128], P('shard'), may hold values from 0.796875 to 1.59375
- k_gain: bfloat16 [128], P('shard'), may hold values from 0.5 to 1.5
- w_out: bfloat16 [4096, 2048], P('shard'), may hold values from -1.5 to 1.5
- norm2_gain: bfloat16 [2048], P('shard'), may hold values from 0.5 to 1.5
- w_router: bfloat16 [2048, 32], P('shard'), may hold values from -0.0625 to 0.0625
- w_gate: bfloat16 [32, 2048, 768], P(('seq', 'shard')), may hold values from -0.125 to 0.125
- w_up: bfloat16 [32, 2048, 768], P(('seq', 'shard')), may hold values from -0.125 to 0.125
- w_down: bfloat16 [32, 768, 2048], P(('seq', 'shard')), may hold values from -0.875 to 0.875
- cotangent: bfloat16 [8, 512, 2048], P('shard', 'seq'), may hold values from -6 to 6
Outputs:
- output: bfloat16 [8, 512, 2048], P('shard', 'seq')
- grad_inputs: float32 [8, 512, 2048], P('shard', 'seq')
- grad_norm1_gain: float32 [2048], P('shard')
- grad_w_query: float32 [2048, 4096], P('shard')
- grad_w_key: float32 [2048, 512], P('shard')
- grad_w_value: float32 [2048, 512], P('shard')
- grad_q_gain: float32 [128], P('shard')
- grad_k_gain: float32 [128], P('shard')
- grad_w_out: float32 [4096, 2048], P('shard')
- grad_norm2_gain: float32 [2048], P('shard')
- grad_w_router: float32 [2048, 32], P('shard')
- grad_w_gate: float32 [32, 2048, 768], P(('seq', 'shard'))
- grad_w_up: float32 [32, 2048, 768], P(('seq', 'shard'))
- grad_w_down: float32 [32, 768, 2048], P(('seq', 'shard'))
The draws below stay inside these ranges and needn't reach their ends.
Inputs may be any that keep to these rules, and one draw needn't show every extreme that they name: `seq_ids`: along each row the ids form three runs 0, 1, 2 in this order; the run of 0 has 1 to 64 tokens, the run of 2 has 1 to 64 tokens. `routes`: among the 128 tokens of one device no expert is named more than 40 times; some expert is named exactly 40 times.
All inputs are finite; a program needn't handle non-finite values.
Results may differ from the reference program's by a relative error of at most 0.024.
Values may be sent and summed in bfloat16 or wider, within the bound.
No kernel may reach another device: no remote copies, remote signals or barrier semaphores. Data moves between devices by JAX's collectives and lax.ppermute only.
A program may use at most 256 MiB of HBM per device.

```python
import math
import jax
import jax.numpy as jnp
import numpy as np
from jax import lax

MODEL_DIMENSION = 2048
HQ = 32
KEY_VALUE_HEADS = 4
HEAD_DIMENSION = 128
FF = 768
TOPK = 8
TOK_DEV = 128
LENGTH = 512
ROWS = 8
EXPERTS = 32
CAP = 40
RECV = 1280
N_SEQ = 4


def draw_seq_ids(key, part):
    key = jax.random.fold_in(key, 7)
    key_first, key_last = jax.random.split(key)
    first_end = jax.random.randint(key_first, (ROWS, 1), 1, TOK_DEV // 2 + 1)
    last_begin = jax.random.randint(key_last, (ROWS, 1), LENGTH - TOK_DEV // 2, LENGTH)
    positions = jnp.arange(LENGTH, dtype=jnp.int32)[None, :]
    return (positions >= first_end).astype(jnp.int32) + (positions >= last_begin).astype(jnp.int32)


def shard_levels(rng, dims, cuts, low, largest):
    def one(position, parts):
        draws = jax.random.uniform(jax.random.fold_in(jax.random.fold_in(rng, 6), position), (parts,), jnp.float32, low / len(cuts), largest / len(cuts))
        return jnp.repeat(jnp.exp(draws), dims[position] // parts).reshape((-1,) + (1,) * (len(dims) - position - 1))

    loudness = one(*cuts[0])
    for cut in cuts[1:]:
        loudness = loudness * one(*cut)
    return loudness


def assign_block(key, own, number, rows, amount, top, most, slope):
    ranking = jax.random.permutation(key, amount)
    crowded, ordinary = load_shares(amount, rows * top, most, slope, True), load_shares(amount, rows * top, most, slope, False)
    places = jnp.arange(amount)

    def named(sizes, offset_by):
        used = int((sizes > 0).sum())
        fixed = max(1, used // 4)
        passed = fixed + (places - fixed + offset_by * (used - fixed)) % max(1, amount - fixed)
        return jnp.zeros((amount,), jnp.int32).at[ranking[jnp.where(places < fixed, places, passed)]].set(jnp.asarray(sizes, jnp.int32))

    sizes = jnp.where(number % 4 == 0, named(crowded, number // 4), named(ordinary, number - number // 4 - 1))
    mixed = jax.random.permutation(jax.random.fold_in(own, 3), amount)
    donor, taker = mixed[0:amount // 2 * 2:2], mixed[1:amount // 2 * 2:2]
    room = jnp.minimum(sizes[donor] - 1, most - sizes[taker]) // 2
    room = jnp.where((donor == ranking[0]) | (taker == ranking[0]) | (sizes[taker] == 0), 0, jnp.maximum(room, 0))
    passed = jax.random.randint(jax.random.fold_in(own, 4), (amount // 2,), 0, 1 << 20) % (room + 1)
    sizes = sizes.at[donor].add(-passed).at[taker].add(passed)
    members = jnp.searchsorted(jnp.cumsum(sizes), jnp.arange(rows * top), side="right").astype(jnp.int32)
    grid = members.reshape(top, rows).T
    grid = grid[jax.random.permutation(jax.random.fold_in(own, 1), rows)]
    offset_by = jax.random.randint(jax.random.fold_in(own, 2), (rows, 1), 0, top)
    return jnp.take_along_axis(grid, (jnp.arange(top)[None, :] + offset_by) % top, axis=1)


def load_shares(number_of, total, most, skew, full):
    loads = [(1 << 20) // math.isqrt(grade ** skew) + 1 for grade in range(1, number_of + 1)]
    largest = most if full else min(most, max(-(-total // number_of), total * loads[0] // sum(loads)))
    least = 1 if total - largest >= number_of - 1 else 0
    given, surplus = [largest] + [least] * (number_of - 1), total - largest - least * (number_of - 1)
    while surplus > 0:
        movable = [i for i in range(1, number_of) if given[i] < largest] or [i for i in range(1, number_of) if given[i] < most]
        whole, budget = sum([loads[i] for i in movable]), surplus
        for i in movable:
            addition = min(most - given[i], max(1, budget * loads[i] // whole), surplus)
            given[i] = given[i] + addition
            surplus = surplus - addition
    return np.array(given)


def noise(own_key, extent, deviation, bound, cuts=(), held_as=jnp.bfloat16):
    result = deviation * jax.random.normal(own_key, extent, jnp.float32)
    if cuts:
        result = result * shard_levels(own_key, extent, cuts, -0.22, 0.18)
    return jnp.clip(result, -bound, bound).astype(held_as)


def setup_inputs(seed: int = 0) -> dict:
    seeds = jax.random.split(jax.random.key(seed), 17)
    inputs = noise(seeds[0], (ROWS, LENGTH, MODEL_DIMENSION), 1.0, 6.0, ((0, 8), (1, 4)))
    seq_ids = draw_seq_ids(jax.random.fold_in(seeds[16], 71), 0)
    routes_keys = jax.random.split(jax.random.fold_in(seeds[2], 1), ROWS * LENGTH // TOK_DEV)
    routes_turns = jax.random.permutation(jax.random.fold_in(seeds[2], 3), ROWS * LENGTH // TOK_DEV)
    routes = jax.vmap(lambda own, number: assign_block(jax.random.fold_in(seeds[2], 2), own, number, TOK_DEV, EXPERTS, TOPK, CAP, 1))(routes_keys, routes_turns).reshape((ROWS, LENGTH, TOPK))
    norm1_gain = jnp.clip(1.0 + 0.1 * jax.random.normal(seeds[3], (MODEL_DIMENSION,), jnp.float32), 0.5, 1.5).astype(jnp.bfloat16)
    w_query = noise(seeds[4], (MODEL_DIMENSION, HQ * HEAD_DIMENSION), MODEL_DIMENSION ** -0.5, 0.125, ((0, 8),))
    key_weight = noise(seeds[5], (MODEL_DIMENSION, KEY_VALUE_HEADS * HEAD_DIMENSION), MODEL_DIMENSION ** -0.5, 0.125, ((0, 8),))
    value_weight = noise(seeds[6], (MODEL_DIMENSION, KEY_VALUE_HEADS * HEAD_DIMENSION), MODEL_DIMENSION ** -0.5, 0.125, ((0, 8),))
    q_gain = jnp.clip(0.796875 + 0.796875 * jax.random.uniform(seeds[7], (HEAD_DIMENSION,), jnp.float32) ** shard_levels(seeds[7], (HEAD_DIMENSION,), ((0, 8),), -0.2, 0.2), 0.796875, 1.59375).astype(jnp.bfloat16)
    k_gain = jnp.clip(1.0 + 0.1 * jax.random.normal(seeds[8], (HEAD_DIMENSION,), jnp.float32), 0.5, 1.5).astype(jnp.bfloat16)
    w_out = noise(seeds[9], (HQ * HEAD_DIMENSION, MODEL_DIMENSION), (HQ * HEAD_DIMENSION // 256) ** -0.5, 1.5, ((0, 8),))
    norm2_gain = jnp.clip(1.0 + 0.1 * jax.random.normal(seeds[10], (MODEL_DIMENSION,), jnp.float32), 0.5, 1.5).astype(jnp.bfloat16)
    w_router = noise(seeds[11], (MODEL_DIMENSION, EXPERTS), (4 * MODEL_DIMENSION) ** -0.5, 0.0625, ((0, 8),))
    w_gate = noise(seeds[12], (EXPERTS, MODEL_DIMENSION, FF), MODEL_DIMENSION ** -0.5, 0.125, ((0, 32),))
    w_up = noise(seeds[13], (EXPERTS, MODEL_DIMENSION, FF), MODEL_DIMENSION ** -0.5, 0.125, ((0, 32),))
    w_down = noise(seeds[14], (EXPERTS, FF, MODEL_DIMENSION), (FF // 16) ** -0.5, 0.875, ((0, 32),))
    cotangent = noise(seeds[15], (ROWS, LENGTH, MODEL_DIMENSION), 1.0, 6.0, ((0, 8), (1, 4)))
    return {"inputs": inputs, "seq_ids": seq_ids, "routes": routes, "norm1_gain": norm1_gain, "w_query": w_query, "key_weight": key_weight, "value_weight": value_weight, "q_gain": q_gain, "k_gain": k_gain, "w_out": w_out, "norm2_gain": norm2_gain, "w_router": w_router, "w_gate": w_gate, "w_up": w_up, "w_down": w_down, "cotangent": cotangent}


EPSILON = 1e-06
ROPE_BASE = 1000000.0
NEGATIVE = -1e+30
EXACT_PRECISION = lax.Precision.HIGHEST

@jax.custom_vjp
def reduced_precision(v):
    return lax.optimization_barrier(v.astype(jnp.bfloat16)).astype(jnp.float32)

@jax.custom_vjp
def reduced_backward(v):
    return v

def low_keep(v):
    return (reduced_precision(v), None)

def low_pass(kept, grad):
    return (grad,)

def back_keep(v):
    return (v, None)

def back_low(kept, grad):
    return (reduced_precision(grad),)
reduced_precision.defvjp(low_keep, low_pass)
reduced_backward.defvjp(back_keep, back_low)

def rope_tables(positions, head_size):
    half_size = head_size // 2
    inverse = ROPE_BASE ** (-2.0 * jnp.arange(half_size, dtype=jnp.float32) / head_size)
    angles = positions.astype(jnp.float32)[:, None] * inverse[None, :]
    return (jnp.cos(angles), jnp.sin(angles))

def apply_rotary(values, cosine_table, sine_values):
    half_size = values.shape[-1] // 2
    first_half = values[..., :half_size]
    second_half = values[..., half_size:]
    cos_b = cosine_table[:, None, :]
    sin_b = sine_values[:, None, :]
    return jnp.concatenate([first_half * cos_b - second_half * sin_b, second_half * cos_b + first_half * sin_b], axis=-1)

def root_mean_scale(values):
    return lax.rsqrt(lax.optimization_barrier(jnp.mean(values * values, axis=-1, keepdims=True)) + EPSILON)

def route_tables(routes):
    flat_routes = routes.reshape(-1).astype(jnp.int32)
    assign_count = flat_routes.shape[0]
    sort_order = jnp.argsort(flat_routes, stable=True).astype(jnp.int32)
    ordered = flat_routes[sort_order]
    first_at = jnp.searchsorted(ordered, jnp.arange(EXPERTS, dtype=jnp.int32)).astype(jnp.int32)
    slot_rank = jnp.arange(assign_count, dtype=jnp.int32) - first_at[ordered]
    placed = ordered * RECV + slot_rank
    slot_of = jnp.zeros((assign_count,), jnp.int32).at[sort_order].set(placed)
    owners = jnp.zeros((EXPERTS * RECV,), jnp.int32).at[placed].set(sort_order // TOPK)
    filled = jnp.zeros((EXPERTS * RECV,), jnp.float32).at[placed].set(1.0)
    return (owners.reshape(EXPERTS, RECV), filled.reshape(EXPERTS, RECV), slot_of)

def attend_row(queries, keys, values, row_ids):
    keys_full = jnp.repeat(keys, HQ // N_SEQ, axis=1)
    values_full = jnp.repeat(values, HQ // N_SEQ, axis=1)
    block_rows = min(512, LENGTH)
    block_count = LENGTH // block_rows
    query_blocks = queries.reshape(block_count, block_rows, HQ, HEAD_DIMENSION)
    starts = jnp.arange(block_count, dtype=jnp.int32) * block_rows

    def one_block(pieces):
        query_block, first_row = pieces
        scores = jnp.einsum('qhd,khd->hqk', query_block, keys_full, precision=EXACT_PRECISION) * HEAD_DIMENSION ** (-0.5)
        scores = reduced_backward(scores)
        query_pos = first_row + jnp.arange(block_rows, dtype=jnp.int32)
        key_pos = jnp.arange(LENGTH, dtype=jnp.int32)
        query_ids = lax.dynamic_slice_in_dim(row_ids, first_row, block_rows)
        allowed = (key_pos[None, :] <= query_pos[:, None]) & (query_ids[:, None] == row_ids[None, :])
        scores = jnp.where(allowed[None], scores, NEGATIVE)
        weights_bf = reduced_precision(jax.nn.softmax(scores, axis=-1))
        return jnp.einsum('hqk,khd->qhd', weights_bf, values_full, precision=EXACT_PRECISION)
    return lax.map(jax.checkpoint(one_block), (query_blocks, starts)).reshape(LENGTH, HQ, HEAD_DIMENSION)

def one_row(pieces):
    return attend_row(pieces[0], pieces[1], pieces[2], pieces[3])

def one_expert(pieces):
    rows_in, gate_e, up_e, down_e = pieces
    gate_pre = reduced_backward(jnp.dot(rows_in, gate_e, precision=EXACT_PRECISION))
    up_pre = reduced_backward(jnp.dot(rows_in, up_e, precision=EXACT_PRECISION))
    hidden = reduced_precision(jax.nn.silu(gate_pre) * up_pre)
    return reduced_backward(reduced_precision(jnp.dot(hidden, down_e, precision=EXACT_PRECISION)))

def reference(inputs, seq_ids, routes, norm1_gain, w_query, key_weight, value_weight, q_gain, k_gain, w_out, norm2_gain, w_router, w_gate, w_up, w_down, cotangent):
    owners, filled, slot_of = route_tables(routes)
    flat_routes = routes.reshape(-1, TOPK).astype(jnp.int32)

    def forward(x_float, gain_one, query_w, key_matrix, value_matrix, qgain_w, key_gain_matrix, out_w, gain_two, router_w, gate_w, up_w, down_w):
        tokens_flat = x_float.reshape(-1, MODEL_DIMENSION)
        normed_one = tokens_flat * root_mean_scale(tokens_flat)
        first_hidden = reduced_precision(normed_one * gain_one)
        q_raw = reduced_backward(jnp.dot(first_hidden, query_w, precision=EXACT_PRECISION)).reshape(-1, HQ, HEAD_DIMENSION)
        key_projected = reduced_backward(jnp.dot(first_hidden, key_matrix, precision=EXACT_PRECISION)).reshape(-1, KEY_VALUE_HEADS, HEAD_DIMENSION)
        value_projected = reduced_backward(jnp.dot(first_hidden, value_matrix, precision=EXACT_PRECISION)).reshape(-1, KEY_VALUE_HEADS, HEAD_DIMENSION)
        positions = jnp.tile(jnp.arange(LENGTH, dtype=jnp.int32), ROWS)
        cosine_table, sine_values = rope_tables(positions, HEAD_DIMENSION)
        q_slots = reduced_backward(reduced_precision(apply_rotary(q_raw * root_mean_scale(q_raw) * qgain_w, cosine_table, sine_values)))
        key_slot_rows = reduced_backward(jnp.repeat(reduced_precision(apply_rotary(key_projected * root_mean_scale(key_projected) * key_gain_matrix, cosine_table, sine_values)), N_SEQ // KEY_VALUE_HEADS, axis=1))
        value_slot_rows = reduced_backward(jnp.repeat(reduced_precision(value_projected), N_SEQ // KEY_VALUE_HEADS, axis=1))
        attended = lax.map(one_row, (q_slots.reshape(ROWS, LENGTH, HQ, HEAD_DIMENSION), key_slot_rows.reshape(ROWS, LENGTH, N_SEQ, HEAD_DIMENSION), value_slot_rows.reshape(ROWS, LENGTH, N_SEQ, HEAD_DIMENSION), seq_ids))
        attn_low = reduced_backward(reduced_precision(attended.reshape(-1, HQ * HEAD_DIMENSION)))
        x_second = tokens_flat + reduced_backward(jnp.dot(attn_low, out_w, precision=EXACT_PRECISION))
        hidden_two = reduced_precision(x_second * root_mean_scale(x_second) * gain_two)
        logits = jnp.dot(hidden_two, router_w, precision=EXACT_PRECISION)
        gate_probs = jax.nn.softmax(jnp.take_along_axis(logits, flat_routes, axis=1), axis=-1)
        expert_rows = reduced_backward(hidden_two[owners]) * filled[:, :, None]
        expert_out = lax.map(jax.checkpoint(one_expert), (expert_rows, gate_w, up_w, down_w))
        picked = expert_out.reshape(-1, MODEL_DIMENSION)[slot_of].reshape(-1, TOPK, MODEL_DIMENSION)
        mixture = lax.optimization_barrier(jnp.sum(gate_probs[:, :, None] * picked, axis=1))
        return (x_second + mixture).reshape(ROWS, LENGTH, MODEL_DIMENSION)
    output, pull_back = jax.vjp(forward, inputs.astype(jnp.float32), norm1_gain.astype(jnp.float32), w_query.astype(jnp.float32), key_weight.astype(jnp.float32), value_weight.astype(jnp.float32), q_gain.astype(jnp.float32), k_gain.astype(jnp.float32), w_out.astype(jnp.float32), norm2_gain.astype(jnp.float32), w_router.astype(jnp.float32), w_gate.astype(jnp.float32), w_up.astype(jnp.float32), w_down.astype(jnp.float32))
    grads = pull_back(cotangent.astype(jnp.float32))
    return (output.astype(jnp.bfloat16), grads[0], grads[1], grads[2], grads[3], grads[4], grads[5], grads[6], grads[7], grads[8], grads[9], grads[10], grads[11], grads[12])
```

```python
import jax
import jax.numpy as jnp
import numpy as np
from jax import lax
from jax.sharding import PartitionSpec as P

HQ = 32
KEY_VALUE_HEADS = 4
HEAD_DIMENSION = 128
TOPK = 8

EPSILON = 1e-06
ROPE_BASE = 1000000.0
NEGATIVE = -1e30
EXACT_PRECISION = lax.Precision.HIGHEST
BF = jnp.bfloat16
F32 = jnp.float32


def ring_order(count):
    width = 4 if count >= 16 else 2
    if count % width or count // width < 2:
        return list(range(count))
    depth = count // width
    order = [z * width for z in range(depth)]
    for turn, z in enumerate(reversed(range(depth))):
        columns = range(1, width) if turn % 2 == 0 else range(width - 1, 0, -1)
        order += [z * width + y for y in columns]
    return order


class Ring:
    def __init__(self, count):
        self.n = count
        self.order = ring_order(count)
        place = [0] * count
        for i, d in enumerate(self.order):
            place[d] = i
        self.up = [(self.order[i], self.order[(i + 1) % count]) for i in range(count)]
        self.down = [(b, a) for a, b in self.up]
        me = jnp.asarray(place, jnp.int32)[lax.axis_index("shard")]
        table = jnp.asarray(self.order, jnp.int32)
        self.index = [table[(me + r) % count] for r in range(count)]

    def forward(self, value):
        return lax.ppermute(value, "shard", self.up)

    def backward(self, value):
        return lax.ppermute(value, "shard", self.down)

    def gather(self, value):
        n, half = self.n, self.n // 2
        blocks = [None] * n
        blocks[0] = value
        for j in range(1, half):
            blocks[n - j] = self.forward(blocks[(n - j + 1) % n])
            blocks[j] = self.backward(blocks[j - 1])
        cut = value.shape[0] // 2 // 16 * 16
        top = self.forward(blocks[(half + 1) % n][:cut])
        bottom = self.backward(blocks[half - 1][cut:])
        blocks[half] = jnp.concatenate([top, bottom], axis=0)
        return blocks

    def reduce(self, part):
        n, half = self.n, self.n // 2
        far = part(half)
        rows = far.shape[0]
        cut = rows // 2 // 16 * 16
        top = self.forward(far[:cut].astype(BF)).astype(F32)
        bottom = self.backward(far[cut:].astype(BF)).astype(F32)
        ahead = jnp.pad(top, ((0, rows - cut), (0, 0)))
        behind = jnp.pad(bottom, ((cut, 0), (0, 0)))
        for j in range(half - 1, 0, -1):
            ahead = self.forward((part(j) + ahead).astype(BF)).astype(F32)
            behind = self.backward((part(n - j) + behind).astype(BF)).astype(F32)
        return part(0) + ahead + behind

    def chunks(self):
        n, half = self.n, self.n // 2
        if half < 2:
            return [[0], [1]]
        near = [[j, n - j] for j in range(1, half - 1)]
        return [[0]] + near + [[half - 1, n - half + 1, half]]


def swap(value, bit, count):
    return lax.ppermute(value, "seq", [(i, i ^ bit) for i in range(count)])


def seq_gather(value, count):
    have = {0: value}
    bit = count // 2
    while bit:
        keys = sorted(have)
        got = swap(jnp.stack([have[k] for k in keys]), bit, count)
        for i, k in enumerate(keys):
            have[k ^ bit] = got[i]
        bit //= 2
    return [have[k] for k in range(count)]


def seq_reduce(parts, count):
    have = dict(enumerate(parts))
    bit = 1
    while bit < count:
        keys = [k for k in sorted(have) if k & bit]
        got = swap(jnp.stack([have[k].astype(BF) for k in keys]), bit, count)
        for i, k in enumerate(keys):
            have[k ^ bit] = have[k ^ bit] + got[i].astype(F32)
            del have[k]
        bit *= 2
    return have[0]


def tree_sum(values):
    values = list(values)
    while len(values) > 1:
        values = [values[i] + values[i + 1] for i in range(0, len(values), 2)]
    return values[0]


def after(value, *others):
    return lax.optimization_barrier((value,) + others)[0]


def matmul(a, b):
    return jnp.dot(a, b, preferred_element_type=F32)


def matmul_nt(a, b):
    return lax.dot_general(a, b, (((1,), (1,)), ((), ())), preferred_element_type=F32)


def matmul_tn(a, b):
    return lax.dot_general(a, b, (((0,), (0,)), ((), ())), preferred_element_type=F32)


def apply_rotary(values, cosine_table, sine_values):
    half_size = values.shape[-1] // 2
    first_half = values[..., :half_size]
    second_half = values[..., half_size:]
    cos_b = cosine_table[:, None, :]
    sin_b = sine_values[:, None, :]
    return jnp.concatenate(
        [first_half * cos_b - second_half * sin_b, second_half * cos_b + first_half * sin_b],
        axis=-1,
    )


def root_mean_scale(values):
    return lax.rsqrt(jnp.mean(values * values, axis=-1, keepdims=True) + EPSILON)


def rms_back(grad_out, values, gain):
    factor = root_mean_scale(values)
    normed = values * factor
    grad_norm = grad_out * gain
    grad_values = factor * (
        grad_norm - normed * jnp.mean(grad_norm * normed, axis=-1, keepdims=True)
    )
    return (grad_values, grad_out * normed)


def attend_scores(queries, keys, allowed):
    scores = jnp.einsum("qhd,kd->hqk", queries, keys, preferred_element_type=F32)
    scores = scores * queries.shape[-1] ** (-0.5)
    return jnp.where(allowed[None], scores, NEGATIVE)


def attend_forward(queries, keys, values, allowed):
    scores = attend_scores(queries, keys, allowed)
    highest = jnp.max(scores, axis=-1, keepdims=True)
    exp_terms = jnp.exp(scores - highest)
    row_total = jnp.sum(exp_terms, axis=-1, keepdims=True)
    weights_bf = (exp_terms / row_total).astype(BF)
    out = jnp.einsum("hqk,kd->qhd", weights_bf, values, preferred_element_type=F32)
    return out.astype(BF), highest + jnp.log(row_total)


def attend_backward(queries, keys, values, grad_heads, log_totals, allowed):
    scale = queries.shape[-1] ** (-0.5)
    weights = jnp.exp(attend_scores(queries, keys, allowed) - log_totals)
    grad_weights = jnp.einsum("qhd,kd->hqk", grad_heads, values, preferred_element_type=F32)
    centre = jnp.sum(weights * grad_weights, axis=-1, keepdims=True)
    grad_scores = (weights * (grad_weights - centre)).astype(BF)
    grad_q = jnp.einsum("hqk,kd->qhd", grad_scores, keys, preferred_element_type=F32) * scale
    grad_k = jnp.einsum("hqk,qhd->kd", grad_scores, queries, preferred_element_type=F32) * scale
    grad_v = jnp.einsum(
        "hqk,qhd->kd", weights.astype(BF), grad_heads, preferred_element_type=F32
    )
    return grad_q.astype(BF), grad_k.astype(BF), grad_v.astype(BF)


def per_device(
    inputs,
    seq_ids,
    routes,
    norm1_gain,
    w_query,
    key_weight,
    value_weight,
    q_gain,
    k_gain,
    w_out,
    norm2_gain,
    w_router,
    w_gate,
    w_up,
    w_down,
    cotangent,
):
    tokens = inputs.shape[1]
    width = inputs.shape[2]
    S = lax.axis_size("seq")
    N = lax.axis_size("shard")
    s = lax.axis_index("seq")
    d = lax.axis_index("shard")
    ring = Ring(N)
    heads = HQ // S
    replicas = S // KEY_VALUE_HEADS
    HD = HEAD_DIMENSION
    length = tokens * S
    experts = S * N
    cap = max(2, tokens * TOPK * 5 // (4 * experts))
    slab = width // N
    q_cols = heads * HD
    cols = q_cols + 2 * HD
    kv_at = (s // replicas) * HD

    pieces = [
        norm1_gain,
        norm2_gain,
        q_gain,
        k_gain,
        w_router.reshape(-1),
        routes.astype(BF).reshape(-1),
    ]
    sizes = [p.shape[0] for p in pieces]
    starts = np.cumsum([0] + sizes)
    extra = -(-int(starts[-1]) // (8 * cols)) * 8
    packed = jnp.concatenate(pieces + [jnp.zeros((extra * cols - int(starts[-1]),), BF)])
    block = jnp.concatenate(
        [
            lax.dynamic_slice(w_query, (0, s * q_cols), (slab, q_cols)),
            lax.dynamic_slice(key_weight, (0, kv_at), (slab, HD)),
            lax.dynamic_slice(value_weight, (0, kv_at), (slab, HD)),
        ],
        axis=1,
    )
    block = jnp.concatenate([block, packed.reshape(extra, cols)], axis=0)
    x_row = jnp.stack(seq_gather(inputs[0], S))
    ids = jnp.stack(seq_gather(seq_ids[0], S)).reshape(length)

    blocks = ring.gather(block)
    w_qkv = jnp.zeros((width, cols), BF)
    small = jnp.zeros((N, extra * cols), BF)
    route_blocks = []
    for r in range(N):
        w_qkv = lax.dynamic_update_slice(w_qkv, blocks[r][:slab], (ring.index[r] * slab, 0))
        flat = blocks[r][slab:].reshape(1, -1)
        small = lax.dynamic_update_slice(small, flat, (ring.index[r], 0))
        route_blocks.append(flat[0, int(starts[5]) : int(starts[6])].reshape(tokens, TOPK))

    def unpack(i):
        return small[:, int(starts[i]) : int(starts[i + 1])]

    gain_one, gain_two = unpack(0).reshape(-1), unpack(1).reshape(-1)
    qgain, kgain = unpack(2).reshape(-1), unpack(3).reshape(-1)
    router = unpack(4).reshape(width, experts)

    rows_out = w_out.shape[0] // S
    piece = lax.dynamic_slice(w_out, (s * rows_out, 0), (rows_out, width))
    spread = [((g % S) * N + g // S, g) for g in range(S * N)]
    piece = lax.ppermute(piece, ("seq", "shard"), spread)
    piece = after(piece, blocks[N // 2])
    out_blocks = ring.gather(piece)
    w_o = jnp.zeros((q_cols, width), BF)
    for r in range(N):
        w_o = lax.dynamic_update_slice(w_o, out_blocks[r], (ring.index[r] * rows_out, 0))

    grad_low = cotangent[0]
    dy_blocks = ring.gather(after(grad_low, out_blocks[N // 2]))

    x_all = x_row.reshape(length, width).astype(F32)
    factor_one = root_mean_scale(x_all)
    h1 = (x_all * factor_one * gain_one).astype(BF)
    qkv = matmul(h1, w_qkv)
    q_raw = qkv[:, :q_cols].reshape(length, heads, HD)
    k_raw = qkv[:, q_cols : q_cols + HD].reshape(length, 1, HD)
    v_low = qkv[:, q_cols + HD :].astype(BF)
    sources = jnp.arange(S, dtype=jnp.int32) ^ s
    positions = (sources[:, None] * tokens + jnp.arange(tokens, dtype=jnp.int32)).reshape(-1)
    inverse = ROPE_BASE ** (-2.0 * jnp.arange(HD // 2, dtype=F32) / HD)
    angles = positions.astype(F32)[:, None] * inverse[None, :]
    cosine_table, sine_values = jnp.cos(angles), jnp.sin(angles)
    q_rot = apply_rotary(q_raw * root_mean_scale(q_raw) * qgain, cosine_table, sine_values)
    k_rot = apply_rotary(k_raw * root_mean_scale(k_raw) * kgain, cosine_table, sine_values)
    q_rot = q_rot.astype(BF)
    k_rot = k_rot.astype(BF).reshape(length, HD)
    allowed = (positions[None, :] <= positions[:, None]) & (ids[:, None] == ids[None, :])
    attended, log_totals = attend_forward(q_rot, k_rot, v_low, allowed)
    attended = attended.reshape(length, q_cols)

    out_part = matmul(attended, w_o).reshape(S, tokens, width)
    x_first = inputs[0].astype(F32)
    x_second = x_first + seq_reduce([out_part[k] for k in range(S)], S)
    normed_two = x_second * root_mean_scale(x_second)
    h2 = (normed_two * gain_two).astype(BF)

    my_experts = ((jnp.arange(S, dtype=jnp.int32) ^ s) * N + d).astype(F32)
    route_all = jnp.stack(route_blocks).astype(F32)
    hits = jnp.any(
        route_all[:, None, :, :] == my_experts[None, :, None, None], axis=-1
    )
    before = jnp.asarray(np.triu(np.ones((tokens, tokens), np.float32), 1), BF)
    ranks = jnp.einsum("rkt,tu->rku", hits.astype(BF), before, preferred_element_type=F32)
    ranks = jnp.where(hits, ranks, -1.0)
    chosen = (
        ranks[:, :, None, :] == jnp.arange(cap, dtype=F32)[None, None, :, None]
    ).astype(BF)
    chunks = ring.chunks()

    def select(c):
        m = len(c)
        table = jnp.stack([chosen[r] for r in c], axis=1)
        eye = jnp.eye(m, dtype=BF)
        wide = table[:, :, :, None, :] * eye[None, :, None, :, None]
        return wide.reshape(S * m * cap, m * tokens)

    tables = [select(c) for c in chunks]

    def exchange(rows):
        size = rows.shape[0] // S
        got = [rows[:size]]
        for k in range(1, S):
            got.append(swap(rows[k * size : (k + 1) * size], k, S))
        return jnp.concatenate(got, axis=0)

    def dispatch(token_blocks):
        result = []
        for c, table in zip(chunks, tables):
            source = jnp.concatenate([token_blocks[r] for r in c], axis=0)
            result.append(exchange(matmul(table, source).astype(BF)))
        return result

    dy_rows = dispatch(dy_blocks)
    down_w, gate_w, up_w = w_down[0], w_gate[0], w_up[0]
    pulled = [matmul_nt(rows, down_w) for rows in dy_rows]

    h2_blocks = ring.gather(h2)
    h2_rows = dispatch(h2_blocks)

    logits = [matmul(block, router) for block in h2_blocks]
    expert_ids = jnp.arange(experts, dtype=F32)

    def gates_of(r):
        pick = route_all[r][:, :, None] == expert_ids[None, None, :]
        taken = jnp.sum(jnp.where(pick, logits[r][:, None, :], 0.0), axis=-1)
        return jax.nn.softmax(taken, axis=-1), pick

    gate_list = [gates_of(r) for r in range(N)]
    gate_here = jnp.stack(
        [
            jnp.sum(
                jnp.where(
                    route_all[r][:, :, None] == my_experts[None, None, :],
                    gate_list[r][0][:, :, None],
                    0.0,
                ),
                axis=1,
            )
            for r in range(N)
        ]
    )
    slot_gates = jnp.sum(
        chosen.astype(F32) * jnp.transpose(gate_here, (0, 2, 1))[:, :, None, :], axis=-1
    )
    slot_gates = jnp.transpose(slot_gates, (1, 0, 2))
    slot_gates = jnp.stack(
        [slot_gates[0]] + [swap(slot_gates[k], k, S) for k in range(1, S)]
    )

    def of_chunk(values, c):
        return jnp.stack([values[:, r] for r in c], axis=1).reshape(-1)

    y_rows, back_rows, gate_terms = [], [], []
    weighted_hidden, weighted_gate, weighted_up = [], [], []
    for i, c in enumerate(chunks):
        rows, pull = h2_rows[i], pulled[i]
        g = matmul(rows, gate_w)
        u = matmul(rows, up_w)
        sig = jax.nn.sigmoid(g)
        silu = g * sig
        hidden = (silu * u).astype(BF)
        dg = pull * u * sig * (1.0 + g * (1.0 - sig))
        du = pull * silu
        back_rows.append(
            (matmul_nt(dg.astype(BF), gate_w) + matmul_nt(du.astype(BF), up_w)).astype(BF)
        )
        gate_terms.append(jnp.sum(pull * hidden.astype(F32), axis=-1))
        y_rows.append(matmul(hidden, down_w).astype(BF))
        weight = of_chunk(slot_gates, c)[:, None]
        weighted_hidden.append((hidden.astype(F32) * weight).astype(BF))
        weighted_gate.append((dg * weight).astype(BF))
        weighted_up.append((du * weight).astype(BF))

    def combine_table(i):
        c = chunks[i]
        m = len(c)
        gates = jnp.stack([gate_here[r] for r in c])
        scale = jnp.broadcast_to(
            jnp.transpose(gates, (2, 0, 1))[:, None, None], (S, m, cap, m, tokens)
        ).reshape(S * m * cap, m * tokens)
        return (tables[i].astype(F32) * scale).astype(BF)

    mixers = [combine_table(i) for i in range(len(chunks))]

    term_slots = jnp.zeros((N, S, cap), F32)
    terms = {}
    for i, c in enumerate(chunks):
        parts = gate_terms[i].reshape(S, len(c), cap)
        for j, r in enumerate(c):
            terms[r] = parts[:, j]
    terms = jnp.stack([terms[r] for r in range(N)], axis=1)
    terms = jnp.stack([terms[0]] + [swap(terms[k], k, S) for k in range(1, S)])
    term_tokens = jnp.einsum(
        "rkct,krc->rtk", chosen.astype(F32), terms, precision=EXACT_PRECISION
    )
    lanes = -(-experts // 128) * 128
    column = (
        my_experts[:, None] == jnp.arange(lanes, dtype=F32)[None, :]
    ).astype(F32)
    term_columns = jnp.einsum("rtk,ke->rte", term_tokens, column, precision=EXACT_PRECISION)

    def combine(expert_rows):
        sums = {}
        for i in reversed(range(len(chunks))):
            c = chunks[i]
            returned = exchange(expert_rows[i])
            mixed = matmul_tn(mixers[i], returned)
            for j, r in enumerate(c):
                sums[r] = mixed[j * tokens : (j + 1) * tokens]
        return sums

    back_sums = combine(back_rows)
    with_terms = ring.reduce(
        lambda r: jnp.concatenate([back_sums[r], term_columns[r]], axis=1)
    )

    y_rows[-1] = after(y_rows[-1], with_terms)
    y_sums = combine(y_rows)
    mixture = ring.reduce(lambda r: y_sums[r])
    result = (x_second + mixture).astype(BF)

    grad_final = grad_low.astype(F32)
    gate_probs, pick = gate_list[0]
    columns = with_terms[:, width : width + experts]
    grad_gates = jnp.sum(jnp.where(pick, columns[:, None, :], 0.0), axis=-1)
    grad_chosen = gate_probs * (
        grad_gates - jnp.sum(gate_probs * grad_gates, axis=-1, keepdims=True)
    )
    grad_logits = jnp.sum(jnp.where(pick, grad_chosen[:, :, None], 0.0), axis=1)
    grad_two = with_terms[:, :width] + jnp.dot(
        grad_logits, router.astype(F32).T, precision=EXACT_PRECISION
    )
    grad_router = jnp.dot(h2.astype(F32).T, grad_logits, precision=EXACT_PRECISION)
    grad_x_norm, norm_terms = rms_back(grad_two, x_second, gain_two)
    grad_gain_two = jnp.sum(norm_terms, axis=0)
    grad_second = grad_final + grad_x_norm
    grad_attn = jnp.stack(seq_gather(grad_second.astype(BF), S)).reshape(length, width)

    grad_heads = matmul_nt(grad_attn, w_o).astype(BF).reshape(length, heads, HD)
    out_sum = ring.reduce(
        lambda r: matmul_tn(
            lax.dynamic_slice(attended, (0, ring.index[r] * rows_out), (length, rows_out)),
            grad_attn,
        )
    ).astype(BF)
    out_sum = lax.ppermute(out_sum, ("seq", "shard"), [(b, a) for a, b in spread])
    out_sum = seq_gather(out_sum, S)
    grad_out_w = jnp.zeros((S * rows_out, width), F32)
    for k in range(S):
        grad_out_w = lax.dynamic_update_slice(
            grad_out_w, out_sum[k].astype(F32), (sources[k] * rows_out, 0)
        )

    grad_q, grad_k, grad_v = attend_backward(
        q_rot, k_rot, v_low, grad_heads, log_totals, allowed
    )
    grad_k, grad_v = grad_k.astype(F32), grad_v.astype(F32)
    bit = 1
    while bit < replicas:
        both = jnp.stack([grad_k, grad_v])
        both = both + swap(both.astype(BF), bit, S).astype(F32)
        grad_k, grad_v = both[0], both[1]
        bit *= 2
    grad_q_norm, q_terms = rms_back(
        apply_rotary(grad_q.astype(F32), cosine_table, -sine_values), q_raw, qgain
    )
    grad_k_norm, k_terms = rms_back(
        apply_rotary(grad_k.reshape(length, 1, HD), cosine_table, -sine_values), k_raw, kgain
    )
    grad_qgain = jnp.sum(q_terms, axis=(0, 1))
    grad_kgain = jnp.sum(k_terms, axis=(0, 1)) / replicas
    grad_q_raw = grad_q_norm.reshape(length, q_cols).astype(BF)
    grad_k_raw = grad_k_norm.reshape(length, HD).astype(BF)
    grad_v_raw = grad_v.astype(BF)
    grad_qkv = jnp.concatenate([grad_q_raw, grad_k_raw, grad_v_raw], axis=1)
    if replicas > 1:
        shared = jnp.concatenate(
            [grad_q_raw, grad_k_raw / replicas, grad_v_raw / replicas], axis=1
        )
    else:
        shared = grad_qkv
    grad_one_part = matmul_nt(shared, w_qkv)
    grad_gain_one = jnp.sum(grad_one_part * (x_all * factor_one), axis=0)

    small_grads = jnp.concatenate(
        [
            grad_gain_one.reshape(N, -1),
            grad_gain_two.reshape(N, -1),
            grad_qgain.reshape(N, -1),
            grad_kgain.reshape(N, -1),
            grad_router.reshape(N, -1),
        ],
        axis=1,
    )
    rest = extra * cols - small_grads.shape[1]
    small_grads = jnp.pad(small_grads, ((0, 0), (0, rest))).reshape(N, extra, cols)

    def grad_block(r):
        part = matmul_tn(
            lax.dynamic_slice(h1, (0, ring.index[r] * slab), (length, slab)), grad_qkv
        )
        tail = lax.dynamic_index_in_dim(small_grads, ring.index[r], 0, keepdims=False)
        return jnp.concatenate([part, tail], axis=0)

    qkv_sum = seq_gather(ring.reduce(grad_block).astype(BF), S)
    grad_query = jnp.zeros((slab, S * q_cols), F32)
    grad_key = jnp.zeros((slab, KEY_VALUE_HEADS * HD), F32)
    grad_value = jnp.zeros((slab, KEY_VALUE_HEADS * HD), F32)
    for k in range(S):
        full = qkv_sum[k][:slab].astype(F32)
        at = (sources[k] // replicas) * HD
        grad_query = lax.dynamic_update_slice(
            grad_query, full[:, :q_cols], (0, sources[k] * q_cols)
        )
        grad_key = lax.dynamic_update_slice(grad_key, full[:, q_cols : q_cols + HD], (0, at))
        grad_value = lax.dynamic_update_slice(grad_value, full[:, q_cols + HD :], (0, at))
    tail = tree_sum([qkv_sum[k][slab:].astype(F32) for k in range(S)]).reshape(-1)

    def tail_part(i):
        return tail[int(starts[i]) : int(starts[i + 1])]

    grad_one = seq_reduce(list(grad_one_part.reshape(S, tokens, width)), S)
    grad_x_first, _ = rms_back(grad_one, x_first, gain_one)
    grad_inputs = grad_second + grad_x_first

    def over_rows(left, right):
        return matmul_tn(jnp.concatenate(left, axis=0), jnp.concatenate(right, axis=0))

    grad_gate = over_rows(h2_rows, weighted_gate)
    grad_up = over_rows(h2_rows, weighted_up)
    grad_down = over_rows(weighted_hidden, dy_rows)

    return (
        result[None],
        grad_inputs[None],
        tail_part(0),
        grad_query,
        grad_key,
        grad_value,
        tail_part(2),
        tail_part(3),
        grad_out_w,
        tail_part(1),
        tail_part(4).reshape(slab, experts),
        grad_gate[None],
        grad_up[None],
        grad_down[None],
    )


def solution(mesh):
    in_specs = (
        P("shard", "seq", None),
        P("shard", "seq"),
        P("shard", "seq", None),
        P("shard"),
        P("shard", None),
        P("shard", None),
        P("shard", None),
        P("shard"),
        P("shard"),
        P("shard", None),
        P("shard"),
        P("shard", None),
        P(("seq", "shard"), None, None),
        P(("seq", "shard"), None, None),
        P(("seq", "shard"), None, None),
        P("shard", "seq", None),
    )
    out_specs = (
        P("shard", "seq", None),
        P("shard", "seq", None),
        P("shard"),
        P("shard", None),
        P("shard", None),
        P("shard", None),
        P("shard"),
        P("shard"),
        P("shard", None),
        P("shard"),
        P("shard", None),
        P(("seq", "shard"), None, None),
        P(("seq", "shard"), None, None),
        P(("seq", "shard"), None, None),
    )
    return jax.shard_map(
        per_device, mesh=mesh, in_specs=in_specs, out_specs=out_specs, check_vma=False
    )
```

```python
import jax
import jax.numpy as jnp
import numpy as np
from jax import lax
from jax.experimental import pallas as pl
from jax.experimental.pallas import tpu as pltpu
from jax.sharding import PartitionSpec as P

HQ = 32
KEY_VALUE_HEADS = 4
HEAD_DIMENSION = 128
TOPK = 8

EPSILON = 1e-06
ROPE_BASE = 1000000.0
NEGATIVE = -1e30
EXACT = lax.Precision.HIGHEST
BF = jnp.bfloat16
F32 = jnp.float32
I32 = jnp.int32


def ring_order(count):
    width = 4 if count >= 16 else 2
    if count % width or count // width < 2:
        return list(range(count))
    depth = count // width
    order = [z * width for z in range(depth)]
    for turn, z in enumerate(reversed(range(depth))):
        columns = range(1, width) if turn % 2 == 0 else range(width - 1, 0, -1)
        order += [z * width + y for y in columns]
    return order


class Ring:
    def __init__(self, count):
        self.n = count
        self.order = ring_order(count)
        place = [0] * count
        for i, d in enumerate(self.order):
            place[d] = i
        self.up = [(self.order[i], self.order[(i + 1) % count]) for i in range(count)]
        self.down = [(b, a) for a, b in self.up]
        seats = jnp.arange(count, dtype=I32)
        mine = seats == lax.axis_index("shard")
        me = jnp.sum(jnp.where(mine, jnp.asarray(place, I32), 0))
        ahead = (me + seats) % count
        table = jnp.asarray(self.order, I32)
        self.index = jnp.sum(
            jnp.where(ahead[:, None] == seats[None, :], table[None, :], 0), axis=1
        )

    def forward(self, value):
        return lax.ppermute(value, "shard", self.up)

    def backward(self, value):
        return lax.ppermute(value, "shard", self.down)

    def gather(self, value):
        n, half = self.n, self.n // 2
        blocks = [None] * n
        blocks[0] = value
        for j in range(1, half):
            blocks[n - j] = self.forward(blocks[(n - j + 1) % n])
            blocks[j] = self.backward(blocks[j - 1])
        cut = value.shape[0] // 2 // 16 * 16
        top = self.forward(blocks[(half + 1) % n][:cut])
        bottom = self.backward(blocks[half - 1][cut:])
        blocks[half] = jnp.concatenate([top, bottom], axis=0)
        return blocks

    def reduce(self, parts):
        n, half = self.n, self.n // 2
        far = parts[half]
        rows = far.shape[0]
        cut = rows // 2 // 16 * 16
        top = self.forward(far[:cut].astype(BF))
        bottom = self.backward(far[cut:].astype(BF))
        ahead = jnp.pad(top.astype(F32), ((0, rows - cut), (0, 0)))
        behind = jnp.pad(bottom.astype(F32), ((cut, 0), (0, 0)))
        for j in range(half - 1, 0, -1):
            ahead = self.forward((parts[j] + ahead).astype(BF))
            behind = self.backward((parts[n - j] + behind).astype(BF))
        return parts[0], ahead, behind

    def chunks(self):
        n, half = self.n, self.n // 2
        if half < 3:
            return [[r] for r in range(n)]
        near = [[j, n - j] for j in range(1, half - 1)]
        return [[0]] + near + [[half - 1, n - half + 1, half]]


def swap(value, bit, count):
    return lax.ppermute(value, "seq", [(i, i ^ bit) for i in range(count)])


def seq_gather(value, count):
    have = {0: value}
    bit = count // 2
    while bit:
        for k in sorted(have):
            have[k ^ bit] = swap(have[k], bit, count)
        bit //= 2
    return [have[k] for k in range(count)]


def seq_reduce(parts, count):
    have = dict(enumerate(parts))
    bit = 1
    while bit < count:
        keys = [k for k in sorted(have) if k & bit]
        got = swap(jnp.concatenate([have[k].astype(BF) for k in keys]), bit, count)
        if bit * 2 == count:
            return have[0], got
        size = parts[0].shape[0]
        for i, k in enumerate(keys):
            have[k ^ bit] = have[k ^ bit] + got[i * size : (i + 1) * size].astype(F32)
            del have[k]
        bit *= 2
    return have[0], jnp.zeros_like(have[0], BF)


def tree_sum(values):
    values = list(values)
    while len(values) > 1:
        values = [values[i] + values[i + 1] for i in range(0, len(values), 2)]
    return values[0]


def after(value, *others):
    return lax.optimization_barrier((value,) + others)[0]


def shaped(shape, dtype):
    return jax.ShapeDtypeStruct(tuple(shape), dtype)


def run(body, outs, operands, scratch=()):
    spaces = {"s": pltpu.SMEM, "a": pl.ANY, "v": pltpu.VMEM}
    specs, arrays = [], []
    for item in operands:
        kind, array = item if isinstance(item, tuple) else ("v", item)
        specs.append(pl.BlockSpec(memory_space=spaces[kind]))
        arrays.append(array)
    results = pl.pallas_call(
        body,
        out_shape=list(outs),
        in_specs=specs,
        out_specs=[pl.BlockSpec(memory_space=pltpu.VMEM)] * len(outs),
        scratch_shapes=list(scratch),
        compiler_params=pltpu.CompilerParams(vmem_limit_bytes=60 << 20),
        cost_estimate=pl.CostEstimate(flops=1 << 20, bytes_accessed=1 << 16, transcendentals=0),
    )(*arrays)
    return list(results)


def dot(a, b, precision=None):
    return jnp.dot(a, b, preferred_element_type=F32, precision=precision)


def dot_nt(a, b, precision=None):
    return lax.dot_general(
        a, b, (((1,), (1,)), ((), ())), preferred_element_type=F32, precision=precision
    )


def dot_tn(a, b, precision=None):
    return lax.dot_general(
        a, b, (((0,), (0,)), ((), ())), preferred_element_type=F32, precision=precision
    )


def iota(shape, dim):
    return lax.broadcasted_iota(I32, shape, dim)


def at(start, size):
    return pl.ds(pl.multiple_of(start, size), size)


def row_scale(values):
    return lax.rsqrt(jnp.mean(values * values, axis=-1, keepdims=True) + EPSILON)


def as_column(row):
    size = row.shape[-1]
    same = iota((size, size), 0) == iota((size, size), 1)
    return jnp.sum(jnp.where(same, row, 0.0), axis=1, keepdims=True)


def turn(values, cosines, sines):
    return values * cosines + pltpu.roll(values, HEAD_DIMENSION // 2, 1) * sines


def weights_of(query, keys, bias):
    scores = dot_nt(query, keys) * HEAD_DIMENSION ** (-0.5) + bias
    terms = jnp.exp(scores - jnp.max(scores, axis=-1, keepdims=True))
    return terms * (1.0 / jnp.sum(terms, axis=-1, keepdims=True))


def per_device(
    inputs,
    seq_ids,
    routes,
    norm1_gain,
    w_query,
    key_weight,
    value_weight,
    q_gain,
    k_gain,
    w_out,
    norm2_gain,
    w_router,
    w_gate,
    w_up,
    w_down,
    cotangent,
):
    T = inputs.shape[1]
    D = inputs.shape[2]
    S = lax.axis_size("seq")
    N = lax.axis_size("shard")
    s = lax.axis_index("seq")
    d = lax.axis_index("shard")
    ring = Ring(N)
    heads = HQ // S
    replicas = S // KEY_VALUE_HEADS
    HD = HEAD_DIMENSION
    L = T * S
    E = S * N
    SP = -(-S // 8) * 8
    FF = w_gate.shape[2]
    cap = max(2, T * TOPK * 5 // (4 * E))
    slab = D // N
    QC = heads * HD
    C = QC + 2 * HD
    PR = w_out.shape[0] // S
    W = D + 128
    chunks = ring.chunks()

    sources = jnp.arange(S, dtype=I32) ^ s
    meta = jnp.concatenate([ring.index, sources, sources * N + d, jnp.stack([s])]).astype(I32)
    meta_s = ("s", meta)
    SRC, EXP = N, N + S

    XR = 16
    while E % XR or (E // XR) * slab + slab + 128 + T > C:
        XR *= 2
    groups = E // XR
    misc = groups * slab
    spare = C - (misc + slab + 128 + T)

    seat = jnp.arange(128, dtype=I32)[None, :] // (128 // N) == d

    def placed(gain):
        return jnp.where(seat, jnp.tile(gain, N)[None, :], jnp.zeros((), BF))

    def pack_body(m, wq, wk, wv, g1, g2, qg, kg, router, table, out, sems):
        me = m[N + 2 * S]
        copies = [
            pltpu.make_async_copy(
                wq.at[:, at(me * QC, QC)], out.at[pl.ds(0, slab), pl.ds(0, QC)], sems.at[0]
            ),
            pltpu.make_async_copy(
                wk.at[:, at(me // replicas * HD, HD)],
                out.at[pl.ds(0, slab), pl.ds(QC, HD)],
                sems.at[1],
            ),
            pltpu.make_async_copy(
                wv.at[:, at(me // replicas * HD, HD)],
                out.at[pl.ds(0, slab), pl.ds(QC + HD, HD)],
                sems.at[2],
            ),
        ]
        for c in copies:
            c.start()
        low = pl.ds(slab, XR)
        for g in range(groups):
            out[low, g * slab : (g + 1) * slab] = router[g * XR : (g + 1) * XR, :]

        def two(first, second, size):
            line = iota((XR, size), 0)
            first, second = first[...].astype(F32), second[...].astype(F32)
            return jnp.where(line == 0, first, jnp.where(line == 8, second, 0.0)).astype(BF)

        out[low, misc : misc + slab] = two(g1, g2, slab)
        out[low, misc + slab : misc + slab + 128] = two(qg, kg, 128)
        lines = table[...].astype(F32)
        lines = jnp.concatenate([lines, jnp.zeros((XR - TOPK, T), F32)], axis=0)
        out[low, misc + slab + 128 : misc + slab + 128 + T] = lines.astype(BF)
        if spare:
            out[low, C - spare :] = jnp.zeros((XR, spare), BF)
        for c in copies:
            c.wait()

    (block,) = run(
        pack_body,
        [shaped((slab + XR, C), BF)],
        [
            meta_s,
            ("a", w_query),
            ("a", key_weight),
            ("a", value_weight),
            norm1_gain.reshape(1, -1),
            norm2_gain.reshape(1, -1),
            placed(q_gain),
            placed(k_gain),
            w_router.T,
            routes[0].T,
        ],
        [pltpu.SemaphoreType.DMA((3,))],
    )
    x_rows = seq_gather(inputs[0], S)
    id_rows = seq_gather(seq_ids, S)
    blocks = ring.gather(block)

    piece = lax.dynamic_slice(w_out, (s * PR, 0), (PR, D))
    spread = [((g % S) * N + g // S, g) for g in range(S * N)]
    piece = lax.ppermute(piece, ("seq", "shard"), spread)
    piece = after(piece, blocks[N // 2])
    out_blocks = ring.gather(piece)

    grad_low = cotangent[0]
    dy_blocks = ring.gather(after(grad_low, out_blocks[N // 2]))

    positions = (sources[:, None] * T + jnp.arange(T, dtype=I32)).reshape(-1)
    inverse = ROPE_BASE ** (-2.0 * jnp.arange(HD // 2, dtype=F32) / HD)
    angles = positions.astype(F32)[:, None] * inverse[None, :]
    cosines, sines = jnp.cos(angles), jnp.sin(angles)
    cosines = jnp.concatenate([cosines, cosines], axis=1)
    sines = jnp.concatenate([-sines, sines], axis=1)

    def attend_body(*refs):
        m, xs, ids = refs[0], refs[1 : 1 + S], refs[1 + S : 1 + 2 * S]
        cos, sin = refs[1 + 2 * S : 3 + 2 * S]
        blk = refs[3 + 2 * S : 3 + 2 * S + N]
        rest = refs[3 + 2 * S + N :]
        h1, raw, rot, krot, vlow, out, bias, g1, g2, gq, router, table, keys = rest[:13]
        full, ext, sems = rest[13:]
        copies, small = [], []
        for r in range(N):
            c = pltpu.make_async_copy(
                blk[r].at[pl.ds(slab, XR)], ext.at[r], sems.at[0, r]
            )
            c.start()
            small.append(c)
        for r in range(N):
            c = pltpu.make_async_copy(
                blk[r].at[pl.ds(0, slab)], full.at[at(m[r] * slab, slab)], sems.at[1, r]
            )
            c.start()
            copies.append(c)

        id_f = [i[...].astype(F32) for i in ids]
        for a in range(S):
            column = as_column(id_f[a])
            q_pos = m[SRC + a] * T + iota((T, T), 0)
            for b in range(S):
                k_pos = m[SRC + b] * T + iota((T, T), 1)
                allowed = (k_pos <= q_pos) & (column == id_f[b])
                bias[a * T : (a + 1) * T, b * T : (b + 1) * T] = jnp.where(
                    allowed, 0.0, NEGATIVE
                )

        for c in small:
            c.wait()
        gq[...] = jnp.zeros((8, 128), F32)
        for r in range(N):
            place = at(m[r] * slab, slab)
            for g in range(groups):
                router[g * XR : (g + 1) * XR, place] = ext[r, :, g * slab : (g + 1) * slab]
            gains = ext[r, :, misc : misc + slab].astype(F32)
            g1[:, place] = gains[0:1]
            g2[:, place] = gains[8:9]
            pair = ext[r, :, misc + slab : misc + slab + 128].astype(F32)
            gq[0:1, :] += pair[0:1]
            gq[1:2, :] += pair[8:9]
            lines = ext[r, :, misc + slab + 128 : misc + slab + 128 + T].astype(F32)[:TOPK]
            table[r] = lines
            keys[r] = jnp.zeros((SP, T), F32)
            for k in range(S):
                expert = m[EXP + k].astype(F32)
                keys[r, k : k + 1, :] = jnp.max(
                    jnp.where(lines == expert, 1.0, 0.0), axis=0, keepdims=True
                )
        hits = keys[...].reshape(N * SP, T)
        earlier = jnp.where(iota((T, T), 0) < iota((T, T), 1), 1.0, 0.0).astype(BF)
        ranks = dot(hits.astype(BF), earlier)
        keys[...] = jnp.where(hits > 0.0, ranks, -1e6).reshape(N, SP, T)

        for k in range(S):
            x = xs[k][...].astype(F32)
            h1[k * T : (k + 1) * T, :] = (x * row_scale(x) * g1[...]).astype(BF)
        for c in copies:
            c.wait()

        wide = 256 if C % 256 == 0 else 128

        def project(i, carry):
            raw[:, at(i * wide, wide)] = dot(h1[...], full[:, at(i * wide, wide)])
            return carry

        lax.fori_loop(0, C // wide, project, 0)
        k_raw = raw[:, QC : QC + HD]
        krot[...] = turn(k_raw * row_scale(k_raw) * gq[1:2, :], cos[...], sin[...]).astype(BF)
        vlow[...] = raw[:, QC + HD :].astype(BF)

        def head(h, carry):
            lanes = at(h * HD, HD)
            q_raw = raw[:, lanes]
            q = turn(q_raw * row_scale(q_raw) * gq[0:1, :], cos[...], sin[...]).astype(BF)
            rot[:, lanes] = q
            p = weights_of(q, krot[...], bias[...]).astype(BF)
            out[:, lanes] = dot(p, vlow[...]).astype(BF)
            return carry

        lax.fori_loop(0, heads, head, 0)

    (
        h1,
        qkv,
        q_rot,
        k_rot,
        v_low,
        attended,
        bias,
        gain_one,
        gain_two,
        gain_qk,
        router_t,
        route_t,
        keys,
    ) = run(
        attend_body,
        [
            shaped((L, D), BF),
            shaped((L, C), F32),
            shaped((L, QC), BF),
            shaped((L, HD), BF),
            shaped((L, HD), BF),
            shaped((L, QC), BF),
            shaped((L, L), F32),
            shaped((1, D), F32),
            shaped((1, D), F32),
            shaped((8, 128), F32),
            shaped((E, D), BF),
            shaped((N, TOPK, T), F32),
            shaped((N, SP, T), F32),
        ],
        [meta_s] + x_rows + id_rows + [cosines, sines] + [("a", b) for b in blocks],
        [
            pltpu.VMEM((D, C), BF),
            pltpu.VMEM((N, XR, C), BF),
            pltpu.SemaphoreType.DMA((2, N)),
        ],
    )

    def fetch_out(m, pieces, full, sems):
        copies = []
        for r in range(N):
            c = pltpu.make_async_copy(pieces[r], full.at[at(m[r] * PR, PR)], sems.at[r])
            c.start()
            copies.append(c)
        return copies

    def project_body(*refs):
        m, o, pieces = refs[0], refs[1], refs[2 : 2 + N]
        out, full, sems = refs[2 + N :]
        for c in fetch_out(m, pieces, full, sems):
            c.wait()

        def tile(i, carry):
            out[:, at(i * 512, 512)] = dot(o[...], full[:, at(i * 512, 512)])
            return carry

        lax.fori_loop(0, D // 512, tile, 0)

    (out_part,) = run(
        project_body,
        [shaped((L, D), F32)],
        [meta_s, attended] + [("a", b) for b in out_blocks],
        [pltpu.VMEM((QC, D), BF), pltpu.SemaphoreType.DMA((N,))],
    )
    x2_own, x2_got = seq_reduce([out_part[k * T : (k + 1) * T] for k in range(S)], S)

    def second_body(x, own, got, g2, x2_out, h2_out):
        x2 = x[...].astype(F32) + own[...] + got[...].astype(F32)
        x2_out[...] = x2
        h2_out[...] = (x2 * row_scale(x2) * g2[...]).astype(BF)

    x_second, h2 = run(
        second_body,
        [shaped((T, D), F32), shaped((T, D), BF)],
        [inputs[0], x2_own, x2_got, gain_two],
    )

    def select(token_blocks, c):
        m = len(c)

        def body(*refs):
            key, tokens, outs = refs[0], refs[1 : 1 + m], refs[1 + m :]
            for k in range(S):
                acc = None
                for j, r in enumerate(c):
                    slot = key[r, k : k + 1, :] + float(j * cap)
                    pick = jnp.where(
                        iota((m * cap, T), 0).astype(F32) == slot, 1.0, 0.0
                    ).astype(BF)
                    term = dot(pick, tokens[j][...])
                    acc = term if acc is None else acc + term
                outs[k][...] = acc.astype(BF)

        return run(
            body, [shaped((m * cap, D), BF)] * S, [keys] + [token_blocks[r] for r in c]
        )

    def exchange(pieces):
        return [pieces[0]] + [swap(pieces[k], k, S) for k in range(1, S)]

    dy_rows = [exchange(select(dy_blocks, c)) for c in chunks]
    h2_blocks = ring.gather(h2)
    h2_rows = [exchange(select(h2_blocks, c)) for c in chunks]

    def gate_body(*refs):
        m, tokens = refs[0], refs[1 : 1 + N]
        router, table, key, gates_k, own, slots = refs[1 + N :]
        line = iota((E, T), 0).astype(F32)
        for r in range(N):
            logits = dot_nt(router[...], tokens[r][...])
            routed = jnp.zeros((E, T), F32)
            for j in range(TOPK):
                routed = jnp.where(line == table[r, j : j + 1, :], 1.0, routed)
            top = jnp.max(jnp.where(routed > 0.0, logits, NEGATIVE), axis=0, keepdims=True)
            terms = jnp.where(routed > 0.0, jnp.exp(logits - top), 0.0)
            gates = terms / jnp.sum(terms, axis=0, keepdims=True)
            if r == 0:
                eye = jnp.where(iota((E, 128), 0) == iota((E, 128), 1), 1.0, 0.0)
                own[...] = dot_tn(gates, eye, EXACT)
            gates_k[r] = jnp.zeros((SP, T), F32)
            for k in range(S):
                gate = jnp.sum(
                    jnp.where(line == m[EXP + k].astype(F32), gates, 0.0),
                    axis=0,
                    keepdims=True,
                )
                gates_k[r, k : k + 1, :] = gate
                pick = jnp.where(iota((cap, T), 0).astype(F32) == key[r, k : k + 1, :], 1.0, 0.0)
                slots[k, r : r + 1, :] = dot_nt(
                    jnp.broadcast_to(gate, (8, T)), pick, EXACT
                )[0:1]

    gate_k, gate_own, slot_gates = run(
        gate_body,
        [shaped((N, SP, T), F32), shaped((T, 128), F32), shaped((S, N, cap), F32)],
        [meta_s] + h2_blocks + [router_t, route_t, keys],
    )
    slot_gates = [slot_gates[0]] + [swap(slot_gates[k], k, S) for k in range(1, S)]

    gate_w, up_w, down_w = w_gate[0], w_up[0], w_down[0]

    def expert(c, x_pieces, y_pieces):
        m = len(c)
        size = m * cap
        pad = -(-size // 16) * 16
        rows = S * pad

        def body(*refs):
            mt, xs, ys = refs[0], refs[1 : 1 + S], refs[1 + S : 1 + 2 * S]
            wg, wu, wd = refs[1 + 2 * S : 4 + 2 * S]
            rest = refs[4 + 2 * S :]
            backs, fronts = rest[:S], rest[S : 2 * S]
            xp, yp, hid, dg_out, du_out, sums = rest[2 * S :]
            for k in range(S):
                for source, target in ((xs[k], xp), (ys[k], yp)):
                    value = source[...]
                    if pad > size:
                        value = jnp.concatenate(
                            [value, jnp.zeros((pad - size, D), BF)], axis=0
                        )
                    target[k * pad : (k + 1) * pad, :] = value
            sums[...] = jnp.zeros_like(sums)

            def first(i, carry):
                lanes = at(i * 256, 256)
                g = dot(xp[...], wg[:, lanes])
                u = dot(xp[...], wu[:, lanes])
                z = dot_nt(yp[...], wd[lanes, :])
                sig = 1.0 / (1.0 + jnp.exp(-g))
                silu = g * sig
                hidden = (silu * u).astype(BF)
                hid[:, lanes] = hidden
                du_out[:, lanes] = (z * silu).astype(BF)
                dg_out[:, lanes] = (z * u * sig * (1.0 + g * (1.0 - sig))).astype(BF)
                sums[...] += jnp.sum(z * hidden.astype(F32), axis=1, keepdims=True)
                return carry

            lax.fori_loop(0, FF // 256, first, 0)

            def second(i, carry):
                cols = at(i * 512, 512)
                back = dot_nt(dg_out[...], wg[cols, :]) + dot_nt(du_out[...], wu[cols, :])
                front = dot(hid[...], wd[:, cols])
                for k in range(S):
                    part = slice(k * pad, k * pad + size)
                    backs[k][:, cols] = back[part].astype(BF)
                    fronts[k][:, cols] = front[part].astype(BF)
                return carry

            lax.fori_loop(0, D // 512, second, 0)
            mine = iota((pad, 128), 1) == mt[EXP]
            for k in range(S):
                term = jnp.where(mine, sums[k * pad : (k + 1) * pad, 0:1], 0.0)
                backs[k][:, D:] = term[:size].astype(BF)

        outs = run(
            body,
            [shaped((size, W), BF)] * S
            + [shaped((size, D), BF)] * S
            + [shaped((rows, D), BF)] * 2
            + [shaped((rows, FF), BF)] * 3,
            [meta_s] + x_pieces + y_pieces + [gate_w, up_w, down_w],
            [pltpu.VMEM((rows, 128), F32)],
        )
        return outs[:S], outs[S : 2 * S], outs[2 * S :]

    backs, fronts, kept = [], [], []
    for i, c in enumerate(chunks):
        back, front, rest = expert(c, h2_rows[i], dy_rows[i])
        backs.append(back)
        fronts.append(front)
        kept.append(rest)

    def mix(i, pieces):
        c = chunks[i]
        m = len(c)
        wide = pieces[0].shape[1]

        def body(*refs):
            key, gate, rows, outs = refs[0], refs[1], refs[2 : 2 + S], refs[2 + S :]
            for j, r in enumerate(c):
                acc = None
                for k in range(S):
                    slot = key[r, k : k + 1, :] + float(j * cap)
                    hit = iota((m * cap, T), 0).astype(F32) == slot
                    weight = jnp.where(hit, gate[r, k : k + 1, :], 0.0).astype(BF)
                    term = dot_tn(weight, rows[k][...])
                    acc = term if acc is None else acc + term
                outs[j][...] = acc

        return run(body, [shaped((T, wide), F32)] * m, [keys, gate_k] + pieces)

    def combine(expert_pieces):
        sums = {}
        for i in reversed(range(len(chunks))):
            for r, value in zip(chunks[i], mix(i, exchange(expert_pieces[i]))):
                sums[r] = value
        return [sums[r] for r in range(N)]

    back_own, back_ahead, back_behind = ring.reduce(combine(backs))

    fronts[-1] = [after(fronts[-1][0], back_ahead)] + fronts[-1][1:]
    y_own, y_ahead, y_behind = ring.reduce(combine(fronts))
    result = (
        x_second + y_own + y_ahead.astype(F32) + y_behind.astype(F32)
    ).astype(BF)

    extra_rows = -(-(E // 8 * slab + slab) // D) * 8

    def tokens_body(own, ahead, behind, x2, g2, router, gates, hidden, dy, dx2, da, small):
        total = own[...] + ahead[...].astype(F32) + behind[...].astype(F32)
        gated = total[:, D:]
        dl = gated - gates[...] * jnp.sum(gated, axis=1, keepdims=True)
        grad = total[:, :D] + dot(dl[:, :E], router[...].astype(F32), EXACT)
        small[0:E, :] = dot_tn(dl, hidden[...].astype(F32), EXACT)[:E]
        scale = row_scale(x2[...])
        n2 = x2[...] * scale
        dn = grad * g2[...]
        small[E : E + 8, :] = jnp.broadcast_to(
            jnp.sum(grad * n2, axis=0, keepdims=True), (8, D)
        )
        out = dy[...].astype(F32) + scale * (
            dn - n2 * jnp.mean(dn * n2, axis=-1, keepdims=True)
        )
        dx2[...] = out
        da[...] = out.astype(BF)

    grad_second, grad_attn, small_two = run(
        tokens_body,
        [shaped((T, D), F32), shaped((T, D), BF), shaped((E + 8, D), F32)],
        [
            back_own,
            back_ahead,
            back_behind,
            x_second,
            gain_two,
            router_t,
            gate_own,
            h2,
            grad_low,
        ],
    )
    da_rows = seq_gather(grad_attn, S)

    def out_grad_body(*refs):
        m, o, das, small = refs[0], refs[1], refs[2 : 2 + S], refs[2 + S]
        outs, full = refs[3 + S : 3 + S + N], refs[3 + S + N]
        da = jnp.concatenate([a[...] for a in das], axis=0)
        if PR % 128:
            full[...] = dot_tn(o[...], da)
        for r in range(N):
            if PR % 128:
                outs[r][0:PR, :] = full[at(m[r] * PR, PR), :]
            else:
                outs[r][0:PR, :] = dot_tn(o[:, at(m[r] * PR, PR)], da)
            place = at(m[r] * slab, slab)
            tail = [small[8 * g : 8 * (g + 1), place] for g in range(E // 8 + 1)]
            used = len(tail) * slab
            room = extra_rows // 8 * D
            if room > used:
                tail.append(jnp.zeros((8, room - used), F32))
            tail = jnp.concatenate(tail, axis=1)
            for g in range(extra_rows // 8):
                outs[r][PR + 8 * g : PR + 8 * (g + 1), :] = tail[:, g * D : (g + 1) * D]

    out_parts = run(
        out_grad_body,
        [shaped((PR + extra_rows, D), F32)] * N,
        [meta_s, attended] + da_rows + [small_two],
        [pltpu.VMEM((QC, D) if PR % 128 else (8, 128), F32)],
    )
    out_own, out_ahead, out_behind = ring.reduce(out_parts)
    out_sum = (out_own + out_ahead.astype(F32) + out_behind.astype(F32)).astype(BF)
    out_piece = lax.ppermute(out_sum[:PR], ("seq", "shard"), [(b, a) for a, b in spread])
    out_pieces = seq_gather(out_piece, S)
    tail_pieces = seq_gather(out_sum[PR:], S)

    def out_join_body(*refs):
        m, pieces, tails = refs[0], refs[1 : 1 + S], refs[1 + S : 1 + 2 * S]
        out, small = refs[1 + 2 * S :]
        for k in range(S):
            out[at(m[SRC + k] * PR, PR), :] = pieces[k][...].astype(F32)
        small[...] = tree_sum([t[...].astype(F32) for t in tails])

    grad_out_w, tail_two = run(
        out_join_body,
        [shaped((S * PR, D), F32), shaped((extra_rows, D), F32)],
        [meta_s] + out_pieces + tail_pieces,
    )
    lines = [
        tail_two[8 * g : 8 * (g + 1), i * slab : (i + 1) * slab]
        for g in range(extra_rows // 8)
        for i in range(D // slab)
    ]
    grad_router = jnp.concatenate(lines[: E // 8], axis=0).T
    grad_gain_two = lines[E // 8][0]

    def back_body(*refs):
        m, das, pieces = refs[0], refs[1 : 1 + S], refs[1 + S : 1 + S + N]
        raw, rot, krot, vlow, bias_, gq, cos, sin = refs[1 + S + N : 9 + S + N]
        dq, dk_out, dv_out, gain, full, do, dk, dv, sems = refs[9 + S + N :]
        copies = fetch_out(m, pieces, full, sems)
        gain[...] = jnp.zeros_like(gain)
        dk[...] = jnp.zeros_like(dk)
        dv[...] = jnp.zeros_like(dv)
        for c in copies:
            c.wait()
        wide = 256 if QC % 256 == 0 else 128
        for k in range(S):

            def tile(i, carry, k=k):
                do[k * T : (k + 1) * T, at(i * wide, wide)] = dot_nt(
                    das[k][...], full[at(i * wide, wide), :]
                ).astype(BF)
                return carry

            lax.fori_loop(0, QC // wide, tile, 0)

        def head(h, carry):
            lanes = at(h * HD, HD)
            q = rot[:, lanes]
            grad = do[:, lanes]
            p = weights_of(q, krot[...], bias_[...])
            dp = dot_nt(grad, vlow[...])
            centre = jnp.sum(p * dp, axis=-1, keepdims=True)
            ds = (p * (dp - centre)).astype(BF)
            scale = HD ** (-0.5)
            dk[...] += dot_tn(ds, q) * scale
            dv[...] += dot_tn(p.astype(BF), grad)
            dqr = (dot(ds, krot[...]) * scale).astype(BF).astype(F32)
            dqn = turn(dqr, cos[...], -sin[...])
            q_raw = raw[:, lanes]
            factor = row_scale(q_raw)
            nq = q_raw * factor
            gain[0:1, :] += jnp.sum(dqn * nq, axis=0, keepdims=True)
            dn = dqn * gq[0:1, :]
            dq[:, lanes] = (
                factor * (dn - nq * jnp.mean(dn * nq, axis=-1, keepdims=True))
            ).astype(BF)
            return carry

        lax.fori_loop(0, heads, head, 0)
        dk_out[...] = dk[...].astype(BF)
        dv_out[...] = dv[...].astype(BF)

    grad_q, grad_k, grad_v, gain_sum = run(
        back_body,
        [
            shaped((L, QC), BF),
            shaped((L, HD), BF),
            shaped((L, HD), BF),
            shaped((8, 128), F32),
        ],
        [meta_s]
        + da_rows
        + [("a", b) for b in out_blocks]
        + [qkv, q_rot, k_rot, v_low, bias, gain_qk, cosines, sines],
        [
            pltpu.VMEM((QC, D), BF),
            pltpu.VMEM((L, QC), BF),
            pltpu.VMEM((L, HD), F32),
            pltpu.VMEM((L, HD), F32),
            pltpu.SemaphoreType.DMA((N,)),
        ],
    )
    if replicas > 1:
        both = jnp.concatenate([grad_k, grad_v], axis=1).astype(F32)
        bit = 1
        while bit < replicas:
            both = both + swap(both.astype(BF), bit, S).astype(F32)
            bit *= 2
        grad_k, grad_v = both[:, :HD], both[:, HD:]

    def weight_grad_body(m, h, dq, dk, dv, raw, gq, cos, sin, gain, *rest):
        outs, dkv = rest[:N], rest[N]
        k_raw = raw[:, QC : QC + HD]
        factor = row_scale(k_raw)
        nk = k_raw * factor
        dkn = turn(dk[...].astype(F32), cos[...], -sin[...])
        k_gain_part = jnp.sum(dkn * nk, axis=0, keepdims=True) * (1.0 / replicas)
        dn = dkn * gq[1:2, :]
        dk_raw = factor * (dn - nk * jnp.mean(dn * nk, axis=-1, keepdims=True))
        dkv[:, 0:HD] = dk_raw.astype(BF)
        dkv[:, HD:] = dv[...].astype(BF)
        for r in range(N):
            rows = h[:, at(m[r] * slab, slab)]
            outs[r][0:slab, 0:QC] = dot_tn(rows, dq[...])
            outs[r][0:slab, QC:] = dot_tn(rows, dkv[...])
            line = iota((8, 128), 0)
            outs[r][slab:, :] = jnp.zeros((8, C), F32)
            outs[r][slab:, 0:128] = jnp.where(
                line == 0, gain[0:1, :], jnp.where(line == 1, k_gain_part, 0.0)
            )

    results = run(
        weight_grad_body,
        [shaped((slab + 8, C), F32)] * N + [shaped((L, 2 * HD), BF)],
        [meta_s, h1, grad_q, grad_k, grad_v, qkv, gain_qk, cosines, sines, gain_sum],
    )
    block_parts, grad_kv = results[:N], results[N]
    block_own, block_ahead, block_behind = ring.reduce(block_parts)
    block_sum = (block_own + block_ahead.astype(F32) + block_behind.astype(F32)).astype(BF)
    block_pieces = seq_gather(block_sum, S)

    def first_back_body(*refs):
        m, dq, dkv, blk = refs[0], refs[1], refs[2], refs[3 : 3 + N]
        out, full, sems = refs[3 + N :]
        copies = []
        for r in range(N):
            c = pltpu.make_async_copy(
                blk[r].at[pl.ds(0, slab)], full.at[at(m[r] * slab, slab)], sems.at[r]
            )
            c.start()
            copies.append(c)
        share = (dkv[...].astype(F32) * (1.0 / replicas)).astype(BF)
        for c in copies:
            c.wait()

        def tile(i, carry):
            rows = at(i * 512, 512)
            out[:, rows] = dot_nt(dq[...], full[rows, 0:QC]) + dot_nt(share, full[rows, QC:])
            return carry

        lax.fori_loop(0, D // 512, tile, 0)

    (one_part,) = run(
        first_back_body,
        [shaped((L, D), F32)],
        [meta_s, grad_q, grad_kv] + [("a", b) for b in blocks],
        [pltpu.VMEM((D, C), BF), pltpu.SemaphoreType.DMA((N,))],
    )
    one_own, one_got = seq_reduce([one_part[k * T : (k + 1) * T] for k in range(S)], S)

    def inputs_body(x_ref, own, got, g1, dx2, out):
        x = x_ref[...].astype(F32)
        grad = own[...] + got[...].astype(F32)
        scale = row_scale(x)
        n1 = x * scale
        dn = grad * g1[...]
        out[...] = dx2[...] + scale * (
            dn - n1 * jnp.mean(dn * n1, axis=-1, keepdims=True)
        )

    (grad_inputs,) = run(
        inputs_body,
        [shaped((T, D), F32)],
        [inputs[0], one_own, one_got, gain_one, grad_second],
    )

    def join_body(*refs):
        m, pieces = refs[0], refs[1 : 1 + S]
        wq, wk, wv, oq, ok, ov, gains, rows = refs[1 + S :]
        for k in range(S):
            source = m[SRC + k]
            oq[:, at(source * QC, QC)] = pieces[k][0:slab, 0:QC].astype(F32)
            lanes = at(source // replicas * HD, HD)
            ok[:, lanes] = pieces[k][0:slab, QC : QC + HD].astype(F32)
            ov[:, lanes] = pieces[k][0:slab, QC + HD :].astype(F32)
        total = jnp.sum(oq[...] * wq[...].astype(F32), axis=1, keepdims=True)
        total += jnp.sum(ok[...] * wk[...].astype(F32), axis=1, keepdims=True)
        total += jnp.sum(ov[...] * wv[...].astype(F32), axis=1, keepdims=True)
        same = iota((slab, slab), 0) == iota((slab, slab), 1)
        rows[...] = jnp.broadcast_to(
            jnp.sum(jnp.where(same, total, 0.0), axis=0, keepdims=True), (8, slab)
        )
        gains[...] = tree_sum([p[slab:, 0:128].astype(F32) for p in pieces])

    grad_query, grad_key, grad_value, gain_rows, one_rows = run(
        join_body,
        [
            shaped((slab, S * QC), F32),
            shaped((slab, KEY_VALUE_HEADS * HD), F32),
            shaped((slab, KEY_VALUE_HEADS * HD), F32),
            shaped((8, 128), F32),
            shaped((8, slab), F32),
        ],
        [meta_s] + block_pieces + [w_query, key_weight, value_weight],
    )
    grad_gain_one = one_rows[0] / norm1_gain.astype(F32)
    share = HD // N
    grad_qgain = lax.dynamic_slice(gain_rows[0], (d * share,), (share,))
    grad_kgain = lax.dynamic_slice(gain_rows[1], (d * share,), (share,))

    stacked_gates = [
        jnp.stack([jnp.stack([g[r] for r in c]).reshape(-1) for g in slot_gates]) for c in chunks
    ]

    def expert_grad_body(*refs):
        count = len(chunks)
        gates, mats = refs[:count], refs[count : 6 * count]
        outs = refs[6 * count : 6 * count + 3]
        hid_s, dg_s, du_s = refs[6 * count + 3 :]
        offset = 0
        spans = []
        for i, c in enumerate(chunks):
            xp, yp, hid, dg, du = mats[5 * i : 5 * (i + 1)]
            size = len(c) * cap
            pad = -(-size // 16) * 16
            for k in range(S):
                column = as_column(gates[i][k : k + 1, :])
                if pad > size:
                    column = jnp.concatenate([column, jnp.zeros((pad - size, 1), F32)], axis=0)
                part = slice(k * pad, (k + 1) * pad)
                to = slice(offset + k * pad, offset + (k + 1) * pad)
                for source, target in ((hid, hid_s), (dg, dg_s), (du, du_s)):
                    target[to, :] = (source[part, :].astype(F32) * column).astype(BF)
            spans.append((xp, yp, slice(offset, offset + S * pad)))
            offset += S * pad

        def tile(i, carry):
            cols = at(i * 256, 256)
            x = jnp.concatenate([xp[:, cols] for xp, _, _ in spans], axis=0)
            y = jnp.concatenate([yp[:, cols] for _, yp, _ in spans], axis=0)
            outs[0][cols, :] = dot_tn(x, dg_s[...])
            outs[1][cols, :] = dot_tn(x, du_s[...])
            outs[2][:, cols] = dot_tn(hid_s[...], y)
            return carry

        lax.fori_loop(0, D // 256, tile, 0)

    total_rows = sum(S * (-(-len(c) * cap // 16) * 16) for c in chunks)
    grad_gate, grad_up, grad_down = run(
        expert_grad_body,
        [shaped((D, FF), F32), shaped((D, FF), F32), shaped((FF, D), F32)],
        stacked_gates + [a for rest in kept for a in rest],
        [pltpu.VMEM((total_rows, FF), BF)] * 3,
    )

    return (
        result[None],
        grad_inputs[None],
        grad_gain_one,
        grad_query,
        grad_key,
        grad_value,
        grad_qgain,
        grad_kgain,
        grad_out_w,
        grad_gain_two,
        grad_router,
        grad_gate[None],
        grad_up[None],
        grad_down[None],
    )


def solution(mesh):
    in_specs = (
        P("shard", "seq", None),
        P("shard", "seq"),
        P("shard", "seq", None),
        P("shard"),
        P("shard", None),
        P("shard", None),
        P("shard", None),
        P("shard"),
        P("shard"),
        P("shard", None),
        P("shard"),
        P("shard", None),
        P(("seq", "shard"), None, None),
        P(("seq", "shard"), None, None),
        P(("seq", "shard"), None, None),
        P("shard", "seq", None),
    )
    out_specs = (
        P("shard", "seq", None),
        P("shard", "seq", None),
        P("shard"),
        P("shard", None),
        P("shard", None),
        P("shard", None),
        P("shard"),
        P("shard"),
        P("shard", None),
        P("shard"),
        P("shard", None),
        P(("seq", "shard"), None, None),
        P(("seq", "shard"), None, None),
        P(("seq", "shard"), None, None),
    )
    return jax.shard_map(
        per_device, mesh=mesh, in_specs=in_specs, out_specs=out_specs, check_vma=False
    )
```

```python
import jax
import jax.numpy as jnp
import numpy as np
from jax import lax
from jax.experimental import pallas as pl
from jax.experimental.pallas import tpu as pltpu
from jax.sharding import PartitionSpec as P

HQ = 32
KEY_VALUE_HEADS = 4
HEAD_DIMENSION = 128
TOPK = 8

EPSILON = 1e-06
ROPE_BASE = 1000000.0
NEGATIVE = -1e30
EXACT = lax.Precision.HIGHEST
BF = jnp.bfloat16
F32 = jnp.float32
I32 = jnp.int32


def ring_order(count):
    width = 4 if count >= 16 else 2
    if count % width or count // width < 2:
        return list(range(count))
    depth = count // width
    order = [z * width for z in range(depth)]
    for turn, z in enumerate(reversed(range(depth))):
        columns = range(1, width) if turn % 2 == 0 else range(width - 1, 0, -1)
        order += [z * width + y for y in columns]
    return order


class Ring:
    def __init__(self, count):
        self.n = count
        self.half = count // 2
        self.order = ring_order(count)
        place = [0] * count
        for i, d in enumerate(self.order):
            place[d] = i
        self.up = [(self.order[i], self.order[(i + 1) % count]) for i in range(count)]
        self.down = [(b, a) for a, b in self.up]
        seats = jnp.arange(count, dtype=I32)
        mine = seats == lax.axis_index("shard")
        me = jnp.sum(jnp.where(mine, jnp.asarray(place, I32), 0))
        ahead = (me + seats) % count
        table = jnp.asarray(self.order, I32)
        self.index = jnp.sum(
            jnp.where(ahead[:, None] == seats[None, :], table[None, :], 0), axis=1
        )

    def forward(self, value):
        return lax.ppermute(value, "shard", self.up)

    def backward(self, value):
        return lax.ppermute(value, "shard", self.down)


def halfway(rows):
    return rows // 2 // 16 * 16


class Gather:
    def __init__(self, ring, chain, value):
        self.ring, self.chain = ring, chain
        n = ring.n
        self.cut = halfway(value.shape[0])
        self.blocks = [None] * n
        self.blocks[0] = [value]
        self.done = 1
        self.blocks[n - 1] = [ring.forward(value)]
        self.blocks[1] = [ring.backward(value)]

    def step(self):
        ring, n, j = self.ring, self.ring.n, self.done
        a, b = self.chain.gate(self.blocks[n - j][0], self.blocks[j][0])
        self.blocks[n - j], self.blocks[j] = [a], [b]
        self.done = j + 1
        if j + 1 < ring.half:
            self.blocks[n - j - 1] = [ring.forward(a)]
            self.blocks[j + 1] = [ring.backward(b)]
        else:
            self.blocks[ring.half] = [
                ring.forward(a[: self.cut]),
                ring.backward(b[self.cut :]),
            ]

    def arrive(self):
        n, j = self.ring.n, self.done
        a, b = self.chain.gate(self.blocks[n - j][0], self.blocks[j][0])
        self.blocks[n - j], self.blocks[j] = [a], [b]

    def finish(self):
        self.blocks[self.ring.half] = list(self.chain.gate(*self.blocks[self.ring.half]))


class Reduce:
    def __init__(self, ring, chain, top, bottom):
        self.ring, self.chain = ring, chain
        self.cut = top.shape[0]
        self.left = ring.half - 1
        self.ahead, self.behind = ring.forward(top), ring.backward(bottom)

    def step(self, part_ahead, part_behind):
        first = self.left == self.ring.half - 1
        cut = self.cut

        def body(a_ref, a_in, b_ref, b_in, a_out, b_out):
            if first:
                a_out[:cut, :] = (a_ref[:cut, :] + a_in[...].astype(F32)).astype(BF)
                a_out[cut:, :] = a_ref[cut:, :].astype(BF)
                b_out[:cut, :] = b_ref[:cut, :].astype(BF)
                b_out[cut:, :] = (b_ref[cut:, :] + b_in[...].astype(F32)).astype(BF)
            else:
                a_out[...] = (a_ref[...] + a_in[...].astype(F32)).astype(BF)
                b_out[...] = (b_ref[...] + b_in[...].astype(F32)).astype(BF)

        shape = shaped(part_ahead.shape, BF)
        a, b = self.chain.run(
            body, [shape, shape], [part_ahead, self.ahead, part_behind, self.behind]
        )
        self.left -= 1
        self.ahead, self.behind = self.ring.forward(a), self.ring.backward(b)


def swap(value, bit, count):
    return lax.ppermute(value, "seq", [(i, i ^ bit) for i in range(count)])


def seq_gather(chain, value, count):
    have = {0: value}
    bit = count // 2
    while bit:
        for k in sorted(have):
            if k:
                (have[k],) = chain.gate(have[k])
            have[k ^ bit] = swap(have[k], bit, count)
        bit //= 2
    return [have[k] for k in range(count)]


def tree_sum(values):
    values = list(values)
    while len(values) > 1:
        values = [values[i] + values[i + 1] for i in range(0, len(values), 2)]
    return values[0]


def shaped(shape, dtype):
    return jax.ShapeDtypeStruct(tuple(shape), dtype)


class Chain:
    def __init__(self):
        self.token = jnp.zeros((8, 128), F32)

    def gate(self, *arrays):
        *arrays, self.token = lax.optimization_barrier(tuple(arrays) + (self.token,))
        return arrays

    def run(self, body, outs, operands, scratch=()):
        spaces = {"s": pltpu.SMEM, "a": pl.ANY, "v": pltpu.VMEM}
        specs, arrays = [], []
        for item in list(operands) + [("a", self.token)]:
            kind, array = item if isinstance(item, tuple) else ("v", item)
            specs.append(pl.BlockSpec(memory_space=spaces[kind]))
            arrays.append(array)
        given, made = len(operands), len(outs)

        def call(*refs):
            rest = refs[given + 1 :]
            body(*refs[:given], *rest[:made], *rest[made + 1 :])

        *results, self.token = pl.pallas_call(
            call,
            out_shape=list(outs) + [shaped((8, 128), F32)],
            in_specs=specs,
            out_specs=[pl.BlockSpec(memory_space=pltpu.VMEM)] * made
            + [pl.BlockSpec(memory_space=pl.ANY)],
            scratch_shapes=list(scratch),
            input_output_aliases={given: made},
            compiler_params=pltpu.CompilerParams(vmem_limit_bytes=60 << 20),
            cost_estimate=pl.CostEstimate(
                flops=1 << 20, bytes_accessed=1 << 16, transcendentals=0
            ),
        )(*arrays)
        return results


def dot(a, b, precision=None):
    return jnp.dot(a, b, preferred_element_type=F32, precision=precision)


def dot_nt(a, b, precision=None):
    return lax.dot_general(
        a, b, (((1,), (1,)), ((), ())), preferred_element_type=F32, precision=precision
    )


def dot_tn(a, b, precision=None):
    return lax.dot_general(
        a, b, (((0,), (0,)), ((), ())), preferred_element_type=F32, precision=precision
    )


def iota(shape, dim):
    return lax.broadcasted_iota(I32, shape, dim)


def at(start, size):
    return pl.ds(pl.multiple_of(start, size), size)


def row_scale(values):
    return lax.rsqrt(jnp.mean(values * values, axis=-1, keepdims=True) + EPSILON)


def as_column(row):
    size = row.shape[-1]
    same = iota((size, size), 0) == iota((size, size), 1)
    return jnp.sum(jnp.where(same, row, 0.0), axis=1, keepdims=True)


def turn(values, cosines, sines):
    return values * cosines + pltpu.roll(values, HEAD_DIMENSION // 2, 1) * sines


def weights_of(query, keys, bias):
    scores = dot_nt(query, keys) * HEAD_DIMENSION ** (-0.5) + bias
    terms = jnp.exp(scores - jnp.max(scores, axis=-1, keepdims=True))
    return terms * (1.0 / jnp.sum(terms, axis=-1, keepdims=True))


def flat(lists):
    return [a for part in lists for a in part]


def regroup(refs, lists):
    out, i = [], 0
    for part in lists:
        out.append(refs[i : i + len(part)])
        i += len(part)
    return out


def per_device(
    inputs,
    seq_ids,
    routes,
    norm1_gain,
    w_query,
    key_weight,
    value_weight,
    q_gain,
    k_gain,
    w_out,
    norm2_gain,
    w_router,
    w_gate,
    w_up,
    w_down,
    cotangent,
):
    T = inputs.shape[1]
    D = inputs.shape[2]
    S = lax.axis_size("seq")
    N = lax.axis_size("shard")
    s = lax.axis_index("seq")
    d = lax.axis_index("shard")
    ring = Ring(N)
    half = ring.half
    chain = Chain()
    run, gate = chain.run, chain.gate
    heads = HQ // S
    replicas = S // KEY_VALUE_HEADS
    HD = HEAD_DIMENSION
    L = T * S
    E = S * N
    SP = -(-S // 8) * 8
    FF = w_gate.shape[2]
    cap = max(2, T * TOPK * 5 // (4 * E))
    slab = D // N
    QC = heads * HD
    C = QC + 2 * HD
    PR = w_out.shape[0] // S
    W = D + 128

    if (S, N) == (4, 8):
        quarter = [2, 0, 3, 1]
        spot = ring.index % 2 * 4 + ring.index // 2
        spread = []
        for s_to in range(S):
            for d_to in range(N):
                s_from = quarter.index(d_to // 2)
                spread.append((s_from * N + 2 * s_to + d_to % 2, s_to * N + d_to))
    else:
        quarter = list(range(S))
        spot = ring.index
        spread = [((g % S) * N + g // S, g) for g in range(S * N)]
    seat_s = jnp.arange(S, dtype=I32)
    sources = seat_s ^ s
    quarters = jnp.asarray(quarter, I32)
    quarter_of = jnp.sum(
        jnp.where(sources[:, None] == seat_s[None, :], quarters[None, :], 0), axis=1
    )
    meta = jnp.concatenate(
        [ring.index, spot, sources, sources * N + d, quarter_of]
    ).astype(I32)
    meta_s = ("s", meta)
    SPOT, SRC, EXP, QUA = N, 2 * N, 2 * N + S, 2 * N + 2 * S

    XR = 16
    while E % XR or (E // XR) * slab + slab + 128 + T > C:
        XR *= 2
    groups = E // XR
    misc = groups * slab
    spare = C - (misc + slab + 128 + T)

    seat = jnp.arange(128, dtype=I32)[None, :] // (128 // N) == d
    both_gains = jnp.stack([norm1_gain, norm2_gain])
    head_gains = jnp.where(
        seat, jnp.tile(jnp.stack([q_gain, k_gain]), (1, N)), jnp.zeros((), BF)
    )

    def pack_body(m, wq, wk, wv, gains, head_gain, router, table, out, sems):
        me = m[0]
        copies = [
            pltpu.make_async_copy(
                wq.at[:, at(me * QC, QC)], out.at[pl.ds(0, slab), pl.ds(0, QC)], sems.at[0]
            ),
            pltpu.make_async_copy(
                wk.at[:, at(me // replicas * HD, HD)],
                out.at[pl.ds(0, slab), pl.ds(QC, HD)],
                sems.at[1],
            ),
            pltpu.make_async_copy(
                wv.at[:, at(me // replicas * HD, HD)],
                out.at[pl.ds(0, slab), pl.ds(QC + HD, HD)],
                sems.at[2],
            ),
        ]
        for c in copies:
            c.start()
        low = pl.ds(slab, XR)
        for g in range(groups):
            out[low, g * slab : (g + 1) * slab] = router[g * XR : (g + 1) * XR, :]

        def two(pair, size):
            line = iota((XR, size), 0)
            pair = pair[...].astype(F32)
            return jnp.where(
                line == 0, pair[0:1], jnp.where(line == 8, pair[1:2], 0.0)
            ).astype(BF)

        out[low, misc : misc + slab] = two(gains, slab)
        out[low, misc + slab : misc + slab + 128] = two(head_gain, 128)
        lines = table[...].astype(F32)
        lines = jnp.concatenate([lines, jnp.zeros((XR - TOPK, T), F32)], axis=0)
        out[low, misc + slab + 128 : misc + slab + 128 + T] = lines.astype(BF)
        if spare:
            out[low, C - spare :] = jnp.zeros((XR, spare), BF)
        for c in copies:
            c.wait()

    (block,) = run(
        pack_body,
        [shaped((slab + XR, C), BF)],
        [
            ("s", s.reshape(1).astype(I32)),
            ("a", w_query),
            ("a", key_weight),
            ("a", value_weight),
            both_gains,
            head_gains,
            w_router.T,
            routes[0].T,
        ],
        [pltpu.SemaphoreType.DMA((3,))],
    )
    first = Gather(ring, chain, block)
    IR = 16

    def rows_body(x, ids, out):
        out[0:T, :] = x[...]
        line = jnp.broadcast_to(ids[...].astype(F32), (IR, T))
        out[T:, 0:T] = line.astype(BF)
        out[T:, T:] = jnp.zeros((IR, D - T), BF)

    (x_own,) = run(rows_body, [shaped((T + IR, D), BF)], [inputs[0], seq_ids])
    x_have = {0: x_own}
    bit = S // 2
    for step in range(half - 1):
        if bit:
            for k in sorted(x_have):
                if k:
                    (x_have[k],) = gate(x_have[k])
                x_have[k ^ bit] = swap(x_have[k], bit, S)
            bit //= 2
        first.step()
        if step == 0:
            piece = lax.dynamic_slice(w_out, (quarter_of[0] * PR, 0), (PR, D))
            (piece,) = gate(piece)
            piece = lax.ppermute(piece, ("seq", "shard"), spread)
    x_rows = [x_have[k] for k in range(S)]
    x_rows[1:] = gate(*x_rows[1:])

    positions = (sources[:, None] * T + jnp.arange(T, dtype=I32)).reshape(-1)
    inverse = ROPE_BASE ** (-2.0 * jnp.arange(HD // 2, dtype=F32) / HD)
    angles = positions.astype(F32)[:, None] * inverse[None, :]
    cosines, sines = jnp.cos(angles), jnp.sin(angles)
    cosines = jnp.concatenate([cosines, cosines], axis=1)
    sines = jnp.concatenate([-sines, sines], axis=1)
    cosines, sines, piece = gate(cosines, sines, piece)

    first.finish()
    blocks = first.blocks
    grad_low = cotangent[0]
    (dy_low,) = gate(grad_low)
    dy = Gather(ring, chain, dy_low)

    def fetch_block(m, parts, r, full, sem):
        copies, start = [], 0
        for i, part in enumerate(parts):
            rows = min(slab - start, part.shape[0])
            if rows > 0:
                base = pl.multiple_of(m[r] * slab + start, 16)
                copies.append(
                    pltpu.make_async_copy(
                        part.at[pl.ds(0, rows)], full.at[pl.ds(base, rows)], sem.at[r, i]
                    )
                )
            start += part.shape[0]
        for c in copies:
            c.start()
        return copies

    def project_body(*refs):
        m, xs = refs[0], refs[1 : 1 + S]
        cos, sin = refs[1 + S : 3 + S]
        rest = refs[3 + S :]
        blk = regroup(rest, blocks)
        rest = rest[sum(len(b) for b in blocks) :]
        h1, raw, krot, vlow, bias, g1, g2, gq, router, table, keys = rest[:11]
        full, ext, sems, ext_sems = rest[11:]
        small, copies = [], []
        for r in range(N):
            last = blk[r][-1]
            c = pltpu.make_async_copy(
                last.at[pl.ds(last.shape[0] - XR, XR)], ext.at[r], ext_sems.at[r]
            )
            c.start()
            small.append(c)
        for r in range(N):
            copies += fetch_block(m, blk[r], r, full, sems)

        id_f = [x[T : T + IR, 0:T].astype(F32)[0:1] for x in xs]
        for a in range(S):
            column = as_column(id_f[a])
            q_pos = m[SRC + a] * T + iota((T, T), 0)
            for b in range(S):
                k_pos = m[SRC + b] * T + iota((T, T), 1)
                allowed = (k_pos <= q_pos) & (column == id_f[b])
                bias[a * T : (a + 1) * T, b * T : (b + 1) * T] = jnp.where(
                    allowed, 0.0, NEGATIVE
                )

        for c in small:
            c.wait()
        gq[...] = jnp.zeros((8, 128), F32)
        for r in range(N):
            place = at(m[r] * slab, slab)
            for g in range(groups):
                router[g * XR : (g + 1) * XR, place] = ext[r, :, g * slab : (g + 1) * slab]
            gains = ext[r, :, misc : misc + slab].astype(F32)
            g1[:, place] = gains[0:1]
            g2[:, place] = gains[8:9]
            pair = ext[r, :, misc + slab : misc + slab + 128].astype(F32)
            gq[0:1, :] += pair[0:1]
            gq[1:2, :] += pair[8:9]
            lines = ext[r, :, misc + slab + 128 : misc + slab + 128 + T].astype(F32)[:TOPK]
            table[r] = lines
            keys[r] = jnp.zeros((SP, T), F32)
            for k in range(S):
                expert = m[EXP + k].astype(F32)
                keys[r, k : k + 1, :] = jnp.max(
                    jnp.where(lines == expert, 1.0, 0.0), axis=0, keepdims=True
                )
        hits = keys[...].reshape(N * SP, T)
        earlier = jnp.where(iota((T, T), 0) < iota((T, T), 1), 1.0, 0.0).astype(BF)
        ranks = dot(hits.astype(BF), earlier)
        keys[...] = jnp.where(hits > 0.0, ranks, -1e6).reshape(N, SP, T)

        for k in range(S):
            x = xs[k][0:T, :].astype(F32)
            h1[k * T : (k + 1) * T, :] = (x * row_scale(x) * g1[...]).astype(BF)
        for c in copies:
            c.wait()

        wide = 256 if C % 256 == 0 else 128

        def project(i, carry):
            raw[:, at(i * wide, wide)] = dot(h1[...], full[:, at(i * wide, wide)])
            return carry

        lax.fori_loop(0, C // wide, project, 0)
        k_raw = raw[:, QC : QC + HD]
        krot[...] = turn(k_raw * row_scale(k_raw) * gq[1:2, :], cos[...], sin[...]).astype(BF)
        vlow[...] = raw[:, QC + HD :].astype(BF)

    (
        h1,
        qkv,
        k_rot,
        v_low,
        bias,
        gain_one,
        gain_two,
        gain_qk,
        router_t,
        route_t,
        keys,
    ) = run(
        project_body,
        [
            shaped((L, D), BF),
            shaped((L, C), F32),
            shaped((L, HD), BF),
            shaped((L, HD), BF),
            shaped((L, L), F32),
            shaped((1, D), F32),
            shaped((1, D), F32),
            shaped((8, 128), F32),
            shaped((E, D), BF),
            shaped((N, TOPK, T), F32),
            shaped((N, SP, T), F32),
        ],
        [meta_s] + x_rows + [cosines, sines] + [("a", b) for b in flat(blocks)],
        [
            pltpu.VMEM((D, C), BF),
            pltpu.VMEM((N, XR, C), BF),
            pltpu.SemaphoreType.DMA((N, 2)),
            pltpu.SemaphoreType.DMA((N,)),
        ],
    )

    def attend_body(raw, krot, vlow, bias_, gq, cos, sin, rot, out):
        def head(h, carry):
            lanes = at(h * HD, HD)
            q_raw = raw[:, lanes]
            q = turn(q_raw * row_scale(q_raw) * gq[0:1, :], cos[...], sin[...]).astype(BF)
            rot[:, lanes] = q
            p = weights_of(q, krot[...], bias_[...]).astype(BF)
            out[:, lanes] = dot(p, vlow[...]).astype(BF)
            return carry

        lax.fori_loop(0, heads, head, 0)

    near_pairs = [[j, N - j] for j in range(half - 2, 0, -1)]
    near = flat(near_pairs) + [0]
    far = [half - 1, N - half + 1, half]

    def select(token_blocks, groups, rows=0, joint=False):
        order = flat(groups)
        chosen = [token_blocks[r] for r in order]
        size = len(order) * cap
        rows = max(rows, size)

        def body(*refs):
            mt, key, rest = refs[0], refs[1], refs[2:]
            tokens = regroup(rest, chosen)
            outs = rest[sum(len(b) for b in chosen) :]
            start = i = 0
            for group in groups:
                m = len(group)
                values = []
                for j in range(m):
                    parts = [t[...] for t in tokens[i + j]]
                    values.append(parts[0] if len(parts) == 1 else jnp.concatenate(parts, axis=0))
                for k in range(S):
                    acc = None
                    for j, r in enumerate(group):
                        slot = key[r, k : k + 1, :] + float(j * cap)
                        pick = jnp.where(
                            iota((m * cap, T), 0).astype(F32) == slot, 1.0, 0.0
                        ).astype(BF)
                        term = dot(pick, values[j])
                        acc = term if acc is None else acc + term
                    if joint:
                        outs[0][mt[SRC + k], start : start + m * cap, :] = acc.astype(BF)
                    else:
                        outs[k][start : start + m * cap, :] = acc.astype(BF)
                start += m * cap
                i += m
            if rows > size:
                for k in range(S):
                    outs[k][size:, :] = jnp.zeros((rows - size, D), BF)

        shapes = [shaped((S, rows, D), BF)] if joint else [shaped((rows, D), BF)] * S
        return run(body, shapes, [meta_s, keys] + flat(chosen))

    def exchange(pieces):
        return [pieces[0]] + [swap(pieces[k], k, S) for k in range(1, S)]

    def arrive(pieces):
        pieces[1:] = gate(*pieces[1:])

    def all_to_all(rows):
        return lax.all_to_all(rows, "seq", 0, 0, tiled=True)

    last_pair = near_pairs[-1] + [0]
    longer = T + 8
    dy.step()
    q_rot, attended = run(
        attend_body,
        [shaped((L, QC), BF), shaped((L, QC), BF)],
        [qkv, k_rot, v_low, bias, gain_qk, cosines, sines],
    )
    for j in range(2, half - 1):
        dy.arrive()
        if j + 1 < half - 1:
            dy.step()
    (piece,) = gate(piece)
    out_ring = Gather(ring, chain, piece)
    (dy_near,) = select(dy.blocks, near_pairs + [[0]], joint=True)
    dy_near = all_to_all(dy_near)
    while out_ring.done < half:
        out_ring.step()
    out_ring.finish()
    out_blocks = out_ring.blocks
    dy.step()

    def fetch_out(m, parts, full, sems):
        copies = []
        for r in range(N):
            start = 0
            for i, part in enumerate(parts[r]):
                rows = part.shape[0]
                base = pl.multiple_of(m[SPOT + r] * PR + start, 16)
                copies.append(
                    pltpu.make_async_copy(part, full.at[pl.ds(base, rows)], sems.at[r, i])
                )
                start += rows
        for c in copies:
            c.start()
        return copies

    def seq_reduce(make, ring_step=None):
        sent, kept = make()
        have = dict(zip(range(0, S, 2), kept))
        if ring_step is not None:
            ring_step()
        got = [swap(v, 1, S) for v in sent]
        bit = 2
        while bit < S:
            keys_sent = [k for k in sorted(have) if k & bit]
            keys_kept = [k for k in sorted(have) if not k & bit]
            order = sorted(have)

            def body(*refs):
                n = len(order)
                values, arrived, outs = refs[:n], refs[n : 2 * n], refs[2 * n :]
                total = {
                    k: values[i][...] + arrived[i][...].astype(F32)
                    for i, k in enumerate(order)
                }
                for i, k in enumerate(keys_sent):
                    outs[i][...] = total[k].astype(BF)
                for i, k in enumerate(keys_kept):
                    outs[len(keys_sent) + i][...] = total[k]

            result = run(
                body,
                [shaped((T, D), BF)] * len(keys_sent)
                + [shaped((T, D), F32)] * len(keys_kept),
                [have[k] for k in order] + got,
            )
            sent, kept = result[: len(keys_sent)], result[len(keys_sent) :]
            have = dict(zip(keys_kept, kept))
            if ring_step is not None:
                ring_step()
            got = [swap(v, bit, S) for v in sent]
            bit *= 2
        return have[0], got[0]

    reduce_shapes = [shaped((T, D), BF)] * (S // 2) + [shaped((T, D), F32)] * (S // 2)

    def make_output():
        def body(*refs):
            m, o, rest = refs[0], refs[1], refs[2:]
            parts = regroup(rest, out_blocks)
            rest = rest[sum(len(b) for b in out_blocks) :]
            outs, (full, sems) = rest[:S], rest[S:]
            for c in fetch_out(m, parts, full, sems):
                c.wait()

            def tile(i, carry):
                lanes = at(i * 512, 512)
                value = dot(o[...], full[:, lanes])
                for j, k in enumerate(range(1, S, 2)):
                    outs[j][:, lanes] = value[k * T : (k + 1) * T].astype(BF)
                for j, k in enumerate(range(0, S, 2)):
                    outs[S // 2 + j][:, lanes] = value[k * T : (k + 1) * T]
                return carry

            lax.fori_loop(0, D // 512, tile, 0)

        result = run(
            body,
            reduce_shapes,
            [meta_s, attended] + [("a", b) for b in flat(out_blocks)],
            [pltpu.VMEM((QC, D), BF), pltpu.SemaphoreType.DMA((N, 2))],
        )
        return result[: S // 2], result[S // 2 :]

    x2_own, x2_got = seq_reduce(make_output)
    (dy_near,) = gate(dy_near)
    dy.step()
    dy.finish()
    picked = select(dy.blocks, [far], longer)
    (x2_got,) = gate(x2_got)

    def second_body(x, own, got, g2, x2_out, h2_out):
        x2 = x[...].astype(F32) + own[...] + got[...].astype(F32)
        x2_out[...] = x2
        h2_out[...] = (x2 * row_scale(x2) * g2[...]).astype(BF)

    x_second, h2 = run(
        second_body,
        [shaped((T, D), F32), shaped((T, D), BF)],
        [inputs[0], x2_own, x2_got, gain_two],
    )

    walk = Gather(ring, chain, h2)
    dy_far = exchange(picked)
    h2_near = [None] * (len(near_pairs))
    for j in range(1, half):
        walk.step()
        if j == 1:
            picked = select(walk.blocks, [near_pairs[-1], [0]], longer)
            arrive(dy_far)
            moving = h2_near[-1] = exchange(picked)
        elif j < half - 1:
            picked = select(walk.blocks, [[j, N - j]])
            arrive(moving)
            moving = h2_near[half - 2 - j] = exchange(picked)
    walk.finish()
    picked = select(walk.blocks, [far])

    def gate_body(*refs):
        m, rest = refs[0], refs[1:]
        tokens = regroup(rest, walk.blocks)
        rest = rest[sum(len(b) for b in walk.blocks) :]
        router, table, key, gates_k, own, slots = rest
        line = iota((E, T), 0).astype(F32)
        for r in range(N):
            logits = [dot_nt(router[...], t[...]) for t in tokens[r]]
            logits = logits[0] if len(logits) == 1 else jnp.concatenate(logits, axis=1)
            routed = jnp.zeros((E, T), F32)
            for j in range(TOPK):
                routed = jnp.where(line == table[r, j : j + 1, :], 1.0, routed)
            top = jnp.max(jnp.where(routed > 0.0, logits, NEGATIVE), axis=0, keepdims=True)
            terms = jnp.where(routed > 0.0, jnp.exp(logits - top), 0.0)
            gates = terms / jnp.sum(terms, axis=0, keepdims=True)
            if r == 0:
                eye = jnp.where(iota((E, 128), 0) == iota((E, 128), 1), 1.0, 0.0)
                own[...] = dot_tn(gates, eye, EXACT)
            gates_k[r] = jnp.zeros((SP, T), F32)
            for k in range(S):
                value = jnp.sum(
                    jnp.where(line == m[EXP + k].astype(F32), gates, 0.0),
                    axis=0,
                    keepdims=True,
                )
                gates_k[r, k : k + 1, :] = value
                pick = jnp.where(iota((cap, T), 0).astype(F32) == key[r, k : k + 1, :], 1.0, 0.0)
                slots[k, r : r + 1, :] = dot_nt(
                    jnp.broadcast_to(value, (8, T)), pick, EXACT
                )[0:1]

    gate_k, gate_own, slot_gates = run(
        gate_body,
        [shaped((N, SP, T), F32), shaped((T, 128), F32), shaped((S, N, cap), F32)],
        [meta_s] + flat(walk.blocks) + [router_t, route_t, keys],
    )

    slot_pieces = [slot_gates[0]] + [swap(slot_gates[k], k, S) for k in range(1, 3)]
    arrive(moving)
    arrive(slot_pieces)
    h2_far = exchange(picked)
    slot_pieces += [swap(slot_gates[k], k, S) for k in range(3, S)]

    gate_w, up_w, down_w = w_gate[0], w_up[0], w_down[0]

    def expert(x_parts, y_parts, back_sizes, front_rows=0, joint=False):
        x_used = [used for _, used in x_parts]
        y_used = [used for _, used in y_parts]
        x_parts = [part for part, _ in x_parts]
        y_parts = [part for part, _ in y_parts]
        size = sum(x_used)
        pad = -(-size // 16) * 16
        rows = S * pad
        starts = np.cumsum([0] + list(back_sizes))
        front_count = 1 if joint else S

        def body(*refs):
            mt, rest = refs[0], refs[1:]
            xs = regroup(rest, x_parts)
            rest = rest[S * len(x_parts) :]
            ys = regroup(rest, y_parts)
            rest = rest[sum(len(p) for p in y_parts) :]
            wg_in, wu_in, wd_in = rest[:3]
            rest = rest[3:]
            outs = [rest[i * S : (i + 1) * S] for i in range(len(back_sizes))]
            rest = rest[S * len(back_sizes) :]
            fronts, rest = rest[:front_count], rest[front_count:]
            xp, yp, hid, dg_out, du_out, sums, wg, wu, wd, sems = rest

            def copies(i):
                lanes = at(i * 256, 256)
                return [
                    pltpu.make_async_copy(wg_in.at[:, lanes], wg.at[:, lanes], sems.at[0, i]),
                    pltpu.make_async_copy(wu_in.at[:, lanes], wu.at[:, lanes], sems.at[1, i]),
                    pltpu.make_async_copy(wd_in.at[lanes, :], wd.at[lanes, :], sems.at[2, i]),
                ]

            for i in range(FF // 256):
                for c in copies(i):
                    c.start()
            for k in range(S):
                for sources_, used, target in ((xs, x_used, xp), (ys, y_used, yp)):
                    values = [
                        part[0][mt[SRC + k], 0:n, :] if len(part) == 1 else part[k][0:n, :]
                        for part, n in zip(sources_, used)
                    ]
                    if pad > size:
                        values.append(jnp.zeros((pad - size, D), BF))
                    value = values[0] if len(values) == 1 else jnp.concatenate(values, axis=0)
                    target[k * pad : (k + 1) * pad, :] = value
            sums[...] = jnp.zeros_like(sums)

            def first(i, carry):
                lanes = at(i * 256, 256)
                for c in copies(i):
                    c.wait()
                g = dot(xp[...], wg[:, lanes])
                u = dot(xp[...], wu[:, lanes])
                z = dot_nt(yp[...], wd[lanes, :])
                sig = 1.0 / (1.0 + jnp.exp(-g))
                silu = g * sig
                hidden = (silu * u).astype(BF)
                hid[:, lanes] = hidden
                du_out[:, lanes] = (z * silu).astype(BF)
                dg_out[:, lanes] = (z * u * sig * (1.0 + g * (1.0 - sig))).astype(BF)
                sums[...] += jnp.sum(z * hidden.astype(F32), axis=1, keepdims=True)
                return carry

            lax.fori_loop(0, FF // 256, first, 0)

            def second(i, carry):
                cols = at(i * 512, 512)
                back = dot_nt(dg_out[...], wg[cols, :]) + dot_nt(du_out[...], wu[cols, :])
                front = dot(hid[...], wd[:, cols])
                for k in range(S):
                    for n, part in enumerate(outs):
                        low = k * pad + int(starts[n])
                        high = k * pad + int(starts[n + 1])
                        part[k][:, cols] = back[low:high].astype(BF)
                    part = front[k * pad : k * pad + size].astype(BF)
                    if joint:
                        fronts[0][mt[SRC + k], :, cols] = part
                    else:
                        fronts[k][0:size, cols] = part
                    if front_rows > size:
                        fronts[k][size:, cols] = jnp.zeros((front_rows - size, 512), BF)
                return carry

            lax.fori_loop(0, D // 512, second, 0)
            mine = iota((pad, 128), 1) == mt[EXP]
            for k in range(S):
                term = jnp.where(mine, sums[k * pad : (k + 1) * pad, 0:1], 0.0)
                for n, part in enumerate(outs):
                    part[k][:, D:] = term[int(starts[n]) : int(starts[n + 1])].astype(BF)

        result = run(
            body,
            [shaped((b, W), BF) for b in back_sizes for _ in range(S)]
            + (
                [shaped((S, size, D), BF)]
                if joint
                else [shaped((max(size, front_rows), D), BF)] * S
            )
            + [shaped((rows, D), BF)] * 2
            + [shaped((rows, FF), BF)] * 3,
            [meta_s]
            + flat(x_parts)
            + flat(y_parts)
            + [("a", gate_w), ("a", up_w), ("a", down_w)],
            [
                pltpu.VMEM((rows, 128), F32),
                pltpu.VMEM((D, FF), BF),
                pltpu.VMEM((D, FF), BF),
                pltpu.VMEM((FF, D), BF),
                pltpu.SemaphoreType.DMA((3, FF // 256)),
            ],
        )
        count = len(back_sizes)
        returned = [result[i * S : (i + 1) * S] for i in range(count)]
        rest = result[S * count :]
        return returned, rest[:front_count], rest[front_count:]

    pair = 2 * cap
    near_sizes = [pair] * (len(near_pairs) - 1) + [pair + cap]
    near_used = [pair] * (len(near_pairs) - 1) + [pair + cap]
    near_back, near_front, near_kept = expert(
        list(zip(h2_near, near_used)), [([dy_near], sum(near_used))], near_sizes, 0, True
    )
    arrive(h2_far)
    slot_pieces[3:] = gate(*slot_pieces[3:])
    near_back[-1] = exchange(near_back[-1])
    (far_back,), far_front, far_kept = expert(
        [(h2_far, 3 * cap)], [(dy_far, 3 * cap)], [3 * cap], T + 16
    )
    arrive(near_back[-1])
    far_back = exchange(far_back)

    def mix(group, pieces, split=False, first=0):
        m = len(group)
        wide = pieces[0].shape[-1]
        joint = pieces[0].ndim == 3
        cut = halfway(T)

        def body(*refs):
            mt, key, gate_ = refs[:3]
            rows, outs = refs[3 : 3 + len(pieces)], refs[3 + len(pieces) :]
            used = slice(first * cap, (first + m) * cap)
            for j, r in enumerate(group):
                acc = None
                for k in range(S):
                    slot = key[r, k : k + 1, :] + float(j * cap)
                    hit = iota((m * cap, T), 0).astype(F32) == slot
                    weight = jnp.where(hit, gate_[r, k : k + 1, :], 0.0).astype(BF)
                    source = rows[0][mt[SRC + k], used, :] if joint else rows[k][used, :]
                    term = dot_tn(weight, source)
                    acc = term if acc is None else acc + term
                if split and j == m - 1:
                    outs[j][...] = acc[:cut].astype(BF)
                    outs[j + 1][...] = acc[cut:].astype(BF)
                else:
                    outs[j][...] = acc

        shapes = [shaped((T, wide), F32)] * m
        if split:
            shapes[-1:] = [shaped((cut, wide), BF), shaped((T - cut, wide), BF)]
        return run(body, shapes, [meta_s, keys, gate_k] + pieces)

    def mix_and_step(walk_, group, pieces):
        m = len(group)

        def body(key, gate_, a_in, b_in, *refs):
            rows, outs = refs[:S], refs[S:]
            for j, (r, arrived) in enumerate(zip(group, (a_in, b_in))):
                acc = arrived[...].astype(F32)
                for k in range(S):
                    slot = key[r, k : k + 1, :] + float(j * cap)
                    hit = iota((m * cap, T), 0).astype(F32) == slot
                    weight = jnp.where(hit, gate_[r, k : k + 1, :], 0.0).astype(BF)
                    acc += dot_tn(weight, rows[k][0 : m * cap, :])
                outs[j][...] = acc.astype(BF)

        shape = shaped(walk_.ahead.shape, BF)
        a, b = run(
            body, [shape, shape], [keys, gate_k, walk_.ahead, walk_.behind] + pieces
        )
        walk_.left -= 1
        walk_.ahead, walk_.behind = ring.forward(a), ring.backward(b)

    def as_rows(values, group):
        return jnp.stack([jnp.stack([v[r] for r in group]).reshape(-1) for v in values])

    row_gates = [as_rows(slot_pieces, near), as_rows(slot_pieces, far)]

    def row_grad(left, right, scale_left, shape, by_column):
        def body(*refs):
            gates, lefts, rights = refs[:2], refs[2:4], refs[4:6]
            out, scaled = refs[6:]
            offset = 0
            source = lefts if scale_left else rights
            for i, g in enumerate(gates):
                size, rows = g.shape[1], source[i].shape[0] // S
                for k in range(S):
                    column = as_column(g[k : k + 1, :])
                    if rows > size:
                        column = jnp.concatenate(
                            [column, jnp.zeros((rows - size, 1), F32)], axis=0
                        )
                    scaled[offset : offset + rows, :] = (
                        source[i][k * rows : (k + 1) * rows, :].astype(F32) * column
                    ).astype(BF)
                    offset += rows
            plain = rights if scale_left else lefts

            def tile(i, carry):
                cols = at(i * 512, 512)
                other = jnp.concatenate([p[:, cols] for p in plain], axis=0)
                if by_column:
                    out[:, cols] = dot_tn(scaled[...], other)
                else:
                    out[cols, :] = dot_tn(other, scaled[...])
                return carry

            lax.fori_loop(0, D // 512, tile, 0)

        total = sum(a.shape[0] for a in left)
        (result,) = run(
            body,
            [shaped(shape, F32)],
            row_gates + list(left) + list(right),
            [pltpu.VMEM((total, FF), BF)],
        )
        return result

    kept = list(zip(near_kept, far_kept))
    x_kept, y_kept, hid_kept, dg_kept, du_kept = kept

    back_parts = {}
    a, b, c = last_pair
    back_parts[a], back_parts[b], back_parts[c] = mix(last_pair, near_back[-1])
    grad_gate = row_grad(x_kept, dg_kept, False, (D, FF), False)
    arrive(far_back)
    far_top, far_bottom = mix(far[2:], far_back, split=True, first=2)
    back = Reduce(ring, chain, far_top, far_bottom)
    back_parts[far[0]], back_parts[far[1]] = mix(far[:2], far_back)

    def back_step():
        back.step(back_parts[back.left], back_parts[N - back.left])

    back_step()
    grads = [
        lambda: row_grad(x_kept, du_kept, False, (D, FF), False),
        lambda: row_grad(hid_kept, y_kept, True, (FF, D), True),
    ]
    done_grads = []
    for i in range(len(near_pairs) - 1):
        near_back[i] = exchange(near_back[i])
        if grads:
            done_grads.append(grads.pop(0)())
        arrive(near_back[i])
        if i + 2 == len(near_pairs):
            far_front = exchange(far_front)
        mix_and_step(back, near_pairs[i], near_back[i])
    if grads:
        done_grads.append(grads.pop(0)())
    while back.left > 0:
        back_step()
    grad_up, grad_down = done_grads
    arrive(far_front)
    y_parts = {}
    y_parts[far[0]], y_parts[far[1]], y_top, y_bottom = mix(far, far_front, split=True)
    back.ahead, back.behind, y_top, y_bottom = gate(back.ahead, back.behind, y_top, y_bottom)
    front = Reduce(ring, chain, y_top, y_bottom)

    extra_rows = -(-(E // 8 * slab + slab) // D) * 8

    def tokens_body(own, ahead, behind, x2, g2, router, gates, hidden, dy_, dx2, da, small):
        total = own[...] + ahead[...].astype(F32) + behind[...].astype(F32)
        gated = total[:, D:]
        dl = gated - gates[...] * jnp.sum(gated, axis=1, keepdims=True)
        grad = total[:, :D] + dot(dl[:, :E], router[...].astype(F32), EXACT)
        small[0:E, :] = dot_tn(dl, hidden[...].astype(F32), EXACT)[:E]
        scale = row_scale(x2[...])
        n2 = x2[...] * scale
        dn = grad * g2[...]
        small[E : E + 8, :] = jnp.broadcast_to(
            jnp.sum(grad * n2, axis=0, keepdims=True), (8, D)
        )
        out = dy_[...].astype(F32) + scale * (
            dn - n2 * jnp.mean(dn * n2, axis=-1, keepdims=True)
        )
        dx2[...] = out
        da[...] = out.astype(BF)

    grad_second, grad_attn, small_two = run(
        tokens_body,
        [shaped((T, D), F32), shaped((T, D), BF), shaped((E + 8, D), F32)],
        [
            back_parts[0],
            back.ahead,
            back.behind,
            x_second,
            gain_two,
            router_t,
            gate_own,
            h2,
            grad_low,
        ],
    )
    da_have = {0: grad_attn}
    bit = S // 2
    front_sent = False
    while bit:
        for k in sorted(da_have):
            if k:
                (da_have[k],) = gate(da_have[k])
            da_have[k ^ bit] = swap(da_have[k], bit, S)
        if bit == S // 2:
            front.step(y_parts[half - 1], y_parts[N - half + 1])
        elif not front_sent:
            near_front = [all_to_all(gate(near_front[0])[0])]
            front_sent = True
        bit //= 2
    da_rows = [da_have[k] for k in range(S)]
    da_rows[1:] = gate(*da_rows[1:])

    def out_grad_body(*refs):
        m, o, das, small = refs[0], refs[1], refs[2 : 2 + S], refs[2 + S]
        outs, full = refs[3 + S : 4 + S + N], refs[4 + S + N]
        da = jnp.concatenate([a[...] for a in das], axis=0)
        if PR % 128:
            full[...] = dot_tn(o[...], da)
        cut = halfway(PR + extra_rows)
        for r in range(N):
            if PR % 128:
                value = full[at(m[SPOT + r] * PR, PR), :]
            else:
                value = dot_tn(o[:, at(m[SPOT + r] * PR, PR)], da)
            place = at(m[r] * slab, slab)
            tail = [small[8 * g : 8 * (g + 1), place] for g in range(E // 8 + 1)]
            used = len(tail) * slab
            room = extra_rows // 8 * D
            if room > used:
                tail.append(jnp.zeros((8, room - used), F32))
            tail = jnp.concatenate(tail, axis=1)
            tail = [tail[:, g * D : (g + 1) * D] for g in range(extra_rows // 8)]
            if r == half:
                whole = jnp.concatenate([value] + tail, axis=0).astype(BF)
                outs[N - 1][...] = whole[:cut]
                outs[N][...] = whole[cut:]
            else:
                target = outs[r - (r > half)]
                target[0:PR, :] = value
                for g in range(extra_rows // 8):
                    target[PR + 8 * g : PR + 8 * (g + 1), :] = tail[g]

    out_cut = halfway(PR + extra_rows)
    *out_list, out_top, out_bottom = run(
        out_grad_body,
        [shaped((PR + extra_rows, D), F32)] * (N - 1)
        + [shaped((out_cut, D), BF), shaped((PR + extra_rows - out_cut, D), BF)],
        [meta_s, attended] + da_rows + [small_two],
        [pltpu.VMEM((QC, D) if PR % 128 else (8, 128), F32)],
    )
    out_parts = {r: out_list[r - (r > half)] for r in range(N) if r != half}
    out_walk = Reduce(ring, chain, out_top, out_bottom)

    def both_steps():
        if out_walk.left > 0:
            out_walk.step(out_parts[out_walk.left], out_parts[N - out_walk.left])

    def do_body(*refs):
        m, das, rest = refs[0], refs[1 : 1 + S], refs[1 + S :]
        parts = regroup(rest, out_blocks)
        do, full, sems = rest[sum(len(b) for b in out_blocks) :]
        for c in fetch_out(m, parts, full, sems):
            c.wait()
        da = jnp.concatenate([a[...] for a in das], axis=0)
        wide = 256 if QC % 256 == 0 else 128

        def tile(i, carry):
            do[:, at(i * wide, wide)] = dot_nt(da, full[at(i * wide, wide), :]).astype(BF)
            return carry

        lax.fori_loop(0, QC // wide, tile, 0)

    (grad_heads,) = run(
        do_body,
        [shaped((L, QC), BF)],
        [meta_s] + da_rows + [("a", b) for b in flat(out_blocks)],
        [pltpu.VMEM((QC, D), BF), pltpu.SemaphoreType.DMA((N, 2))],
    )
    front.ahead, front.behind = gate(front.ahead, front.behind)
    out_walk.step(out_parts[out_walk.left], out_parts[N - out_walk.left])

    def back_body(first_head, count):
        def body(raw_in, rot_in, do_in, krot, vlow, bias_, gq, cos, sin, dk0, dv0, gain0, *rest):
            dq, dk, dv, gain, raw, rot, do, sems = rest
            lanes_here = pl.ds(first_head * HD, count * HD)
            copies = [
                pltpu.make_async_copy(raw_in.at[:, lanes_here], raw, sems.at[0]),
                pltpu.make_async_copy(rot_in.at[:, lanes_here], rot, sems.at[1]),
                pltpu.make_async_copy(do_in.at[:, lanes_here], do, sems.at[2]),
            ]
            for c in copies:
                c.start()
            dk[...] = dk0[...]
            dv[...] = dv0[...]
            gain[...] = gain0[...]
            for c in copies:
                c.wait()

            def head(h, carry):
                lanes = at(h * HD, HD)
                q = rot[:, lanes]
                grad = do[:, lanes]
                p = weights_of(q, krot[...], bias_[...])
                dp = dot_nt(grad, vlow[...])
                centre = jnp.sum(p * dp, axis=-1, keepdims=True)
                ds = (p * (dp - centre)).astype(BF)
                scale = HD ** (-0.5)
                dk[...] += dot_tn(ds, q) * scale
                dv[...] += dot_tn(p.astype(BF), grad)
                dqr = (dot(ds, krot[...]) * scale).astype(BF).astype(F32)
                dqn = turn(dqr, cos[...], -sin[...])
                q_raw = raw[:, lanes]
                factor = row_scale(q_raw)
                nq = q_raw * factor
                gain[0:1, :] += jnp.sum(dqn * nq, axis=0, keepdims=True)
                dn = dqn * gq[0:1, :]
                dq[:, lanes] = (
                    factor * (dn - nq * jnp.mean(dn * nq, axis=-1, keepdims=True))
                ).astype(BF)
                return carry

            lax.fori_loop(0, count, head, 0)

        return body

    calls = 2
    per_call = heads // calls
    grad_k, grad_v = jnp.zeros((L, HD), F32), jnp.zeros((L, HD), F32)
    gain_sum = jnp.zeros((8, 128), F32)
    grad_q = []
    for i in range(calls):
        dq, grad_k, grad_v, gain_sum = run(
            back_body(i * per_call, per_call),
            [
                shaped((L, per_call * HD), BF),
                shaped((L, HD), F32),
                shaped((L, HD), F32),
                shaped((8, 128), F32),
            ],
            [("a", qkv), ("a", q_rot), ("a", grad_heads)]
            + [k_rot, v_low, bias, gain_qk, cosines, sines, grad_k, grad_v, gain_sum],
            [
                pltpu.VMEM((L, per_call * HD), F32),
                pltpu.VMEM((L, per_call * HD), BF),
                pltpu.VMEM((L, per_call * HD), BF),
                pltpu.SemaphoreType.DMA((3,)),
            ],
        )
        grad_q.append(dq)
        both_steps()
    while out_walk.left > 0:
        both_steps()

    def final_y_body(x2, own, ahead, behind, out):
        out[...] = (
            x2[...] + own[...] + ahead[...].astype(F32) + behind[...].astype(F32)
        ).astype(BF)

    grad_k, grad_v = grad_k.astype(BF), grad_v.astype(BF)
    if replicas > 1:
        both = jnp.concatenate([grad_k, grad_v], axis=1).astype(F32)
        bit = 1
        while bit < replicas:
            both = both + swap(both.astype(BF), bit, S).astype(F32)
            bit *= 2
        grad_k, grad_v = both[:, :HD], both[:, HD:]

    def key_body(dk, dv, raw_in, gq, cos, sin, gain, dkv, gains, raw, sem):
        c = pltpu.make_async_copy(raw_in.at[:, pl.ds(QC, HD)], raw, sem)
        c.start()
        c.wait()
        k_raw = raw[...]
        factor = row_scale(k_raw)
        nk = k_raw * factor
        dkn = turn(dk[...].astype(F32), cos[...], -sin[...])
        k_part = jnp.sum(dkn * nk, axis=0, keepdims=True) * (1.0 / replicas)
        dn = dkn * gq[1:2, :]
        dk_raw = factor * (dn - nk * jnp.mean(dn * nk, axis=-1, keepdims=True))
        dkv[:, 0:HD] = dk_raw.astype(BF)
        dkv[:, HD:] = dv[...].astype(BF)
        line = iota((8, 128), 0)
        gains[...] = jnp.where(line == 0, gain[0:1, :], jnp.where(line == 1, k_part, 0.0))

    grad_kv, gain_lines = run(
        key_body,
        [shaped((L, 2 * HD), BF), shaped((8, 128), F32)],
        [grad_k, grad_v, ("a", qkv), gain_qk, cosines, sines, gain_sum],
        [pltpu.VMEM((L, HD), F32), pltpu.SemaphoreType.DMA],
    )

    block_rows = slab + 8
    block_cut = halfway(block_rows)

    def weight_grad(offsets, split=False):
        def body(m, h, *rest):
            dqs, rest = rest[:calls], rest[calls:]
            dkv, gains, outs = rest[0], rest[1], rest[2:]
            span = per_call * HD
            for j, r in enumerate(offsets):
                rows = h[:, at(m[r] * slab, slab)]
                pieces = [dot_tn(rows, dq[...]) for dq in dqs] + [dot_tn(rows, dkv[...])]
                spots = [slice(i * span, (i + 1) * span) for i in range(calls)]
                spots.append(slice(QC, C))
                tail = jnp.concatenate([gains[...], jnp.zeros((8, C - 128), F32)], axis=1)
                for spot_, piece_ in zip(spots, pieces):
                    if split:
                        outs[0][:, spot_] = piece_[:block_cut].astype(BF)
                        low = jnp.concatenate([piece_[block_cut:], tail[:, spot_]], axis=0)
                        outs[1][:, spot_] = low.astype(BF)
                    else:
                        outs[j][0:slab, spot_] = piece_
                if not split:
                    outs[j][slab:, :] = tail

        if split:
            shapes = [shaped((block_cut, C), BF), shaped((block_rows - block_cut, C), BF)]
        else:
            shapes = [shaped((block_rows, C), F32)] * len(offsets)
        return run(body, shapes, [meta_s, h1] + grad_q + [grad_kv, gain_lines])

    def total_body(own, ahead, behind, *outs):
        total = own[...] + ahead[...].astype(F32) + behind[...].astype(F32)
        start = 0
        for out in outs:
            out[...] = total[start : start + out.shape[0]].astype(BF)
            start += out.shape[0]

    out_piece, out_tail = run(
        total_body,
        [shaped((PR, D), BF), shaped((extra_rows, D), BF)],
        [out_parts[0], out_walk.ahead, out_walk.behind],
    )
    block_top, block_bottom = weight_grad([half], split=True)
    block_walk = Reduce(ring, chain, block_top, block_bottom)
    out_piece = lax.ppermute(out_piece, ("seq", "shard"), [(b, a) for a, b in spread])
    block_parts = {}

    def more_blocks(offsets):
        block_parts.update(zip(offsets, weight_grad(offsets)))

    def block_step():
        block_walk.step(block_parts[block_walk.left], block_parts[N - block_walk.left])

    more_blocks([half - 1, N - half + 1])
    block_step()
    more_blocks([r for r in range(N) if r not in block_parts and r != half])
    def make_first():
        def body(*refs):
            m, dqs, rest = refs[0], refs[1 : 1 + calls], refs[1 + calls :]
            dkv, rest = rest[0], rest[1:]
            blk = regroup(rest, blocks)
            rest = rest[sum(len(b) for b in blocks) :]
            outs, (full, sems) = rest[:S], rest[S:]
            copies = []
            for r in range(N):
                copies += fetch_block(m, blk[r], r, full, sems)
            share = (dkv[...].astype(F32) * (1.0 / replicas)).astype(BF)
            for c in copies:
                c.wait()
            span = per_call * HD

            def tile(i, carry):
                lanes = at(i * 512, 512)
                value = dot_nt(share, full[lanes, QC:])
                for j in range(calls):
                    value += dot_nt(dqs[j][...], full[lanes, j * span : (j + 1) * span])
                for j, k in enumerate(range(1, S, 2)):
                    outs[j][:, lanes] = value[k * T : (k + 1) * T].astype(BF)
                for j, k in enumerate(range(0, S, 2)):
                    outs[S // 2 + j][:, lanes] = value[k * T : (k + 1) * T]
                return carry

            lax.fori_loop(0, D // 512, tile, 0)

        result = run(
            body,
            reduce_shapes,
            [meta_s] + grad_q + [grad_kv] + [("a", b) for b in flat(blocks)],
            [pltpu.VMEM((D, C), BF), pltpu.SemaphoreType.DMA((N, 2))],
        )
        return result[: S // 2], result[S // 2 :]

    out_have = {0: out_piece}
    tail_have = {0: out_tail}
    bits = []
    while not bits or bits[-1] > 1:
        bits.append(bits[-1] // 2 if bits else S // 2)

    def tail_step():
        bit_ = bits.pop(0) if bits else 0
        pairs = [(have, k) for have in (out_have, tail_have) for k in sorted(have)]
        for have, k in pairs:
            if bit_ and k:
                (have[k],) = gate(have[k])
        if block_walk.left > 0:
            block_step()
        for have, k in pairs:
            if bit_:
                if not k:
                    (have[k],) = gate(have[k])
                have[k ^ bit_] = swap(have[k], bit_, S)

    one_own, one_got = seq_reduce(make_first, tail_step)
    near_front[:] = gate(*near_front)
    for r, part in zip(near, mix(near, near_front)):
        y_parts[r] = part
    while block_walk.left > 0 or bits:
        tail_step()
    out_pieces = [out_have[k] for k in range(S)]
    tail_pieces = [tail_have[k] for k in range(S)]
    out_pieces[1:] = gate(*out_pieces[1:])

    def out_join_body(*refs):
        m, pieces, tails = refs[0], refs[1 : 1 + S], refs[1 + S : 1 + 2 * S]
        out, small = refs[1 + 2 * S :]
        for k in range(S):
            out[at(m[QUA + k] * PR, PR), :] = pieces[k][...].astype(F32)
        small[...] = tree_sum([t_[...].astype(F32) for t_ in tails])

    grad_out_w, tail_two = run(
        out_join_body,
        [shaped((S * PR, D), F32), shaped((extra_rows, D), F32)],
        [meta_s] + out_pieces + tail_pieces,
    )

    def inputs_body(x_ref, own, got, g1, dx2, out):
        x = x_ref[...].astype(F32)
        grad = own[...] + got[...].astype(F32)
        scale = row_scale(x)
        n1 = x * scale
        dn = grad * g1[...]
        out[...] = dx2[...] + scale * (
            dn - n1 * jnp.mean(dn * n1, axis=-1, keepdims=True)
        )

    (grad_inputs,) = run(
        inputs_body,
        [shaped((T, D), F32)],
        [inputs[0], one_own, one_got, gain_one, grad_second],
    )

    (block_sum,) = run(
        total_body,
        [shaped((block_rows, C), BF)],
        [block_parts[0], block_walk.ahead, block_walk.behind],
    )
    block_have = {0: block_sum}
    bit = S // 2
    for k in sorted(block_have):
        block_have[k ^ bit] = swap(block_have[k], bit, S)

    front.step(y_parts[front.left], y_parts[N - front.left])
    while bit > 1:
        bit //= 2
        for k in sorted(block_have):
            if k:
                (block_have[k],) = gate(block_have[k])
            block_have[k ^ bit] = swap(block_have[k], bit, S)
    block_pieces = [block_have[k] for k in range(S)]
    while front.left > 0:
        front.step(y_parts[front.left], y_parts[N - front.left])
    block_pieces[1:] = gate(*block_pieces[1:])

    def join_body(*refs):
        m, pieces = refs[0], refs[1 : 1 + S]
        wq, wk, wv, oq, ok, ov, gains, rows = refs[1 + S :]
        for k in range(S):
            source = m[SRC + k]
            oq[:, at(source * QC, QC)] = pieces[k][0:slab, 0:QC].astype(F32)
            lanes = at(source // replicas * HD, HD)
            ok[:, lanes] = pieces[k][0:slab, QC : QC + HD].astype(F32)
            ov[:, lanes] = pieces[k][0:slab, QC + HD :].astype(F32)
        total = jnp.sum(oq[...] * wq[...].astype(F32), axis=1, keepdims=True)
        total += jnp.sum(ok[...] * wk[...].astype(F32), axis=1, keepdims=True)
        total += jnp.sum(ov[...] * wv[...].astype(F32), axis=1, keepdims=True)
        same = iota((slab, slab), 0) == iota((slab, slab), 1)
        rows[...] = jnp.broadcast_to(
            jnp.sum(jnp.where(same, total, 0.0), axis=0, keepdims=True), (8, slab)
        )
        gains[...] = tree_sum([p[slab:, 0:128].astype(F32) for p in pieces])

    grad_query, grad_key, grad_value, gain_rows, one_rows = run(
        join_body,
        [
            shaped((slab, S * QC), F32),
            shaped((slab, KEY_VALUE_HEADS * HD), F32),
            shaped((slab, KEY_VALUE_HEADS * HD), F32),
            shaped((8, 128), F32),
            shaped((8, slab), F32),
        ],
        [meta_s] + block_pieces + [w_query, key_weight, value_weight],
    )
    (result,) = run(
        final_y_body,
        [shaped((T, D), BF)],
        [x_second, y_parts[0], front.ahead, front.behind],
    )

    grad_gain_one = one_rows[0] / norm1_gain.astype(F32)
    share = HD // N
    grad_qgain = lax.dynamic_slice(gain_rows[0], (d * share,), (share,))
    grad_kgain = lax.dynamic_slice(gain_rows[1], (d * share,), (share,))

    lines = [
        tail_two[8 * g : 8 * (g + 1), i * slab : (i + 1) * slab]
        for g in range(extra_rows // 8)
        for i in range(D // slab)
    ]
    grad_router = jnp.concatenate(lines[: E // 8], axis=0).T
    grad_gain_two = lines[E // 8][0]

    return (
        result[None],
        grad_inputs[None],
        grad_gain_one,
        grad_query,
        grad_key,
        grad_value,
        grad_qgain,
        grad_kgain,
        grad_out_w,
        grad_gain_two,
        grad_router,
        grad_gate[None],
        grad_up[None],
        grad_down[None],
    )


def solution(mesh):
    in_specs = (
        P("shard", "seq", None),
        P("shard", "seq"),
        P("shard", "seq", None),
        P("shard"),
        P("shard", None),
        P("shard", None),
        P("shard", None),
        P("shard"),
        P("shard"),
        P("shard", None),
        P("shard"),
        P("shard", None),
        P(("seq", "shard"), None, None),
        P(("seq", "shard"), None, None),
        P(("seq", "shard"), None, None),
        P("shard", "seq", None),
    )
    out_specs = (
        P("shard", "seq", None),
        P("shard", "seq", None),
        P("shard"),
        P("shard", None),
        P("shard", None),
        P("shard", None),
        P("shard"),
        P("shard"),
        P("shard", None),
        P("shard"),
        P("shard", None),
        P(("seq", "shard"), None, None),
        P(("seq", "shard"), None, None),
        P(("seq", "shard"), None, None),
    )
    return jax.shard_map(
        per_device, mesh=mesh, in_specs=in_specs, out_specs=out_specs, check_vma=False
    )
```

```python
import jax
import jax.numpy as jnp
import numpy as np
from jax import lax
from jax.experimental import pallas as pl
from jax.experimental.pallas import tpu as pltpu
from jax.sharding import PartitionSpec as P

HQ = 32
KEY_VALUE_HEADS = 4
HEAD_DIMENSION = 128
TOPK = 8

EPSILON = 1e-06
ROPE_BASE = 1000000.0
NEGATIVE = -1e30
EXACT = lax.Precision.HIGHEST
BF = jnp.bfloat16
F32 = jnp.float32
I32 = jnp.int32
LIMIT = 8


def ring_order(count):
    width = 4 if count >= 16 else 2
    if count % width or count // width < 2:
        return list(range(count))
    depth = count // width
    order = [z * width for z in range(depth)]
    for turn, z in enumerate(reversed(range(depth))):
        columns = range(1, width) if turn % 2 == 0 else range(width - 1, 0, -1)
        order += [z * width + y for y in columns]
    return order


class Ring:
    def __init__(self, count):
        self.n = count
        self.half = count // 2
        self.order = ring_order(count)
        place = [0] * count
        for i, d in enumerate(self.order):
            place[d] = i
        self.up = [(self.order[i], self.order[(i + 1) % count]) for i in range(count)]
        self.down = [(b, a) for a, b in self.up]
        seats = jnp.arange(count, dtype=I32)
        mine = seats == lax.axis_index("shard")
        me = jnp.sum(jnp.where(mine, jnp.asarray(place, I32), 0))
        ahead = (me + seats) % count
        table = jnp.asarray(self.order, I32)
        self.index = jnp.sum(
            jnp.where(ahead[:, None] == seats[None, :], table[None, :], 0), axis=1
        )

    def forward(self, value):
        return lax.ppermute(value, "shard", self.up)

    def backward(self, value):
        return lax.ppermute(value, "shard", self.down)


def halfway(rows):
    return rows // 2 // 16 * 16


class Gather:
    def __init__(self, ring, chain, value):
        self.ring, self.chain = ring, chain
        n = ring.n
        self.cut = halfway(value.shape[0])
        self.blocks = [None] * n
        self.blocks[0] = [value]
        self.done = 1
        self.blocks[n - 1] = [ring.forward(value)]
        self.blocks[1] = [ring.backward(value)]

    def step(self):
        ring, n, j = self.ring, self.ring.n, self.done
        a, b = self.chain.gate(self.blocks[n - j][0], self.blocks[j][0])
        self.blocks[n - j], self.blocks[j] = [a], [b]
        self.done = j + 1
        if j + 1 < ring.half:
            self.blocks[n - j - 1] = [ring.forward(a)]
            self.blocks[j + 1] = [ring.backward(b)]
        else:
            self.blocks[ring.half] = [
                ring.forward(a[: self.cut]),
                ring.backward(b[self.cut :]),
            ]

    def arrive(self):
        n, j = self.ring.n, self.done
        a, b = self.chain.gate(self.blocks[n - j][0], self.blocks[j][0])
        self.blocks[n - j], self.blocks[j] = [a], [b]

    def finish(self):
        self.blocks[self.ring.half] = list(self.chain.gate(*self.blocks[self.ring.half]))


class Reduce:
    def __init__(self, ring, chain, top, bottom):
        self.ring, self.chain = ring, chain
        self.cut = top.shape[0]
        self.left = ring.half - 1
        self.ahead, self.behind = ring.forward(top), ring.backward(bottom)

    def step(self, part_ahead, part_behind):
        first = self.left == self.ring.half - 1
        cut = self.cut

        def body(a_ref, a_in, b_ref, b_in, a_out, b_out):
            if first:
                a_out[:cut, :] = (a_ref[:cut, :] + a_in[...].astype(F32)).astype(BF)
                a_out[cut:, :] = a_ref[cut:, :].astype(BF)
                b_out[:cut, :] = b_ref[:cut, :].astype(BF)
                b_out[cut:, :] = (b_ref[cut:, :] + b_in[...].astype(F32)).astype(BF)
            else:
                a_out[...] = (a_ref[...] + a_in[...].astype(F32)).astype(BF)
                b_out[...] = (b_ref[...] + b_in[...].astype(F32)).astype(BF)

        shape = shaped(part_ahead.shape, BF)
        a, b = self.chain.run(
            body, [shape, shape], [part_ahead, self.ahead, part_behind, self.behind]
        )
        self.left -= 1
        self.ahead, self.behind = self.ring.forward(a), self.ring.backward(b)


def swap(value, bit, count):
    return lax.ppermute(value, "seq", [(i, i ^ bit) for i in range(count)])


def seq_gather(chain, value, count):
    have = {0: value}
    bit = count // 2
    while bit:
        for k in sorted(have):
            if k:
                (have[k],) = chain.gate(have[k])
            have[k ^ bit] = swap(have[k], bit, count)
        bit //= 2
    return [have[k] for k in range(count)]


def tree_sum(values):
    values = list(values)
    while len(values) > 1:
        values = [values[i] + values[i + 1] for i in range(0, len(values), 2)]
    return values[0]


def shaped(shape, dtype):
    return jax.ShapeDtypeStruct(tuple(shape), dtype)


class Chain:
    def __init__(self):
        self.token = jnp.zeros((8, 128), F32)

    def gate(self, *arrays):
        *arrays, self.token = lax.optimization_barrier(tuple(arrays) + (self.token,))
        return arrays

    def run(self, body, outs, operands, scratch=(), alone=False):
        spaces = {"s": pltpu.SMEM, "a": pl.ANY, "v": pltpu.VMEM}
        specs, arrays = [], []
        for item in list(operands) + [("a", self.token)]:
            kind, array = item if isinstance(item, tuple) else ("v", item)
            specs.append(pl.BlockSpec(memory_space=spaces[kind]))
            arrays.append(array)
        given, made = len(operands), len(outs)
        need = 0
        for spec, array in list(zip(specs, arrays)) + [(None, o) for o in outs]:
            if spec is None or spec.memory_space == pltpu.VMEM:
                need += array.size * array.dtype.itemsize
        for item in scratch:
            if getattr(item, "memory_space", None) == pltpu.VMEM:
                need += int(np.prod(item.shape)) * jnp.dtype(item.dtype).itemsize
        limit = 60 << 20 if alone else min(60 << 20, need * 3 // 2 + (LIMIT << 20))

        def call(*refs):
            rest = refs[given + 1 :]
            body(*refs[:given], *rest[:made], *rest[made + 1 :])

        *results, self.token = pl.pallas_call(
            call,
            out_shape=list(outs) + [shaped((8, 128), F32)],
            in_specs=specs,
            out_specs=[pl.BlockSpec(memory_space=pltpu.VMEM)] * made
            + [pl.BlockSpec(memory_space=pl.ANY)],
            scratch_shapes=list(scratch),
            input_output_aliases={given: made},
            compiler_params=pltpu.CompilerParams(vmem_limit_bytes=limit),
            cost_estimate=pl.CostEstimate(
                flops=1 << 20, bytes_accessed=1 << 16, transcendentals=0
            ),
        )(*arrays)
        return results


def dot(a, b, precision=None):
    return jnp.dot(a, b, preferred_element_type=F32, precision=precision)


def dot_nt(a, b, precision=None):
    return lax.dot_general(
        a, b, (((1,), (1,)), ((), ())), preferred_element_type=F32, precision=precision
    )


def dot_tn(a, b, precision=None):
    return lax.dot_general(
        a, b, (((0,), (0,)), ((), ())), preferred_element_type=F32, precision=precision
    )


def iota(shape, dim):
    return lax.broadcasted_iota(I32, shape, dim)


def at(start, size):
    return pl.ds(pl.multiple_of(start, size), size)


def row_scale(values):
    return lax.rsqrt(jnp.mean(values * values, axis=-1, keepdims=True) + EPSILON)


def as_column(row):
    size = row.shape[-1]
    same = iota((size, size), 0) == iota((size, size), 1)
    return jnp.sum(jnp.where(same, row, 0.0), axis=1, keepdims=True)


def turn(values, cosines, sines):
    return values * cosines + pltpu.roll(values, HEAD_DIMENSION // 2, 1) * sines


def weights_of(query, keys, bias):
    scores = dot_nt(query, keys) * HEAD_DIMENSION ** (-0.5) + bias
    terms = jnp.exp(scores - jnp.max(scores, axis=-1, keepdims=True))
    return terms * (1.0 / jnp.sum(terms, axis=-1, keepdims=True))


def flat(lists):
    return [a for part in lists for a in part]


def regroup(refs, lists):
    out, i = [], 0
    for part in lists:
        out.append(refs[i : i + len(part)])
        i += len(part)
    return out


def per_device(
    inputs,
    seq_ids,
    routes,
    norm1_gain,
    w_query,
    key_weight,
    value_weight,
    q_gain,
    k_gain,
    w_out,
    norm2_gain,
    w_router,
    w_gate,
    w_up,
    w_down,
    cotangent,
):
    T = inputs.shape[1]
    D = inputs.shape[2]
    S = lax.axis_size("seq")
    N = lax.axis_size("shard")
    s = lax.axis_index("seq")
    d = lax.axis_index("shard")
    ring = Ring(N)
    half = ring.half
    chain = Chain()
    run, gate = chain.run, chain.gate
    heads = HQ // S
    replicas = S // KEY_VALUE_HEADS
    HD = HEAD_DIMENSION
    L = T * S
    E = S * N
    SP = -(-S // 8) * 8
    FF = w_gate.shape[2]
    cap = max(2, T * TOPK * 5 // (4 * E))
    slab = D // N
    QC = heads * HD
    C = QC + 2 * HD
    PR = w_out.shape[0] // S
    W = D + 128

    if (S, N) == (4, 8):
        quarter = [2, 0, 3, 1]
        spot = ring.index % 2 * 4 + ring.index // 2
        spread = []
        for s_to in range(S):
            for d_to in range(N):
                s_from = quarter.index(d_to // 2)
                spread.append((s_from * N + 2 * s_to + d_to % 2, s_to * N + d_to))
    else:
        quarter = list(range(S))
        spot = ring.index
        spread = [((g % S) * N + g // S, g) for g in range(S * N)]
    seat_s = jnp.arange(S, dtype=I32)
    sources = seat_s ^ s
    quarters = jnp.asarray(quarter, I32)
    quarter_of = jnp.sum(
        jnp.where(sources[:, None] == seat_s[None, :], quarters[None, :], 0), axis=1
    )
    meta = jnp.concatenate(
        [ring.index, spot, sources, sources * N + d, quarter_of]
    ).astype(I32)
    meta_s = ("s", meta)
    SPOT, SRC, EXP, QUA = N, 2 * N, 2 * N + S, 2 * N + 2 * S

    XR = 16
    while E % XR or (E // XR) * slab + slab + 128 + T > C:
        XR *= 2
    groups = E // XR
    misc = groups * slab
    spare = C - (misc + slab + 128 + T)

    seat = jnp.arange(128, dtype=I32)[None, :] // (128 // N) == d
    both_gains = jnp.stack([norm1_gain, norm2_gain])
    head_gains = jnp.where(
        seat, jnp.tile(jnp.stack([q_gain, k_gain]), (1, N)), jnp.zeros((), BF)
    )

    def pack_body(m, wq, wk, wv, gains, head_gain, router, table, out, sems):
        me = m[0]
        copies = [
            pltpu.make_async_copy(
                wq.at[:, at(me * QC, QC)], out.at[pl.ds(0, slab), pl.ds(0, QC)], sems.at[0]
            ),
            pltpu.make_async_copy(
                wk.at[:, at(me // replicas * HD, HD)],
                out.at[pl.ds(0, slab), pl.ds(QC, HD)],
                sems.at[1],
            ),
            pltpu.make_async_copy(
                wv.at[:, at(me // replicas * HD, HD)],
                out.at[pl.ds(0, slab), pl.ds(QC + HD, HD)],
                sems.at[2],
            ),
        ]
        for c in copies:
            c.start()
        low = pl.ds(slab, XR)
        for g in range(groups):
            out[low, g * slab : (g + 1) * slab] = router[g * XR : (g + 1) * XR, :]

        def two(pair, size):
            line = iota((XR, size), 0)
            pair = pair[...].astype(F32)
            return jnp.where(
                line == 0, pair[0:1], jnp.where(line == 8, pair[1:2], 0.0)
            ).astype(BF)

        out[low, misc : misc + slab] = two(gains, slab)
        out[low, misc + slab : misc + slab + 128] = two(head_gain, 128)
        lines = table[...].astype(F32)
        lines = jnp.concatenate([lines, jnp.zeros((XR - TOPK, T), F32)], axis=0)
        out[low, misc + slab + 128 : misc + slab + 128 + T] = lines.astype(BF)
        if spare:
            out[low, C - spare :] = jnp.zeros((XR, spare), BF)
        for c in copies:
            c.wait()

    (block,) = run(
        pack_body,
        [shaped((slab + XR, C), BF)],
        [
            ("s", s.reshape(1).astype(I32)),
            ("a", w_query),
            ("a", key_weight),
            ("a", value_weight),
            both_gains,
            head_gains,
            w_router.T,
            routes[0].T,
        ],
        [pltpu.SemaphoreType.DMA((3,))],
        alone=True,
    )
    first = Gather(ring, chain, block)
    IR = 16

    def rows_body(x, ids, out):
        out[0:T, :] = x[...]
        line = jnp.broadcast_to(ids[...].astype(F32), (IR, T))
        out[T:, 0:T] = line.astype(BF)
        out[T:, T:] = jnp.zeros((IR, D - T), BF)

    (x_own,) = run(rows_body, [shaped((T + IR, D), BF)], [inputs[0], seq_ids])
    x_have = {0: x_own}
    bit = S // 2
    for step in range(half - 1):
        if bit:
            for k in sorted(x_have):
                if k:
                    (x_have[k],) = gate(x_have[k])
                x_have[k ^ bit] = swap(x_have[k], bit, S)
            bit //= 2
        first.step()
        if step == 0:
            piece = lax.dynamic_slice(w_out, (quarter_of[0] * PR, 0), (PR, D))
            (piece,) = gate(piece)
            piece = lax.ppermute(piece, ("seq", "shard"), spread)
    x_rows = [x_have[k] for k in range(S)]
    x_rows[1:] = gate(*x_rows[1:])

    positions = (sources[:, None] * T + jnp.arange(T, dtype=I32)).reshape(-1)
    inverse = ROPE_BASE ** (-2.0 * jnp.arange(HD // 2, dtype=F32) / HD)
    angles = positions.astype(F32)[:, None] * inverse[None, :]
    cosines, sines = jnp.cos(angles), jnp.sin(angles)
    cosines = jnp.concatenate([cosines, cosines], axis=1)
    sines = jnp.concatenate([-sines, sines], axis=1)
    cosines, sines, piece = gate(cosines, sines, piece)

    first.finish()
    blocks = first.blocks
    grad_low = cotangent[0]
    (dy_low,) = gate(grad_low)
    dy = Gather(ring, chain, dy_low)

    def fetch_block(m, parts, r, full, sem):
        copies, start = [], 0
        for i, part in enumerate(parts):
            rows = min(slab - start, part.shape[0])
            if rows > 0:
                base = pl.multiple_of(m[r] * slab + start, 16)
                copies.append(
                    pltpu.make_async_copy(
                        part.at[pl.ds(0, rows)], full.at[pl.ds(base, rows)], sem.at[r, i]
                    )
                )
            start += part.shape[0]
        for c in copies:
            c.start()
        return copies

    def project_body(*refs):
        m, xs = refs[0], refs[1 : 1 + S]
        cos, sin = refs[1 + S : 3 + S]
        rest = refs[3 + S :]
        blk = regroup(rest, blocks)
        rest = rest[sum(len(b) for b in blocks) :]
        h1, raw, krot, vlow, bias, g1, g2, gq, router, table, keys = rest[:11]
        full, ext, sems, ext_sems = rest[11:]
        small, copies = [], []
        for r in range(N):
            last = blk[r][-1]
            c = pltpu.make_async_copy(
                last.at[pl.ds(last.shape[0] - XR, XR)], ext.at[r], ext_sems.at[r]
            )
            c.start()
            small.append(c)
        for r in range(N):
            copies += fetch_block(m, blk[r], r, full, sems)

        id_f = [x[T : T + IR, 0:T].astype(F32)[0:1] for x in xs]
        for a in range(S):
            column = as_column(id_f[a])
            q_pos = m[SRC + a] * T + iota((T, T), 0)
            for b in range(S):
                k_pos = m[SRC + b] * T + iota((T, T), 1)
                allowed = (k_pos <= q_pos) & (column == id_f[b])
                bias[a * T : (a + 1) * T, b * T : (b + 1) * T] = jnp.where(
                    allowed, 0.0, NEGATIVE
                )

        for c in small:
            c.wait()
        gq[...] = jnp.zeros((8, 128), F32)
        for r in range(N):
            place = at(m[r] * slab, slab)
            for g in range(groups):
                router[g * XR : (g + 1) * XR, place] = ext[r, :, g * slab : (g + 1) * slab]
            gains = ext[r, :, misc : misc + slab].astype(F32)
            g1[:, place] = gains[0:1]
            g2[:, place] = gains[8:9]
            pair = ext[r, :, misc + slab : misc + slab + 128].astype(F32)
            gq[0:1, :] += pair[0:1]
            gq[1:2, :] += pair[8:9]
            lines = ext[r, :, misc + slab + 128 : misc + slab + 128 + T].astype(F32)[:TOPK]
            table[r] = lines
            keys[r] = jnp.zeros((SP, T), F32)
            for k in range(S):
                expert = m[EXP + k].astype(F32)
                keys[r, k : k + 1, :] = jnp.max(
                    jnp.where(lines == expert, 1.0, 0.0), axis=0, keepdims=True
                )
        hits = keys[...].reshape(N * SP, T)
        earlier = jnp.where(iota((T, T), 0) < iota((T, T), 1), 1.0, 0.0).astype(BF)
        ranks = dot(hits.astype(BF), earlier)
        keys[...] = jnp.where(hits > 0.0, ranks, -1e6).reshape(N, SP, T)

        for k in range(S):
            x = xs[k][0:T, :].astype(F32)
            h1[k * T : (k + 1) * T, :] = (x * row_scale(x) * g1[...]).astype(BF)
        for c in copies:
            c.wait()

        wide = 256 if C % 256 == 0 else 128

        def project(i, carry):
            raw[:, at(i * wide, wide)] = dot(h1[...], full[:, at(i * wide, wide)])
            return carry

        lax.fori_loop(0, C // wide, project, 0)
        k_raw = raw[:, QC : QC + HD]
        krot[...] = turn(k_raw * row_scale(k_raw) * gq[1:2, :], cos[...], sin[...]).astype(BF)
        vlow[...] = raw[:, QC + HD :].astype(BF)

    (
        h1,
        qkv,
        k_rot,
        v_low,
        bias,
        gain_one,
        gain_two,
        gain_qk,
        router_t,
        route_t,
        keys,
    ) = run(
        project_body,
        [
            shaped((L, D), BF),
            shaped((L, C), F32),
            shaped((L, HD), BF),
            shaped((L, HD), BF),
            shaped((L, L), F32),
            shaped((1, D), F32),
            shaped((1, D), F32),
            shaped((8, 128), F32),
            shaped((E, D), BF),
            shaped((N, TOPK, T), F32),
            shaped((N, SP, T), F32),
        ],
        [meta_s] + x_rows + [cosines, sines] + [("a", b) for b in flat(blocks)],
        [
            pltpu.VMEM((D, C), BF),
            pltpu.VMEM((N, XR, C), BF),
            pltpu.SemaphoreType.DMA((N, 2)),
            pltpu.SemaphoreType.DMA((N,)),
        ],
        alone=True,
    )

    def attend_body(raw, krot, vlow, bias_, gq, cos, sin, rot, out):
        def head(h, carry):
            lanes = at(h * HD, HD)
            q_raw = raw[:, lanes]
            q = turn(q_raw * row_scale(q_raw) * gq[0:1, :], cos[...], sin[...]).astype(BF)
            rot[:, lanes] = q
            p = weights_of(q, krot[...], bias_[...]).astype(BF)
            out[:, lanes] = dot(p, vlow[...]).astype(BF)
            return carry

        lax.fori_loop(0, heads, head, 0)

    near_pairs = [[j, N - j] for j in range(half - 2, 0, -1)]
    near = flat(near_pairs) + [0]
    far = [half - 1, N - half + 1, half]

    def select(token_blocks, groups, rows=0, joint=False):
        order = flat(groups)
        chosen = [token_blocks[r] for r in order]
        size = len(order) * cap
        rows = max(rows, size)

        def body(*refs):
            mt, key, rest = refs[0], refs[1], refs[2:]
            tokens = regroup(rest, chosen)
            outs = rest[sum(len(b) for b in chosen) :]
            start = i = 0
            for group in groups:
                m = len(group)
                values = []
                for j in range(m):
                    parts = [t[...] for t in tokens[i + j]]
                    values.append(parts[0] if len(parts) == 1 else jnp.concatenate(parts, axis=0))
                for k in range(S):
                    acc = None
                    for j, r in enumerate(group):
                        slot = key[r, k : k + 1, :] + float(j * cap)
                        pick = jnp.where(
                            iota((m * cap, T), 0).astype(F32) == slot, 1.0, 0.0
                        ).astype(BF)
                        term = dot(pick, values[j])
                        acc = term if acc is None else acc + term
                    if joint:
                        outs[0][mt[SRC + k], start : start + m * cap, :] = acc.astype(BF)
                    else:
                        outs[k][start : start + m * cap, :] = acc.astype(BF)
                start += m * cap
                i += m
            if rows > size:
                for k in range(S):
                    outs[k][size:, :] = jnp.zeros((rows - size, D), BF)

        shapes = [shaped((S, rows, D), BF)] if joint else [shaped((rows, D), BF)] * S
        return run(body, shapes, [meta_s, keys] + flat(chosen))

    def exchange(pieces):
        return [pieces[0]] + [swap(pieces[k], k, S) for k in range(1, S)]

    def arrive(pieces):
        pieces[1:] = gate(*pieces[1:])

    def all_to_all(rows):
        return lax.all_to_all(rows, "seq", 0, 0, tiled=True)

    last_pair = near_pairs[-1] + [0]
    longer = T + 8
    dy.step()
    q_rot, attended = run(
        attend_body,
        [shaped((L, QC), BF), shaped((L, QC), BF)],
        [qkv, k_rot, v_low, bias, gain_qk, cosines, sines],
    )
    for j in range(2, half - 1):
        dy.arrive()
        if j + 1 < half - 1:
            dy.step()
    (piece,) = gate(piece)
    out_ring = Gather(ring, chain, piece)
    (dy_near,) = select(dy.blocks, near_pairs + [[0]], joint=True)
    dy_near = all_to_all(dy_near)
    while out_ring.done < half:
        out_ring.step()
    out_ring.finish()
    out_blocks = out_ring.blocks
    dy.step()

    def fetch_out(m, parts, full, sems):
        copies = []
        for r in range(N):
            start = 0
            for i, part in enumerate(parts[r]):
                rows = part.shape[0]
                base = pl.multiple_of(m[SPOT + r] * PR + start, 16)
                copies.append(
                    pltpu.make_async_copy(part, full.at[pl.ds(base, rows)], sems.at[r, i])
                )
                start += rows
        for c in copies:
            c.start()
        return copies

    def seq_reduce(make, ring_step=None):
        sent, kept = make()
        have = dict(zip(range(0, S, 2), kept))
        if ring_step is not None:
            ring_step()
        got = [swap(v, 1, S) for v in sent]
        bit = 2
        while bit < S:
            keys_sent = [k for k in sorted(have) if k & bit]
            keys_kept = [k for k in sorted(have) if not k & bit]
            order = sorted(have)

            def body(*refs):
                n = len(order)
                values, arrived, outs = refs[:n], refs[n : 2 * n], refs[2 * n :]
                total = {
                    k: values[i][...] + arrived[i][...].astype(F32)
                    for i, k in enumerate(order)
                }
                for i, k in enumerate(keys_sent):
                    outs[i][...] = total[k].astype(BF)
                for i, k in enumerate(keys_kept):
                    outs[len(keys_sent) + i][...] = total[k]

            result = run(
                body,
                [shaped((T, D), BF)] * len(keys_sent)
                + [shaped((T, D), F32)] * len(keys_kept),
                [have[k] for k in order] + got,
            )
            sent, kept = result[: len(keys_sent)], result[len(keys_sent) :]
            have = dict(zip(keys_kept, kept))
            if ring_step is not None:
                ring_step()
            got = [swap(v, bit, S) for v in sent]
            bit *= 2
        return have[0], got[0]

    reduce_shapes = [shaped((T, D), BF)] * (S // 2) + [shaped((T, D), F32)] * (S // 2)

    def make_output():
        def body(*refs):
            m, o, rest = refs[0], refs[1], refs[2:]
            parts = regroup(rest, out_blocks)
            rest = rest[sum(len(b) for b in out_blocks) :]
            outs, (full, sems) = rest[:S], rest[S:]
            for c in fetch_out(m, parts, full, sems):
                c.wait()

            def tile(i, carry):
                lanes = at(i * 512, 512)
                value = dot(o[...], full[:, lanes])
                for j, k in enumerate(range(1, S, 2)):
                    outs[j][:, lanes] = value[k * T : (k + 1) * T].astype(BF)
                for j, k in enumerate(range(0, S, 2)):
                    outs[S // 2 + j][:, lanes] = value[k * T : (k + 1) * T]
                return carry

            lax.fori_loop(0, D // 512, tile, 0)

        result = run(
            body,
            reduce_shapes,
            [meta_s, attended] + [("a", b) for b in flat(out_blocks)],
            [pltpu.VMEM((QC, D), BF), pltpu.SemaphoreType.DMA((N, 2))],
        )
        return result[: S // 2], result[S // 2 :]

    x2_own, x2_got = seq_reduce(make_output)
    (dy_near,) = gate(dy_near)
    dy.step()
    (x2_got,) = gate(x2_got)

    def second_body(x, own, got, g2, x2_out, h2_out):
        x2 = x[...].astype(F32) + own[...] + got[...].astype(F32)
        x2_out[...] = x2
        h2_out[...] = (x2 * row_scale(x2) * g2[...]).astype(BF)

    x_second, h2 = run(
        second_body,
        [shaped((T, D), F32), shaped((T, D), BF)],
        [inputs[0], x2_own, x2_got, gain_two],
    )

    dy.finish()
    (h2,) = gate(h2)
    walk = Gather(ring, chain, h2)
    dy_far = exchange(select(dy.blocks, [far], longer))
    h2_near = [None] * (len(near_pairs))
    walk.step()
    picked = select(walk.blocks, [near_pairs[-1], [0]], longer)
    arrive(dy_far)
    moving = h2_near[-1] = exchange(picked)
    for j in range(2, half):
        walk.step()
        if j < half - 1:
            (picked,) = select(walk.blocks, [[j, N - j]], joint=True)
            if j == half - 2:
                walk.step()
            if j == 2:
                arrive(moving)
            else:
                (h2_near[half - 1 - j],) = gate(h2_near[half - 1 - j])
            (picked,) = gate(picked)
            h2_near[half - 2 - j] = all_to_all(picked)
            if j == half - 2:
                break
    walk.finish()
    h2_far = exchange(gate(*select(walk.blocks, [far])))

    gate_w, up_w, down_w = w_gate[0], w_up[0], w_down[0]

    def expert(x_parts, y_parts, back_sizes, front_rows=0, joint=False):
        x_used = [slice(low, low + used) for _, used, low in x_parts]
        y_used = [slice(low, low + used) for _, used, low in y_parts]
        size = sum(used for _, used, _ in x_parts)
        x_parts = [part for part, _, _ in x_parts]
        y_parts = [part for part, _, _ in y_parts]
        pad = -(-size // 16) * 16
        rows = S * pad
        starts = np.cumsum([0] + list(back_sizes))
        front_count = 1 if joint else S

        def body(*refs):
            mt, rest = refs[0], refs[1:]
            xs = regroup(rest, x_parts)
            rest = rest[sum(len(p) for p in x_parts) :]
            ys = regroup(rest, y_parts)
            rest = rest[sum(len(p) for p in y_parts) :]
            wg_in, wu_in, wd_in = rest[:3]
            rest = rest[3:]
            outs = [rest[i * S : (i + 1) * S] for i in range(len(back_sizes))]
            rest = rest[S * len(back_sizes) :]
            fronts, rest = rest[:front_count], rest[front_count:]
            xp, yp, hid, dg_out, du_out, sums, wg, wu, wd, sems = rest

            def copies(i):
                lanes = at(i * 256, 256)
                return [
                    pltpu.make_async_copy(wg_in.at[:, lanes], wg.at[:, lanes], sems.at[0, i]),
                    pltpu.make_async_copy(wu_in.at[:, lanes], wu.at[:, lanes], sems.at[1, i]),
                    pltpu.make_async_copy(wd_in.at[lanes, :], wd.at[lanes, :], sems.at[2, i]),
                ]

            for i in range(FF // 256):
                for c in copies(i):
                    c.start()
            for k in range(S):
                for sources_, used, target in ((xs, x_used, xp), (ys, y_used, yp)):
                    values = [
                        part[0][mt[SRC + k], n, :] if len(part) == 1 else part[k][n, :]
                        for part, n in zip(sources_, used)
                    ]
                    if pad > size:
                        values.append(jnp.zeros((pad - size, D), BF))
                    value = values[0] if len(values) == 1 else jnp.concatenate(values, axis=0)
                    target[k * pad : (k + 1) * pad, :] = value
            sums[...] = jnp.zeros_like(sums)

            def first(i, carry):
                lanes = at(i * 256, 256)
                for c in copies(i):
                    c.wait()
                g = dot(xp[...], wg[:, lanes])
                u = dot(xp[...], wu[:, lanes])
                z = dot_nt(yp[...], wd[lanes, :])
                sig = 1.0 / (1.0 + jnp.exp(-g))
                silu = g * sig
                hidden = (silu * u).astype(BF)
                hid[:, lanes] = hidden
                du_out[:, lanes] = (z * silu).astype(BF)
                dg_out[:, lanes] = (z * u * sig * (1.0 + g * (1.0 - sig))).astype(BF)
                sums[...] += jnp.sum(z * hidden.astype(F32), axis=1, keepdims=True)
                return carry

            lax.fori_loop(0, FF // 256, first, 0)

            def second(i, carry):
                cols = at(i * 512, 512)
                back = dot_nt(dg_out[...], wg[cols, :]) + dot_nt(du_out[...], wu[cols, :])
                front = dot(hid[...], wd[:, cols])
                for k in range(S):
                    for n, part in enumerate(outs):
                        low = k * pad + int(starts[n])
                        high = k * pad + int(starts[n + 1])
                        part[k][:, cols] = back[low:high].astype(BF)
                    part = front[k * pad : k * pad + size].astype(BF)
                    if joint:
                        fronts[0][mt[SRC + k], :, cols] = part
                    else:
                        fronts[k][0:size, cols] = part
                    if front_rows > size:
                        fronts[k][size:, cols] = jnp.zeros((front_rows - size, 512), BF)
                return carry

            lax.fori_loop(0, D // 512, second, 0)
            mine = iota((pad, 128), 1) == mt[EXP]
            for k in range(S):
                term = jnp.where(mine, sums[k * pad : (k + 1) * pad, 0:1], 0.0)
                for n, part in enumerate(outs):
                    part[k][:, D:] = term[int(starts[n]) : int(starts[n + 1])].astype(BF)

        result = run(
            body,
            [shaped((b, W), BF) for b in back_sizes for _ in range(S)]
            + (
                [shaped((S, size, D), BF)]
                if joint
                else [shaped((max(size, front_rows), D), BF)] * S
            )
            + [shaped((rows, D), BF)] * 2
            + [shaped((rows, FF), BF)] * 3,
            [meta_s]
            + flat(x_parts)
            + flat(y_parts)
            + [("a", gate_w), ("a", up_w), ("a", down_w)],
            [
                pltpu.VMEM((rows, 128), F32),
                pltpu.VMEM((D, FF), BF),
                pltpu.VMEM((D, FF), BF),
                pltpu.VMEM((FF, D), BF),
                pltpu.SemaphoreType.DMA((3, FF // 256)),
            ],
            alone=True,
        )
        count = len(back_sizes)
        returned = [result[i * S : (i + 1) * S] for i in range(count)]
        rest = result[S * count :]
        return returned, rest[:front_count], rest[front_count:]

    pair = 2 * cap
    rest = flat(near_pairs[:-1])
    rest_rows = pair * (len(near_pairs) - 1)
    (last_back,), last_front, last_kept = expert(
        [(h2_near[-1], pair + cap, 0)],
        [([dy_near], pair + cap, rest_rows)],
        [pair + cap],
        0,
        True,
    )
    (h2_near[0],) = gate(h2_near[0])
    near_back, rest_front, rest_kept = expert(
        [([part], pair, 0) for part in h2_near[:-1]],
        [([dy_near], rest_rows, 0)],
        [pair] * (len(near_pairs) - 1),
        0,
        True,
    )
    arrive(h2_far)
    last_back = exchange(gate(*last_back))
    (far_back,), far_front, far_kept = expert(
        [(h2_far, 3 * cap, 0)], [(dy_far, 3 * cap, 0)], [3 * cap], T + 16
    )
    arrive(last_back)
    far_back = exchange(gate(*far_back))

    def gate_body(*refs):
        m, rest = refs[0], refs[1:]
        tokens = regroup(rest, walk.blocks)
        rest = rest[sum(len(b) for b in walk.blocks) :]
        router, table, key, gates_k, own, *slots = rest
        line = iota((E, T), 0).astype(F32)
        for r in range(N):
            logits = [dot_nt(router[...], t[...]) for t in tokens[r]]
            logits = logits[0] if len(logits) == 1 else jnp.concatenate(logits, axis=1)
            routed = jnp.zeros((E, T), F32)
            for j in range(TOPK):
                routed = jnp.where(line == table[r, j : j + 1, :], 1.0, routed)
            top = jnp.max(jnp.where(routed > 0.0, logits, NEGATIVE), axis=0, keepdims=True)
            terms = jnp.where(routed > 0.0, jnp.exp(logits - top), 0.0)
            gates = terms / jnp.sum(terms, axis=0, keepdims=True)
            if r == 0:
                eye = jnp.where(iota((E, 128), 0) == iota((E, 128), 1), 1.0, 0.0)
                own[...] = dot_tn(gates, eye, EXACT)
            gates_k[r] = jnp.zeros((SP, T), F32)
            for k in range(S):
                value = jnp.sum(
                    jnp.where(line == m[EXP + k].astype(F32), gates, 0.0),
                    axis=0,
                    keepdims=True,
                )
                gates_k[r, k : k + 1, :] = value
                pick = jnp.where(iota((cap, T), 0).astype(F32) == key[r, k : k + 1, :], 1.0, 0.0)
                slots[k][r : r + 1, :] = dot_nt(
                    jnp.broadcast_to(value, (8, T)), pick, EXACT
                )[0:1]

    gate_k, gate_own, *slot_gates = run(
        gate_body,
        [shaped((N, SP, T), F32), shaped((T, 128), F32)] + [shaped((N, cap), F32)] * S,
        [meta_s] + flat(walk.blocks) + [router_t, route_t, keys],
    )

    def mix(group, pieces, split=False, first=0):
        m = len(group)
        wide = pieces[0].shape[-1]
        joint = pieces[0].ndim == 3
        cut = halfway(T)

        def body(*refs):
            mt, key, gate_ = refs[:3]
            rows, outs = refs[3 : 3 + len(pieces)], refs[3 + len(pieces) :]
            used = slice(first * cap, (first + m) * cap)
            for j, r in enumerate(group):
                acc = None
                for k in range(S):
                    slot = key[r, k : k + 1, :] + float(j * cap)
                    hit = iota((m * cap, T), 0).astype(F32) == slot
                    weight = jnp.where(hit, gate_[r, k : k + 1, :], 0.0).astype(BF)
                    source = rows[0][mt[SRC + k], used, :] if joint else rows[k][used, :]
                    term = dot_tn(weight, source)
                    acc = term if acc is None else acc + term
                if split and j == m - 1:
                    outs[j][...] = acc[:cut].astype(BF)
                    outs[j + 1][...] = acc[cut:].astype(BF)
                else:
                    outs[j][...] = acc

        shapes = [shaped((T, wide), F32)] * m
        if split:
            shapes[-1:] = [shaped((cut, wide), BF), shaped((T - cut, wide), BF)]
        return run(body, shapes, [meta_s, keys, gate_k] + pieces)

    def mix_and_step(walk_, group, pieces):
        m = len(group)

        def body(key, gate_, a_in, b_in, *refs):
            rows, outs = refs[:S], refs[S:]
            for j, (r, arrived) in enumerate(zip(group, (a_in, b_in))):
                acc = arrived[...].astype(F32)
                for k in range(S):
                    slot = key[r, k : k + 1, :] + float(j * cap)
                    hit = iota((m * cap, T), 0).astype(F32) == slot
                    weight = jnp.where(hit, gate_[r, k : k + 1, :], 0.0).astype(BF)
                    acc += dot_tn(weight, rows[k][0 : m * cap, :])
                outs[j][...] = acc.astype(BF)

        shape = shaped(walk_.ahead.shape, BF)
        a, b = run(
            body, [shape, shape], [keys, gate_k, walk_.ahead, walk_.behind] + pieces
        )
        walk_.left -= 1
        walk_.ahead, walk_.behind = ring.forward(a), ring.backward(b)

    def row_grad(left, right, scale_left, shape, by_column):
        def body(*refs):
            gates, lefts, rights = refs[:S], refs[S : S + 3], refs[S + 3 : S + 6]
            out, scaled = refs[S + 6 :]
            offset = 0
            source = lefts if scale_left else rights
            for i, group in enumerate((rest, last_pair, far)):
                rows = source[i].shape[0] // S
                spare_rows = rows - len(group) * cap
                for k in range(S):
                    columns = [as_column(gates[k][r : r + 1, :]) for r in group]
                    if spare_rows:
                        columns.append(jnp.zeros((spare_rows, 1), F32))
                    column = jnp.concatenate(columns, axis=0)
                    scaled[offset : offset + rows, :] = (
                        source[i][k * rows : (k + 1) * rows, :].astype(F32) * column
                    ).astype(BF)
                    offset += rows
            plain = rights if scale_left else lefts

            def tile(i, carry):
                cols = at(i * 512, 512)
                other = jnp.concatenate([p[:, cols] for p in plain], axis=0)
                if by_column:
                    out[:, cols] = dot_tn(scaled[...], other)
                else:
                    out[cols, :] = dot_tn(other, scaled[...])
                return carry

            lax.fori_loop(0, D // 512, tile, 0)

        total = sum(a.shape[0] for a in left)
        (result,) = run(
            body,
            [shaped(shape, F32)],
            slot_pieces + list(left) + list(right),
            [pltpu.VMEM((total, FF), BF)],
        )
        return result

    kept = list(zip(rest_kept, last_kept, far_kept))
    x_kept, y_kept, hid_kept, dg_kept, du_kept = kept

    back_parts = {}
    a, b, c = last_pair
    back_parts[a], back_parts[b], back_parts[c] = mix(last_pair, last_back)
    arrive(far_back)
    slot_gates[1:] = gate(*slot_gates[1:])
    far_top, far_bottom = mix(far[2:], far_back, split=True, first=2)
    back = Reduce(ring, chain, far_top, far_bottom)
    slot_pieces = [slot_gates[0]] + [swap(slot_gates[k], k, S) for k in range(1, S)]
    back_parts[far[0]], back_parts[far[1]] = mix(far[:2], far_back)

    def back_step():
        back.step(back_parts[back.left], back_parts[N - back.left])

    back_step()
    arrive(slot_pieces)
    grads = [
        lambda: row_grad(x_kept, dg_kept, False, (D, FF), False),
        lambda: row_grad(x_kept, du_kept, False, (D, FF), False),
    ]
    done_grads = []
    for i in range(len(near_pairs) - 1):
        near_back[i] = exchange(near_back[i])
        if grads:
            done_grads.append(grads.pop(0)())
        arrive(near_back[i])
        if i + 2 == len(near_pairs):
            far_front = exchange(far_front)
        mix_and_step(back, near_pairs[i], near_back[i])
    if grads:
        done_grads.append(grads.pop(0)())
    while back.left > 0:
        back_step()
    grad_gate, grad_up = done_grads
    arrive(far_front)
    y_parts = {}
    y_parts[far[0]], y_parts[far[1]], y_top, y_bottom = mix(far, far_front, split=True)
    back.ahead, back.behind, y_top, y_bottom = gate(back.ahead, back.behind, y_top, y_bottom)
    front = Reduce(ring, chain, y_top, y_bottom)

    extra_rows = -(-(E // 8 * slab + slab) // D) * 8

    def tokens_body(own, ahead, behind, x2, g2, router, gates, hidden, dy_, dx2, da, small):
        total = own[...] + ahead[...].astype(F32) + behind[...].astype(F32)
        gated = total[:, D:]
        dl = gated - gates[...] * jnp.sum(gated, axis=1, keepdims=True)
        grad = total[:, :D] + dot(dl[:, :E], router[...].astype(F32), EXACT)
        small[0:E, :] = dot_tn(dl, hidden[...].astype(F32), EXACT)[:E]
        scale = row_scale(x2[...])
        n2 = x2[...] * scale
        dn = grad * g2[...]
        small[E : E + 8, :] = jnp.broadcast_to(
            jnp.sum(grad * n2, axis=0, keepdims=True), (8, D)
        )
        out = dy_[...].astype(F32) + scale * (
            dn - n2 * jnp.mean(dn * n2, axis=-1, keepdims=True)
        )
        dx2[...] = out
        da[...] = out.astype(BF)

    grad_second, grad_attn, small_two = run(
        tokens_body,
        [shaped((T, D), F32), shaped((T, D), BF), shaped((E + 8, D), F32)],
        [
            back_parts[0],
            back.ahead,
            back.behind,
            x_second,
            gain_two,
            router_t,
            gate_own,
            h2,
            grad_low,
        ],
    )
    da_have = {0: grad_attn}
    bit = S // 2
    front_sent = False
    while bit:
        for k in sorted(da_have):
            if k:
                (da_have[k],) = gate(da_have[k])
            da_have[k ^ bit] = swap(da_have[k], bit, S)
        if bit == S // 2:
            front.step(y_parts[half - 1], y_parts[N - half + 1])
        elif not front_sent:
            (near_front,) = gate(jnp.concatenate(rest_front + last_front, axis=1))
            near_front = [all_to_all(near_front)]
            front_sent = True
        bit //= 2
    da_rows = [da_have[k] for k in range(S)]
    da_rows[1:] = gate(*da_rows[1:])

    def out_grad_body(*refs):
        m, o, das, small = refs[0], refs[1], refs[2 : 2 + S], refs[2 + S]
        outs, full = refs[3 + S : 4 + S + N], refs[4 + S + N]
        da = jnp.concatenate([a[...] for a in das], axis=0)
        if PR % 128:
            full[...] = dot_tn(o[...], da)
        cut = halfway(PR + extra_rows)
        for r in range(N):
            if PR % 128:
                value = full[at(m[SPOT + r] * PR, PR), :]
            else:
                value = dot_tn(o[:, at(m[SPOT + r] * PR, PR)], da)
            place = at(m[r] * slab, slab)
            tail = [small[8 * g : 8 * (g + 1), place] for g in range(E // 8 + 1)]
            used = len(tail) * slab
            room = extra_rows // 8 * D
            if room > used:
                tail.append(jnp.zeros((8, room - used), F32))
            tail = jnp.concatenate(tail, axis=1)
            tail = [tail[:, g * D : (g + 1) * D] for g in range(extra_rows // 8)]
            if r == half:
                whole = jnp.concatenate([value] + tail, axis=0).astype(BF)
                outs[N - 1][...] = whole[:cut]
                outs[N][...] = whole[cut:]
            else:
                target = outs[r - (r > half)]
                target[0:PR, :] = value
                for g in range(extra_rows // 8):
                    target[PR + 8 * g : PR + 8 * (g + 1), :] = tail[g]

    out_cut = halfway(PR + extra_rows)
    *out_list, out_top, out_bottom = run(
        out_grad_body,
        [shaped((PR + extra_rows, D), F32)] * (N - 1)
        + [shaped((out_cut, D), BF), shaped((PR + extra_rows - out_cut, D), BF)],
        [meta_s, attended] + da_rows + [small_two],
        [pltpu.VMEM((QC, D) if PR % 128 else (8, 128), F32)],
    )
    out_parts = {r: out_list[r - (r > half)] for r in range(N) if r != half}
    out_walk = Reduce(ring, chain, out_top, out_bottom)

    def both_steps():
        if out_walk.left > 0:
            out_walk.step(out_parts[out_walk.left], out_parts[N - out_walk.left])

    def do_body(*refs):
        m, das, rest = refs[0], refs[1 : 1 + S], refs[1 + S :]
        parts = regroup(rest, out_blocks)
        do, full, sems = rest[sum(len(b) for b in out_blocks) :]
        for c in fetch_out(m, parts, full, sems):
            c.wait()
        da = jnp.concatenate([a[...] for a in das], axis=0)
        wide = 256 if QC % 256 == 0 else 128

        def tile(i, carry):
            do[:, at(i * wide, wide)] = dot_nt(da, full[at(i * wide, wide), :]).astype(BF)
            return carry

        lax.fori_loop(0, QC // wide, tile, 0)

    (grad_heads,) = run(
        do_body,
        [shaped((L, QC), BF)],
        [meta_s] + da_rows + [("a", b) for b in flat(out_blocks)],
        [pltpu.VMEM((QC, D), BF), pltpu.SemaphoreType.DMA((N, 2))],
    )
    front.ahead, front.behind = gate(front.ahead, front.behind)
    out_walk.step(out_parts[out_walk.left], out_parts[N - out_walk.left])

    def back_body(first_head, count):
        def body(raw_in, rot_in, do_in, krot, vlow, bias_, gq, cos, sin, dk0, dv0, gain0, *rest):
            dq, dk, dv, gain, raw, rot, do, sems = rest
            lanes_here = pl.ds(first_head * HD, count * HD)
            copies = [
                pltpu.make_async_copy(raw_in.at[:, lanes_here], raw, sems.at[0]),
                pltpu.make_async_copy(rot_in.at[:, lanes_here], rot, sems.at[1]),
                pltpu.make_async_copy(do_in.at[:, lanes_here], do, sems.at[2]),
            ]
            for c in copies:
                c.start()
            dk[...] = dk0[...]
            dv[...] = dv0[...]
            gain[...] = gain0[...]
            for c in copies:
                c.wait()

            def head(h, carry):
                lanes = at(h * HD, HD)
                q = rot[:, lanes]
                grad = do[:, lanes]
                p = weights_of(q, krot[...], bias_[...])
                dp = dot_nt(grad, vlow[...])
                centre = jnp.sum(p * dp, axis=-1, keepdims=True)
                ds = (p * (dp - centre)).astype(BF)
                scale = HD ** (-0.5)
                dk[...] += dot_tn(ds, q) * scale
                dv[...] += dot_tn(p.astype(BF), grad)
                dqr = (dot(ds, krot[...]) * scale).astype(BF).astype(F32)
                dqn = turn(dqr, cos[...], -sin[...])
                q_raw = raw[:, lanes]
                factor = row_scale(q_raw)
                nq = q_raw * factor
                gain[0:1, :] += jnp.sum(dqn * nq, axis=0, keepdims=True)
                dn = dqn * gq[0:1, :]
                dq[:, lanes] = (
                    factor * (dn - nq * jnp.mean(dn * nq, axis=-1, keepdims=True))
                ).astype(BF)
                return carry

            lax.fori_loop(0, count, head, 0)

        return body

    calls = 2
    per_call = heads // calls
    grad_k, grad_v = jnp.zeros((L, HD), F32), jnp.zeros((L, HD), F32)
    gain_sum = jnp.zeros((8, 128), F32)
    grad_q = []
    for i in range(calls):
        dq, grad_k, grad_v, gain_sum = run(
            back_body(i * per_call, per_call),
            [
                shaped((L, per_call * HD), BF),
                shaped((L, HD), F32),
                shaped((L, HD), F32),
                shaped((8, 128), F32),
            ],
            [("a", qkv), ("a", q_rot), ("a", grad_heads)]
            + [k_rot, v_low, bias, gain_qk, cosines, sines, grad_k, grad_v, gain_sum],
            [
                pltpu.VMEM((L, per_call * HD), F32),
                pltpu.VMEM((L, per_call * HD), BF),
                pltpu.VMEM((L, per_call * HD), BF),
                pltpu.SemaphoreType.DMA((3,)),
            ],
        )
        grad_q.append(dq)
        both_steps()
    while out_walk.left > 0:
        both_steps()

    def final_y_body(x2, own, ahead, behind, out):
        out[...] = (
            x2[...] + own[...] + ahead[...].astype(F32) + behind[...].astype(F32)
        ).astype(BF)

    if replicas > 1:
        both = jnp.concatenate([grad_k, grad_v], axis=1).astype(BF).astype(F32)
        bit = 1
        while bit < replicas:
            both = both + swap(both.astype(BF), bit, S).astype(F32)
            bit *= 2
        grad_k, grad_v = both[:, :HD], both[:, HD:]

    def key_body(dk, dv, raw_in, gq, cos, sin, gain, dkv, gains, raw, sem):
        c = pltpu.make_async_copy(raw_in.at[:, pl.ds(QC, HD)], raw, sem)
        c.start()
        c.wait()
        k_raw = raw[...]
        factor = row_scale(k_raw)
        nk = k_raw * factor
        dkn = turn(dk[...].astype(BF).astype(F32), cos[...], -sin[...])
        k_part = jnp.sum(dkn * nk, axis=0, keepdims=True) * (1.0 / replicas)
        dn = dkn * gq[1:2, :]
        dk_raw = factor * (dn - nk * jnp.mean(dn * nk, axis=-1, keepdims=True))
        dkv[:, 0:HD] = dk_raw.astype(BF)
        dkv[:, HD:] = dv[...].astype(BF)
        line = iota((8, 128), 0)
        gains[...] = jnp.where(line == 0, gain[0:1, :], jnp.where(line == 1, k_part, 0.0))

    grad_kv, gain_lines = run(
        key_body,
        [shaped((L, 2 * HD), BF), shaped((8, 128), F32)],
        [grad_k, grad_v, ("a", qkv), gain_qk, cosines, sines, gain_sum],
        [pltpu.VMEM((L, HD), F32), pltpu.SemaphoreType.DMA],
    )

    block_rows = slab + 8
    block_cut = halfway(block_rows)

    def weight_grad(offsets, split=False):
        def body(m, h, *rest):
            dqs, rest = rest[:calls], rest[calls:]
            dkv, gains, outs = rest[0], rest[1], rest[2:]
            span = per_call * HD
            for j, r in enumerate(offsets):
                rows = h[:, at(m[r] * slab, slab)]
                pieces = [dot_tn(rows, dq[...]) for dq in dqs] + [dot_tn(rows, dkv[...])]
                spots = [slice(i * span, (i + 1) * span) for i in range(calls)]
                spots.append(slice(QC, C))
                tail = jnp.concatenate([gains[...], jnp.zeros((8, C - 128), F32)], axis=1)
                for spot_, piece_ in zip(spots, pieces):
                    if split:
                        outs[0][:, spot_] = piece_[:block_cut].astype(BF)
                        low = jnp.concatenate([piece_[block_cut:], tail[:, spot_]], axis=0)
                        outs[1][:, spot_] = low.astype(BF)
                    else:
                        outs[j][0:slab, spot_] = piece_
                if not split:
                    outs[j][slab:, :] = tail

        if split:
            shapes = [shaped((block_cut, C), BF), shaped((block_rows - block_cut, C), BF)]
        else:
            shapes = [shaped((block_rows, C), F32)] * len(offsets)
        return run(body, shapes, [meta_s, h1] + grad_q + [grad_kv, gain_lines])

    def total_body(own, ahead, behind, *outs):
        total = own[...] + ahead[...].astype(F32) + behind[...].astype(F32)
        start = 0
        for out in outs:
            out[...] = total[start : start + out.shape[0]].astype(BF)
            start += out.shape[0]

    out_piece, out_tail = run(
        total_body,
        [shaped((PR, D), BF), shaped((extra_rows, D), BF)],
        [out_parts[0], out_walk.ahead, out_walk.behind],
    )
    block_top, block_bottom = weight_grad([half], split=True)
    block_walk = Reduce(ring, chain, block_top, block_bottom)
    out_piece = lax.ppermute(out_piece, ("seq", "shard"), [(b, a) for a, b in spread])
    block_parts = {}

    def more_blocks(offsets):
        block_parts.update(zip(offsets, weight_grad(offsets)))

    def block_step():
        block_walk.step(block_parts[block_walk.left], block_parts[N - block_walk.left])

    more_blocks([half - 1, N - half + 1])
    block_step()
    more_blocks([r for r in range(N) if r not in block_parts and r != half])
    def make_first():
        def body(*refs):
            m, dqs, rest = refs[0], refs[1 : 1 + calls], refs[1 + calls :]
            dkv, rest = rest[0], rest[1:]
            blk = regroup(rest, blocks)
            rest = rest[sum(len(b) for b in blocks) :]
            outs, (full, sems) = rest[:S], rest[S:]
            copies = []
            for r in range(N):
                copies += fetch_block(m, blk[r], r, full, sems)
            share = (dkv[...].astype(F32) * (1.0 / replicas)).astype(BF)
            for c in copies:
                c.wait()
            span = per_call * HD

            def tile(i, carry):
                lanes = at(i * 512, 512)
                value = dot_nt(share, full[lanes, QC:])
                for j in range(calls):
                    value += dot_nt(dqs[j][...], full[lanes, j * span : (j + 1) * span])
                for j, k in enumerate(range(1, S, 2)):
                    outs[j][:, lanes] = value[k * T : (k + 1) * T].astype(BF)
                for j, k in enumerate(range(0, S, 2)):
                    outs[S // 2 + j][:, lanes] = value[k * T : (k + 1) * T]
                return carry

            lax.fori_loop(0, D // 512, tile, 0)

        result = run(
            body,
            reduce_shapes,
            [meta_s] + grad_q + [grad_kv] + [("a", b) for b in flat(blocks)],
            [pltpu.VMEM((D, C), BF), pltpu.SemaphoreType.DMA((N, 2))],
        )
        return result[: S // 2], result[S // 2 :]

    out_have = {0: out_piece}
    tail_have = {0: out_tail}
    bits = []
    while not bits or bits[-1] > 1:
        bits.append(bits[-1] // 2 if bits else S // 2)

    def tail_step():
        bit_ = bits.pop(0) if bits else 0
        pairs = [(have, k) for have in (out_have, tail_have) for k in sorted(have)]
        for have, k in pairs:
            if bit_ and k:
                (have[k],) = gate(have[k])
        if block_walk.left > 0:
            block_step()
        for have, k in pairs:
            if bit_:
                if not k:
                    (have[k],) = gate(have[k])
                have[k ^ bit_] = swap(have[k], bit_, S)

    one_own, one_got = seq_reduce(make_first, tail_step)
    near_front[:] = gate(*near_front)
    for r, part in zip(near, mix(near, near_front)):
        y_parts[r] = part
    while block_walk.left > 0 or bits:
        tail_step()
    front.step(y_parts[front.left], y_parts[N - front.left])
    out_pieces = [out_have[k] for k in range(S)]
    tail_pieces = [tail_have[k] for k in range(S)]
    out_pieces[1:] = gate(*out_pieces[1:])

    def out_join_body(*refs):
        m, pieces, tails = refs[0], refs[1 : 1 + S], refs[1 + S : 1 + 2 * S]
        out, small = refs[1 + 2 * S :]
        for k in range(S):
            out[at(m[QUA + k] * PR, PR), :] = pieces[k][...].astype(F32)
        small[...] = tree_sum([t_[...].astype(F32) for t_ in tails])

    grad_out_w, tail_two = run(
        out_join_body,
        [shaped((S * PR, D), F32), shaped((extra_rows, D), F32)],
        [meta_s] + out_pieces + tail_pieces,
    )

    def inputs_body(x_ref, own, got, g1, dx2, out):
        x = x_ref[...].astype(F32)
        grad = own[...] + got[...].astype(F32)
        scale = row_scale(x)
        n1 = x * scale
        dn = grad * g1[...]
        out[...] = dx2[...] + scale * (
            dn - n1 * jnp.mean(dn * n1, axis=-1, keepdims=True)
        )

    (grad_inputs,) = run(
        inputs_body,
        [shaped((T, D), F32)],
        [inputs[0], one_own, one_got, gain_one, grad_second],
    )

    (block_sum,) = run(
        total_body,
        [shaped((block_rows, C), BF)],
        [block_parts[0], block_walk.ahead, block_walk.behind],
    )
    block_have = {0: block_sum}
    bit = S // 2
    for k in sorted(block_have):
        block_have[k ^ bit] = swap(block_have[k], bit, S)

    grad_down = row_grad(hid_kept, y_kept, True, (FF, D), True)
    while front.left > 0:
        front.step(y_parts[front.left], y_parts[N - front.left])
    while bit > 1:
        bit //= 2
        for k in sorted(block_have):
            if k:
                (block_have[k],) = gate(block_have[k])
            block_have[k ^ bit] = swap(block_have[k], bit, S)
    block_pieces = [block_have[k] for k in range(S)]
    block_pieces[1:] = gate(*block_pieces[1:])

    def join_body(*refs):
        m, pieces = refs[0], refs[1 : 1 + S]
        wq, wk, wv, oq, ok, ov, gains, rows = refs[1 + S :]
        for k in range(S):
            source = m[SRC + k]
            oq[:, at(source * QC, QC)] = pieces[k][0:slab, 0:QC].astype(F32)
            lanes = at(source // replicas * HD, HD)
            ok[:, lanes] = pieces[k][0:slab, QC : QC + HD].astype(F32)
            ov[:, lanes] = pieces[k][0:slab, QC + HD :].astype(F32)
        total = jnp.sum(oq[...] * wq[...].astype(F32), axis=1, keepdims=True)
        total += jnp.sum(ok[...] * wk[...].astype(F32), axis=1, keepdims=True)
        total += jnp.sum(ov[...] * wv[...].astype(F32), axis=1, keepdims=True)
        same = iota((slab, slab), 0) == iota((slab, slab), 1)
        rows[...] = jnp.broadcast_to(
            jnp.sum(jnp.where(same, total, 0.0), axis=0, keepdims=True), (8, slab)
        )
        gains[...] = tree_sum([p[slab:, 0:128].astype(F32) for p in pieces])

    grad_query, grad_key, grad_value, gain_rows, one_rows = run(
        join_body,
        [
            shaped((slab, S * QC), F32),
            shaped((slab, KEY_VALUE_HEADS * HD), F32),
            shaped((slab, KEY_VALUE_HEADS * HD), F32),
            shaped((8, 128), F32),
            shaped((8, slab), F32),
        ],
        [meta_s] + block_pieces + [w_query, key_weight, value_weight],
    )
    (result,) = run(
        final_y_body,
        [shaped((T, D), BF)],
        [x_second, y_parts[0], front.ahead, front.behind],
    )

    grad_gain_one = one_rows[0] / norm1_gain.astype(F32)
    share = HD // N
    grad_qgain = lax.dynamic_slice(gain_rows[0], (d * share,), (share,))
    grad_kgain = lax.dynamic_slice(gain_rows[1], (d * share,), (share,))

    lines = [
        tail_two[8 * g : 8 * (g + 1), i * slab : (i + 1) * slab]
        for g in range(extra_rows // 8)
        for i in range(D // slab)
    ]
    grad_router = jnp.concatenate(lines[: E // 8], axis=0).T
    grad_gain_two = lines[E // 8][0]

    return (
        result[None],
        grad_inputs[None],
        grad_gain_one,
        grad_query,
        grad_key,
        grad_value,
        grad_qgain,
        grad_kgain,
        grad_out_w,
        grad_gain_two,
        grad_router,
        grad_gate[None],
        grad_up[None],
        grad_down[None],
    )


def solution(mesh):
    in_specs = (
        P("shard", "seq", None),
        P("shard", "seq"),
        P("shard", "seq", None),
        P("shard"),
        P("shard", None),
        P("shard", None),
        P("shard", None),
        P("shard"),
        P("shard"),
        P("shard", None),
        P("shard"),
        P("shard", None),
        P(("seq", "shard"), None, None),
        P(("seq", "shard"), None, None),
        P(("seq", "shard"), None, None),
        P("shard", "seq", None),
    )
    out_specs = (
        P("shard", "seq", None),
        P("shard", "seq", None),
        P("shard"),
        P("shard", None),
        P("shard", None),
        P("shard", None),
        P("shard"),
        P("shard"),
        P("shard", None),
        P("shard"),
        P("shard", None),
        P(("seq", "shard"), None, None),
        P(("seq", "shard"), None, None),
        P(("seq", "shard"), None, None),
    )
    return jax.shard_map(
        per_device, mesh=mesh, in_specs=in_specs, out_specs=out_specs, check_vma=False
    )
```

```python
import jax
import jax.numpy as jnp
import numpy as np
from jax import lax
from jax.experimental import pallas as pl
from jax.experimental.pallas import tpu as pltpu
from jax.sharding import PartitionSpec as P

HQ = 32
KEY_VALUE_HEADS = 4
HEAD_DIMENSION = 128
TOPK = 8

EPSILON = 1e-06
ROPE_BASE = 1000000.0
NEGATIVE = -1e30
EXACT = lax.Precision.HIGHEST
BF = jnp.bfloat16
F32 = jnp.float32
I32 = jnp.int32
LIMIT = 8


def ring_order(count):
    width = 4 if count >= 16 else 2
    if count % width or count // width < 2:
        return list(range(count))
    depth = count // width
    order = [z * width for z in range(depth)]
    for turn, z in enumerate(reversed(range(depth))):
        columns = range(1, width) if turn % 2 == 0 else range(width - 1, 0, -1)
        order += [z * width + y for y in columns]
    return order


class Ring:
    def __init__(self, count):
        self.n = count
        self.half = count // 2
        self.order = ring_order(count)
        place = [0] * count
        for i, d in enumerate(self.order):
            place[d] = i
        self.up = [(self.order[i], self.order[(i + 1) % count]) for i in range(count)]
        self.down = [(b, a) for a, b in self.up]
        seats = jnp.arange(count, dtype=I32)
        mine = seats == lax.axis_index("shard")
        me = jnp.sum(jnp.where(mine, jnp.asarray(place, I32), 0))
        ahead = (me + seats) % count
        table = jnp.asarray(self.order, I32)
        self.index = jnp.sum(
            jnp.where(ahead[:, None] == seats[None, :], table[None, :], 0), axis=1
        )

    def forward(self, value):
        return lax.ppermute(value, "shard", self.up)

    def backward(self, value):
        return lax.ppermute(value, "shard", self.down)


def halfway(rows):
    return rows // 2 // 16 * 16


class Gather:
    def __init__(self, ring, chain, value):
        self.ring, self.chain = ring, chain
        n = ring.n
        self.cut = halfway(value.shape[0])
        self.blocks = [None] * n
        self.blocks[0] = [value]
        self.done = 1
        self.blocks[n - 1] = [ring.forward(value)]
        self.blocks[1] = [ring.backward(value)]

    def step(self):
        ring, n, j = self.ring, self.ring.n, self.done
        a, b = self.chain.gate(self.blocks[n - j][0], self.blocks[j][0])
        self.blocks[n - j], self.blocks[j] = [a], [b]
        self.done = j + 1
        if j + 1 < ring.half:
            self.blocks[n - j - 1] = [ring.forward(a)]
            self.blocks[j + 1] = [ring.backward(b)]
        else:
            self.blocks[ring.half] = [
                ring.forward(a[: self.cut]),
                ring.backward(b[self.cut :]),
            ]

    def arrive(self):
        n, j = self.ring.n, self.done
        a, b = self.chain.gate(self.blocks[n - j][0], self.blocks[j][0])
        self.blocks[n - j], self.blocks[j] = [a], [b]

    def finish(self):
        self.blocks[self.ring.half] = list(self.chain.gate(*self.blocks[self.ring.half]))


class Reduce:
    def __init__(self, ring, chain, top, bottom):
        self.ring, self.chain = ring, chain
        self.cut = top.shape[0]
        self.left = ring.half - 1
        self.ahead, self.behind = ring.forward(top), ring.backward(bottom)

    def step(self, part_ahead, part_behind):
        first = self.left == self.ring.half - 1
        cut = self.cut

        def body(a_ref, a_in, b_ref, b_in, a_out, b_out):
            if first:
                a_out[:cut, :] = (a_ref[:cut, :] + a_in[...].astype(F32)).astype(BF)
                a_out[cut:, :] = a_ref[cut:, :].astype(BF)
                b_out[:cut, :] = b_ref[:cut, :].astype(BF)
                b_out[cut:, :] = (b_ref[cut:, :] + b_in[...].astype(F32)).astype(BF)
            else:
                a_out[...] = (a_ref[...] + a_in[...].astype(F32)).astype(BF)
                b_out[...] = (b_ref[...] + b_in[...].astype(F32)).astype(BF)

        shape = shaped(part_ahead.shape, BF)
        a, b = self.chain.run(
            body, [shape, shape], [part_ahead, self.ahead, part_behind, self.behind]
        )
        self.left -= 1
        self.ahead, self.behind = self.ring.forward(a), self.ring.backward(b)


def swap(value, bit, count):
    return lax.ppermute(value, "seq", [(i, i ^ bit) for i in range(count)])


def seq_gather(chain, value, count):
    have = {0: value}
    bit = count // 2
    while bit:
        for k in sorted(have):
            if k:
                (have[k],) = chain.gate(have[k])
            have[k ^ bit] = swap(have[k], bit, count)
        bit //= 2
    return [have[k] for k in range(count)]


def tree_sum(values):
    values = list(values)
    while len(values) > 1:
        values = [values[i] + values[i + 1] for i in range(0, len(values), 2)]
    return values[0]


def shaped(shape, dtype):
    return jax.ShapeDtypeStruct(tuple(shape), dtype)


class Chain:
    def __init__(self):
        self.token = jnp.zeros((8, 128), F32)

    def gate(self, *arrays):
        *arrays, self.token = lax.optimization_barrier(tuple(arrays) + (self.token,))
        return arrays

    def run(self, body, outs, operands, scratch=(), alone=False, streamed=False):
        spaces = {"s": pltpu.SMEM, "a": pl.ANY, "v": pltpu.VMEM}
        specs, arrays = [], []
        for item in operands:
            kind, array = item if isinstance(item, tuple) else ("v", item)
            specs.append(pl.BlockSpec(memory_space=spaces[kind]))
            arrays.append(array)
        first = max(range(len(arrays)), key=lambda i: arrays[i].ndim > 1)
        (arrays[first],) = self.gate(arrays[first])
        need = 0
        for spec, array in list(zip(specs, arrays)) + [(None, o) for o in outs]:
            if spec is None or spec.memory_space == pltpu.VMEM:
                need += array.size * array.dtype.itemsize
        for item in scratch:
            if getattr(item, "memory_space", None) == pltpu.VMEM:
                need += int(np.prod(item.shape)) * jnp.dtype(item.dtype).itemsize
        limit = 60 << 20 if alone else min(60 << 20, need * 3 // 2 + (LIMIT << 20))
        results = list(
            pl.pallas_call(
                body,
                out_shape=list(outs),
                in_specs=specs,
                out_specs=[pl.BlockSpec(memory_space=pl.ANY if streamed else pltpu.VMEM)]
                * len(outs),
                scratch_shapes=list(scratch),
                compiler_params=pltpu.CompilerParams(vmem_limit_bytes=limit),
                cost_estimate=pl.CostEstimate(
                    flops=1 << 20, bytes_accessed=1 << 16, transcendentals=0
                ),
            )(*arrays)
        )
        (results[-1],) = self.gate(results[-1])
        return results


def dot(a, b, precision=None):
    return jnp.dot(a, b, preferred_element_type=F32, precision=precision)


def dot_nt(a, b, precision=None):
    return lax.dot_general(
        a, b, (((1,), (1,)), ((), ())), preferred_element_type=F32, precision=precision
    )


def dot_tn(a, b, precision=None):
    return lax.dot_general(
        a, b, (((0,), (0,)), ((), ())), preferred_element_type=F32, precision=precision
    )


def iota(shape, dim):
    return lax.broadcasted_iota(I32, shape, dim)


def at(start, size):
    return pl.ds(pl.multiple_of(start, size), size)


def row_scale(values):
    return lax.rsqrt(jnp.mean(values * values, axis=-1, keepdims=True) + EPSILON)


def as_column(row):
    size = row.shape[-1]
    same = iota((size, size), 0) == iota((size, size), 1)
    return jnp.sum(jnp.where(same, row, 0.0), axis=1, keepdims=True)


def turn(values, cosines, sines):
    return values * cosines + pltpu.roll(values, HEAD_DIMENSION // 2, 1) * sines


def weights_of(query, keys, bias):
    scores = dot_nt(query, keys) * HEAD_DIMENSION ** (-0.5) + bias
    terms = jnp.exp(scores - jnp.max(scores, axis=-1, keepdims=True))
    return terms * (1.0 / jnp.sum(terms, axis=-1, keepdims=True))


def flat(lists):
    return [a for part in lists for a in part]


def regroup(refs, lists):
    out, i = [], 0
    for part in lists:
        out.append(refs[i : i + len(part)])
        i += len(part)
    return out


def per_device(
    inputs,
    seq_ids,
    routes,
    norm1_gain,
    w_query,
    key_weight,
    value_weight,
    q_gain,
    k_gain,
    w_out,
    norm2_gain,
    w_router,
    w_gate,
    w_up,
    w_down,
    cotangent,
):
    T = inputs.shape[1]
    D = inputs.shape[2]
    S = lax.axis_size("seq")
    N = lax.axis_size("shard")
    s = lax.axis_index("seq")
    d = lax.axis_index("shard")
    ring = Ring(N)
    half = ring.half
    chain = Chain()
    run, gate = chain.run, chain.gate
    heads = HQ // S
    replicas = S // KEY_VALUE_HEADS
    HD = HEAD_DIMENSION
    L = T * S
    E = S * N
    SP = -(-S // 8) * 8
    FF = w_gate.shape[2]
    cap = max(2, T * TOPK * 5 // (4 * E))
    slab = D // N
    QC = heads * HD
    C = QC + 2 * HD
    PR = w_out.shape[0] // S
    W = D + 128

    if (S, N) == (4, 8):
        quarter = [2, 0, 3, 1]
        spot = ring.index % 2 * 4 + ring.index // 2
        spread = []
        for s_to in range(S):
            for d_to in range(N):
                s_from = quarter.index(d_to // 2)
                spread.append((s_from * N + 2 * s_to + d_to % 2, s_to * N + d_to))
    else:
        quarter = list(range(S))
        spot = ring.index
        spread = [((g % S) * N + g // S, g) for g in range(S * N)]
    seat_s = jnp.arange(S, dtype=I32)
    sources = seat_s ^ s
    quarters = jnp.asarray(quarter, I32)
    quarter_of = jnp.sum(
        jnp.where(sources[:, None] == seat_s[None, :], quarters[None, :], 0), axis=1
    )
    meta = jnp.concatenate(
        [ring.index, spot, sources, sources * N + d, quarter_of]
    ).astype(I32)
    meta_s = ("s", meta)
    SPOT, SRC, EXP, QUA = N, 2 * N, 2 * N + S, 2 * N + 2 * S

    XR = 16
    while E % XR or (E // XR) * slab + slab + 128 + T > C:
        XR *= 2
    groups = E // XR
    misc = groups * slab
    spare = C - (misc + slab + 128 + T)

    seat = jnp.arange(128, dtype=I32)[None, :] // (128 // N) == d
    both_gains = jnp.stack([norm1_gain, norm2_gain])
    head_gains = jnp.where(
        seat, jnp.tile(jnp.stack([q_gain, k_gain]), (1, N)), jnp.zeros((), BF)
    )

    def pack_body(m, wq, wk, wv, gains, head_gain, router, table, out, sems):
        me = m[0]
        copies = [
            pltpu.make_async_copy(
                wq.at[:, at(me * QC, QC)], out.at[pl.ds(0, slab), pl.ds(0, QC)], sems.at[0]
            ),
            pltpu.make_async_copy(
                wk.at[:, at(me // replicas * HD, HD)],
                out.at[pl.ds(0, slab), pl.ds(QC, HD)],
                sems.at[1],
            ),
            pltpu.make_async_copy(
                wv.at[:, at(me // replicas * HD, HD)],
                out.at[pl.ds(0, slab), pl.ds(QC + HD, HD)],
                sems.at[2],
            ),
        ]
        for c in copies:
            c.start()
        low = pl.ds(slab, XR)
        for g in range(groups):
            out[low, g * slab : (g + 1) * slab] = router[g * XR : (g + 1) * XR, :]

        def two(pair, size):
            line = iota((XR, size), 0)
            pair = pair[...].astype(F32)
            return jnp.where(
                line == 0, pair[0:1], jnp.where(line == 8, pair[1:2], 0.0)
            ).astype(BF)

        out[low, misc : misc + slab] = two(gains, slab)
        out[low, misc + slab : misc + slab + 128] = two(head_gain, 128)
        lines = table[...].astype(F32)
        lines = jnp.concatenate([lines, jnp.zeros((XR - TOPK, T), F32)], axis=0)
        out[low, misc + slab + 128 : misc + slab + 128 + T] = lines.astype(BF)
        if spare:
            out[low, C - spare :] = jnp.zeros((XR, spare), BF)
        for c in copies:
            c.wait()

    (block,) = run(
        pack_body,
        [shaped((slab + XR, C), BF)],
        [
            ("s", s.reshape(1).astype(I32)),
            ("a", w_query),
            ("a", key_weight),
            ("a", value_weight),
            both_gains,
            head_gains,
            w_router.T,
            routes[0].T,
        ],
        [pltpu.SemaphoreType.DMA((3,))],
        alone=True,
    )
    first = Gather(ring, chain, block)
    IR = 16

    def rows_body(x, ids, out):
        out[0:T, :] = x[...]
        line = jnp.broadcast_to(ids[...].astype(F32), (IR, T))
        out[T:, 0:T] = line.astype(BF)
        out[T:, T:] = jnp.zeros((IR, D - T), BF)

    (x_own,) = run(rows_body, [shaped((T + IR, D), BF)], [inputs[0], seq_ids])
    x_have = {0: x_own}
    bit = S // 2
    for step in range(half - 1):
        if bit:
            for k in sorted(x_have):
                if k:
                    (x_have[k],) = gate(x_have[k])
                x_have[k ^ bit] = swap(x_have[k], bit, S)
            bit //= 2
        first.step()
        if step == 0:
            piece = lax.dynamic_slice(w_out, (quarter_of[0] * PR, 0), (PR, D))
            (piece,) = gate(piece)
            piece = lax.ppermute(piece, ("seq", "shard"), spread)
    x_rows = [x_have[k] for k in range(S)]
    x_rows[1:] = gate(*x_rows[1:])

    positions = (sources[:, None] * T + jnp.arange(T, dtype=I32)).reshape(-1)
    inverse = ROPE_BASE ** (-2.0 * jnp.arange(HD // 2, dtype=F32) / HD)
    angles = positions.astype(F32)[:, None] * inverse[None, :]
    cosines, sines = jnp.cos(angles), jnp.sin(angles)
    cosines = jnp.concatenate([cosines, cosines], axis=1)
    sines = jnp.concatenate([-sines, sines], axis=1)
    cosines, sines, piece = gate(cosines, sines, piece)

    first.finish()
    blocks = first.blocks
    grad_low = cotangent[0]
    (dy_low,) = gate(grad_low)
    dy = Gather(ring, chain, dy_low)

    def fetch_block(m, parts, r, full, sem):
        copies, start = [], 0
        for i, part in enumerate(parts):
            rows = min(slab - start, part.shape[0])
            if rows > 0:
                base = pl.multiple_of(m[r] * slab + start, 16)
                copies.append(
                    pltpu.make_async_copy(
                        part.at[pl.ds(0, rows)], full.at[pl.ds(base, rows)], sem.at[r, i]
                    )
                )
            start += part.shape[0]
        for c in copies:
            c.start()
        return copies

    def project_body(*refs):
        m, xs = refs[0], refs[1 : 1 + S]
        cos, sin = refs[1 + S : 3 + S]
        rest = refs[3 + S :]
        blk = regroup(rest, blocks)
        rest = rest[sum(len(b) for b in blocks) :]
        h1, raw, krot, vlow, bias, g1, g2, gq, router, table, keys = rest[:11]
        full, ext, sems, ext_sems = rest[11:]
        small, copies = [], []
        for r in range(N):
            last = blk[r][-1]
            c = pltpu.make_async_copy(
                last.at[pl.ds(last.shape[0] - XR, XR)], ext.at[r], ext_sems.at[r]
            )
            c.start()
            small.append(c)
        for r in range(N):
            copies += fetch_block(m, blk[r], r, full, sems)

        id_f = [x[T : T + IR, 0:T].astype(F32)[0:1] for x in xs]
        for a in range(S):
            column = as_column(id_f[a])
            q_pos = m[SRC + a] * T + iota((T, T), 0)
            for b in range(S):
                k_pos = m[SRC + b] * T + iota((T, T), 1)
                allowed = (k_pos <= q_pos) & (column == id_f[b])
                bias[a * T : (a + 1) * T, b * T : (b + 1) * T] = jnp.where(
                    allowed, 0.0, NEGATIVE
                )

        for c in small:
            c.wait()
        gq[...] = jnp.zeros((8, 128), F32)
        for r in range(N):
            place = at(m[r] * slab, slab)
            for g in range(groups):
                router[g * XR : (g + 1) * XR, place] = ext[r, :, g * slab : (g + 1) * slab]
            gains = ext[r, :, misc : misc + slab].astype(F32)
            g1[:, place] = gains[0:1]
            g2[:, place] = gains[8:9]
            pair = ext[r, :, misc + slab : misc + slab + 128].astype(F32)
            gq[0:1, :] += pair[0:1]
            gq[1:2, :] += pair[8:9]
            lines = ext[r, :, misc + slab + 128 : misc + slab + 128 + T].astype(F32)[:TOPK]
            table[r] = lines
            keys[r] = jnp.zeros((SP, T), F32)
            for k in range(S):
                expert = m[EXP + k].astype(F32)
                keys[r, k : k + 1, :] = jnp.max(
                    jnp.where(lines == expert, 1.0, 0.0), axis=0, keepdims=True
                )
        hits = keys[...].reshape(N * SP, T)
        earlier = jnp.where(iota((T, T), 0) < iota((T, T), 1), 1.0, 0.0).astype(BF)
        ranks = dot(hits.astype(BF), earlier)
        keys[...] = jnp.where(hits > 0.0, ranks, -1e6).reshape(N, SP, T)

        for k in range(S):
            x = xs[k][0:T, :].astype(F32)
            h1[k * T : (k + 1) * T, :] = (x * row_scale(x) * g1[...]).astype(BF)
        for c in copies:
            c.wait()

        wide = 256 if C % 256 == 0 else 128

        def project(i, carry):
            raw[:, at(i * wide, wide)] = dot(h1[...], full[:, at(i * wide, wide)])
            return carry

        lax.fori_loop(0, C // wide, project, 0)
        k_raw = raw[:, QC : QC + HD]
        krot[...] = turn(k_raw * row_scale(k_raw) * gq[1:2, :], cos[...], sin[...]).astype(BF)
        vlow[...] = raw[:, QC + HD :].astype(BF)

    (
        h1,
        qkv,
        k_rot,
        v_low,
        bias,
        gain_one,
        gain_two,
        gain_qk,
        router_t,
        route_t,
        keys,
    ) = run(
        project_body,
        [
            shaped((L, D), BF),
            shaped((L, C), F32),
            shaped((L, HD), BF),
            shaped((L, HD), BF),
            shaped((L, L), F32),
            shaped((1, D), F32),
            shaped((1, D), F32),
            shaped((8, 128), F32),
            shaped((E, D), BF),
            shaped((N, TOPK, T), F32),
            shaped((N, SP, T), F32),
        ],
        [meta_s] + x_rows + [cosines, sines] + [("a", b) for b in flat(blocks)],
        [
            pltpu.VMEM((D, C), BF),
            pltpu.VMEM((N, XR, C), BF),
            pltpu.SemaphoreType.DMA((N, 2)),
            pltpu.SemaphoreType.DMA((N,)),
        ],
        alone=True,
    )

    def attend_body(first_head, count):
        def body(raw_in, krot, vlow, bias_, gq, cos, sin, rot, out, raw, sem):
            c = pltpu.make_async_copy(
                raw_in.at[:, pl.ds(first_head * HD, count * HD)], raw, sem
            )
            c.start()
            c.wait()

            def head(h, carry):
                lanes = at(h * HD, HD)
                q_raw = raw[:, lanes]
                q = turn(q_raw * row_scale(q_raw) * gq[0:1, :], cos[...], sin[...]).astype(BF)
                rot[:, lanes] = q
                p = weights_of(q, krot[...], bias_[...]).astype(BF)
                out[:, lanes] = dot(p, vlow[...]).astype(BF)
                return carry

            lax.fori_loop(0, count, head, 0)

        return body

    near_pairs = [[j, N - j] for j in range(half - 2, 0, -1)]
    near = flat(near_pairs) + [0]
    far = [half - 1, N - half + 1, half]

    def select(token_blocks, groups, rows=0, joint=False):
        order = flat(groups)
        chosen = [token_blocks[r] for r in order]
        size = len(order) * cap
        rows = max(rows, size)

        def body(*refs):
            mt, key, rest = refs[0], refs[1], refs[2:]
            tokens = regroup(rest, chosen)
            outs = rest[sum(len(b) for b in chosen) :]
            start = i = 0
            for group in groups:
                m = len(group)
                values = []
                for j in range(m):
                    parts = [t[...] for t in tokens[i + j]]
                    values.append(parts[0] if len(parts) == 1 else jnp.concatenate(parts, axis=0))
                for k in range(S):
                    acc = None
                    for j, r in enumerate(group):
                        slot = key[r, k : k + 1, :] + float(j * cap)
                        pick = jnp.where(
                            iota((m * cap, T), 0).astype(F32) == slot, 1.0, 0.0
                        ).astype(BF)
                        term = dot(pick, values[j])
                        acc = term if acc is None else acc + term
                    if joint:
                        outs[0][mt[SRC + k], start : start + m * cap, :] = acc.astype(BF)
                    else:
                        outs[k][start : start + m * cap, :] = acc.astype(BF)
                start += m * cap
                i += m
            if rows > size:
                for k in range(S):
                    outs[k][size:, :] = jnp.zeros((rows - size, D), BF)

        shapes = [shaped((S, rows, D), BF)] if joint else [shaped((rows, D), BF)] * S
        return run(body, shapes, [meta_s, keys] + flat(chosen))

    def exchange(pieces):
        return [pieces[0]] + [swap(pieces[k], k, S) for k in range(1, S)]

    def arrive(pieces):
        pieces[1:] = gate(*pieces[1:])

    def all_to_all(rows):
        return lax.all_to_all(rows, "seq", 0, 0, tiled=True)

    last_pair = near_pairs[-1] + [0]
    longer = T + 8
    dy.step()
    calls = 2
    per_call = heads // calls
    q_rot, attended = [], []

    def attend(i):
        rot, out = run(
            attend_body(i * per_call, per_call),
            [shaped((L, per_call * HD), BF)] * 2,
            [("a", qkv), k_rot, v_low, bias, gain_qk, cosines, sines],
            [pltpu.VMEM((L, per_call * HD), F32), pltpu.SemaphoreType.DMA],
        )
        q_rot.append(rot)
        attended.append(out)

    attend(0)
    for j in range(2, half - 1):
        dy.arrive()
        if j + 1 < half - 1:
            dy.step()
    (piece,) = gate(piece)
    out_ring = Gather(ring, chain, piece)
    attend(1)
    (dy_near,) = select(dy.blocks, near_pairs + [[0]], joint=True)
    dy_near = all_to_all(dy_near)
    while out_ring.done < half:
        out_ring.step()
    out_ring.finish()
    out_blocks = out_ring.blocks
    dy.step()

    def fetch_out(m, parts, full, sems):
        copies = []
        for r in range(N):
            start = 0
            for i, part in enumerate(parts[r]):
                rows = part.shape[0]
                base = pl.multiple_of(m[SPOT + r] * PR + start, 16)
                copies.append(
                    pltpu.make_async_copy(part, full.at[pl.ds(base, rows)], sems.at[r, i])
                )
                start += rows
        for c in copies:
            c.start()
        return copies

    def seq_reduce(make, ring_step=None):
        sent, kept = make()
        have = dict(zip(range(0, S, 2), kept))
        if ring_step is not None:
            ring_step()
        got = [swap(v, 1, S) for v in sent]
        bit = 2
        while bit < S:
            keys_sent = [k for k in sorted(have) if k & bit]
            keys_kept = [k for k in sorted(have) if not k & bit]
            order = sorted(have)

            def body(*refs):
                n = len(order)
                values, arrived, outs = refs[:n], refs[n : 2 * n], refs[2 * n :]
                total = {
                    k: values[i][...] + arrived[i][...].astype(F32)
                    for i, k in enumerate(order)
                }
                for i, k in enumerate(keys_sent):
                    outs[i][...] = total[k].astype(BF)
                for i, k in enumerate(keys_kept):
                    outs[len(keys_sent) + i][...] = total[k]

            result = run(
                body,
                [shaped((T, D), BF)] * len(keys_sent)
                + [shaped((T, D), F32)] * len(keys_kept),
                [have[k] for k in order] + got,
            )
            sent, kept = result[: len(keys_sent)], result[len(keys_sent) :]
            have = dict(zip(keys_kept, kept))
            if ring_step is not None:
                ring_step()
            got = [swap(v, bit, S) for v in sent]
            bit *= 2
        return have[0], got[0]

    reduce_shapes = [shaped((T, D), BF)] * (S // 2) + [shaped((T, D), F32)] * (S // 2)

    def make_output():
        def body(*refs):
            m, os, rest = refs[0], refs[1 : 1 + calls], refs[1 + calls :]
            o = jnp.concatenate([x[...] for x in os], axis=1)
            parts = regroup(rest, out_blocks)
            rest = rest[sum(len(b) for b in out_blocks) :]
            outs, (full, sems) = rest[:S], rest[S:]
            for c in fetch_out(m, parts, full, sems):
                c.wait()

            def tile(i, carry):
                lanes = at(i * 512, 512)
                value = dot(o, full[:, lanes])
                for j, k in enumerate(range(1, S, 2)):
                    outs[j][:, lanes] = value[k * T : (k + 1) * T].astype(BF)
                for j, k in enumerate(range(0, S, 2)):
                    outs[S // 2 + j][:, lanes] = value[k * T : (k + 1) * T]
                return carry

            lax.fori_loop(0, D // 512, tile, 0)

        result = run(
            body,
            reduce_shapes,
            [meta_s] + attended + [("a", b) for b in flat(out_blocks)],
            [pltpu.VMEM((QC, D), BF), pltpu.SemaphoreType.DMA((N, 2))],
        )
        return result[: S // 2], result[S // 2 :]

    x2_own, x2_got = seq_reduce(make_output)
    (dy_near,) = gate(dy_near)
    dy.step()
    (x2_got,) = gate(x2_got)

    def second_body(x, own, got, g2, x2_out, h2_out):
        x2 = x[...].astype(F32) + own[...] + got[...].astype(F32)
        x2_out[...] = x2
        h2_out[...] = (x2 * row_scale(x2) * g2[...]).astype(BF)

    x_second, h2 = run(
        second_body,
        [shaped((T, D), F32), shaped((T, D), BF)],
        [inputs[0], x2_own, x2_got, gain_two],
    )

    dy.finish()
    (h2,) = gate(h2)
    walk = Gather(ring, chain, h2)
    dy_far = exchange(select(dy.blocks, [far], longer))
    h2_near = [None] * (len(near_pairs))
    walk.step()
    picked = select(walk.blocks, [near_pairs[-1], [0]], longer)
    arrive(dy_far)
    moving = h2_near[-1] = exchange(picked)
    for j in range(2, half):
        walk.step()
        if j < half - 1:
            (picked,) = select(walk.blocks, [[j, N - j]], joint=True)
            if j == half - 2:
                walk.step()
                walk.finish()
                far_rows = select(walk.blocks, [far])
            if j == 2:
                arrive(moving)
            else:
                (h2_near[half - 1 - j],) = gate(h2_near[half - 1 - j])
            (picked,) = gate(picked)
            h2_near[half - 2 - j] = all_to_all(picked)
            if j == half - 2:
                break
    h2_far = exchange(gate(*far_rows))

    gate_w, up_w, down_w = w_gate[0], w_up[0], w_down[0]

    def expert(x_parts, y_parts, back_sizes, front_rows=0, joint=False):
        x_used = [slice(low, low + used) for _, used, low in x_parts]
        y_used = [slice(low, low + used) for _, used, low in y_parts]
        size = sum(used for _, used, _ in x_parts)
        x_parts = [part for part, _, _ in x_parts]
        y_parts = [part for part, _, _ in y_parts]
        pad = -(-size // 16) * 16
        rows = S * pad
        starts = np.cumsum([0] + list(back_sizes))
        front_count = 1 if joint else S

        def body(*refs):
            mt, rest = refs[0], refs[1:]
            xs = regroup(rest, x_parts)
            rest = rest[sum(len(p) for p in x_parts) :]
            ys = regroup(rest, y_parts)
            rest = rest[sum(len(p) for p in y_parts) :]
            wg_in, wu_in, wd_in = rest[:3]
            rest = rest[3:]
            outs = [rest[i * S : (i + 1) * S] for i in range(len(back_sizes))]
            rest = rest[S * len(back_sizes) :]
            fronts, rest = rest[:front_count], rest[front_count:]
            xp, yp, hid, dg_out, du_out, sums, wg, wu, wd, sems = rest

            def copies(i):
                lanes = at(i * 256, 256)
                return [
                    pltpu.make_async_copy(wg_in.at[:, lanes], wg.at[:, lanes], sems.at[0, i]),
                    pltpu.make_async_copy(wu_in.at[:, lanes], wu.at[:, lanes], sems.at[1, i]),
                    pltpu.make_async_copy(wd_in.at[lanes, :], wd.at[lanes, :], sems.at[2, i]),
                ]

            for i in range(FF // 256):
                for c in copies(i):
                    c.start()
            for k in range(S):
                for sources_, used, target in ((xs, x_used, xp), (ys, y_used, yp)):
                    values = [
                        part[0][mt[SRC + k], n, :] if len(part) == 1 else part[k][n, :]
                        for part, n in zip(sources_, used)
                    ]
                    if pad > size:
                        values.append(jnp.zeros((pad - size, D), BF))
                    value = values[0] if len(values) == 1 else jnp.concatenate(values, axis=0)
                    target[k * pad : (k + 1) * pad, :] = value
            sums[...] = jnp.zeros_like(sums)

            def first(i, carry):
                lanes = at(i * 256, 256)
                for c in copies(i):
                    c.wait()
                g = dot(xp[...], wg[:, lanes])
                u = dot(xp[...], wu[:, lanes])
                z = dot_nt(yp[...], wd[lanes, :])
                sig = 1.0 / (1.0 + jnp.exp(-g))
                silu = g * sig
                hidden = (silu * u).astype(BF)
                hid[:, lanes] = hidden
                du_out[:, lanes] = (z * silu).astype(BF)
                dg_out[:, lanes] = (z * u * sig * (1.0 + g * (1.0 - sig))).astype(BF)
                sums[...] += jnp.sum(z * hidden.astype(F32), axis=1, keepdims=True)
                return carry

            lax.fori_loop(0, FF // 256, first, 0)

            def second(i, carry):
                cols = at(i * 512, 512)
                back = dot_nt(dg_out[...], wg[cols, :]) + dot_nt(du_out[...], wu[cols, :])
                front = dot(hid[...], wd[:, cols])
                for k in range(S):
                    for n, part in enumerate(outs):
                        low = k * pad + int(starts[n])
                        high = k * pad + int(starts[n + 1])
                        part[k][:, cols] = back[low:high].astype(BF)
                    part = front[k * pad : k * pad + size].astype(BF)
                    if joint:
                        fronts[0][mt[SRC + k], :, cols] = part
                    else:
                        fronts[k][0:size, cols] = part
                    if front_rows > size:
                        fronts[k][size:, cols] = jnp.zeros((front_rows - size, 512), BF)
                return carry

            lax.fori_loop(0, D // 512, second, 0)
            mine = iota((pad, 128), 1) == mt[EXP]
            for k in range(S):
                term = jnp.where(mine, sums[k * pad : (k + 1) * pad, 0:1], 0.0)
                for n, part in enumerate(outs):
                    part[k][:, D:] = term[int(starts[n]) : int(starts[n + 1])].astype(BF)

        result = run(
            body,
            [shaped((b, W), BF) for b in back_sizes for _ in range(S)]
            + (
                [shaped((S, size, D), BF)]
                if joint
                else [shaped((max(size, front_rows), D), BF)] * S
            )
            + [shaped((rows, D), BF)] * 2
            + [shaped((rows, FF), BF)] * 3,
            [meta_s]
            + flat(x_parts)
            + flat(y_parts)
            + [("a", gate_w), ("a", up_w), ("a", down_w)],
            [
                pltpu.VMEM((rows, 128), F32),
                pltpu.VMEM((D, FF), BF),
                pltpu.VMEM((D, FF), BF),
                pltpu.VMEM((FF, D), BF),
                pltpu.SemaphoreType.DMA((3, FF // 256)),
            ],
            alone=True,
        )
        count = len(back_sizes)
        returned = [result[i * S : (i + 1) * S] for i in range(count)]
        rest = result[S * count :]
        return returned, rest[:front_count], rest[front_count:]

    pair = 2 * cap
    rest = flat(near_pairs[:-1])
    rest_rows = pair * (len(near_pairs) - 1)
    (last_back,), last_front, last_kept = expert(
        [(h2_near[-1], pair + cap, 0)],
        [([dy_near], pair + cap, rest_rows)],
        [pair + cap],
        0,
        True,
    )
    (h2_near[0],) = gate(h2_near[0])
    near_back, rest_front, rest_kept = expert(
        [([part], pair, 0) for part in h2_near[:-1]],
        [([dy_near], rest_rows, 0)],
        [pair] * (len(near_pairs) - 1),
        0,
        True,
    )
    arrive(h2_far)
    last_back = exchange(gate(*last_back))
    (far_back,), far_front, far_kept = expert(
        [(h2_far, 3 * cap, 0)], [(dy_far, 3 * cap, 0)], [3 * cap], T + 16
    )
    arrive(last_back)
    far_back = exchange(gate(*far_back))

    def gate_body(*refs):
        m, rest = refs[0], refs[1:]
        tokens = regroup(rest, walk.blocks)
        rest = rest[sum(len(b) for b in walk.blocks) :]
        router, table, key, gates_k, own, *slots = rest
        line = iota((E, T), 0).astype(F32)
        for r in range(N):
            logits = [dot_nt(router[...], t[...]) for t in tokens[r]]
            logits = logits[0] if len(logits) == 1 else jnp.concatenate(logits, axis=1)
            routed = jnp.zeros((E, T), F32)
            for j in range(TOPK):
                routed = jnp.where(line == table[r, j : j + 1, :], 1.0, routed)
            top = jnp.max(jnp.where(routed > 0.0, logits, NEGATIVE), axis=0, keepdims=True)
            terms = jnp.where(routed > 0.0, jnp.exp(logits - top), 0.0)
            gates = terms / jnp.sum(terms, axis=0, keepdims=True)
            if r == 0:
                eye = jnp.where(iota((E, 128), 0) == iota((E, 128), 1), 1.0, 0.0)
                own[...] = dot_tn(gates, eye, EXACT)
            gates_k[r] = jnp.zeros((SP, T), F32)
            for k in range(S):
                value = jnp.sum(
                    jnp.where(line == m[EXP + k].astype(F32), gates, 0.0),
                    axis=0,
                    keepdims=True,
                )
                gates_k[r, k : k + 1, :] = value
                pick = jnp.where(iota((cap, T), 0).astype(F32) == key[r, k : k + 1, :], 1.0, 0.0)
                slots[k][r : r + 1, :] = dot_nt(
                    jnp.broadcast_to(value, (8, T)), pick, EXACT
                )[0:1]

    gate_k, gate_own, *slot_gates = run(
        gate_body,
        [shaped((N, SP, T), F32), shaped((T, 128), F32)] + [shaped((N, cap), F32)] * S,
        [meta_s] + flat(walk.blocks) + [router_t, route_t, keys],
    )

    def mix(group, pieces, split=False, first=0):
        m = len(group)
        wide = pieces[0].shape[-1]
        joint = pieces[0].ndim == 3
        cut = halfway(T)

        def body(*refs):
            mt, key, gate_ = refs[:3]
            rows, outs = refs[3 : 3 + len(pieces)], refs[3 + len(pieces) :]
            used = slice(first * cap, (first + m) * cap)
            for j, r in enumerate(group):
                acc = None
                for k in range(S):
                    slot = key[r, k : k + 1, :] + float(j * cap)
                    hit = iota((m * cap, T), 0).astype(F32) == slot
                    weight = jnp.where(hit, gate_[r, k : k + 1, :], 0.0).astype(BF)
                    source = rows[0][mt[SRC + k], used, :] if joint else rows[k][used, :]
                    term = dot_tn(weight, source)
                    acc = term if acc is None else acc + term
                if split and j == m - 1:
                    outs[j][...] = acc[:cut].astype(BF)
                    outs[j + 1][...] = acc[cut:].astype(BF)
                else:
                    outs[j][...] = acc

        shapes = [shaped((T, wide), F32)] * m
        if split:
            shapes[-1:] = [shaped((cut, wide), BF), shaped((T - cut, wide), BF)]
        return run(body, shapes, [meta_s, keys, gate_k] + pieces)

    def mix_and_step(walk_, group, pieces):
        m = len(group)

        def body(key, gate_, a_in, b_in, *refs):
            rows, outs = refs[:S], refs[S:]
            for j, (r, arrived) in enumerate(zip(group, (a_in, b_in))):
                acc = arrived[...].astype(F32)
                for k in range(S):
                    slot = key[r, k : k + 1, :] + float(j * cap)
                    hit = iota((m * cap, T), 0).astype(F32) == slot
                    weight = jnp.where(hit, gate_[r, k : k + 1, :], 0.0).astype(BF)
                    acc += dot_tn(weight, rows[k][0 : m * cap, :])
                outs[j][...] = acc.astype(BF)

        shape = shaped(walk_.ahead.shape, BF)
        a, b = run(
            body, [shape, shape], [keys, gate_k, walk_.ahead, walk_.behind] + pieces
        )
        walk_.left -= 1
        walk_.ahead, walk_.behind = ring.forward(a), ring.backward(b)

    def row_grad(left, right, scale_left, shape, by_column):
        def body(*refs):
            gates, lefts, rights = refs[:S], refs[S : S + 3], refs[S + 3 : S + 6]
            out, scaled = refs[S + 6 :]
            offset = 0
            source = lefts if scale_left else rights
            for i, group in enumerate((rest, last_pair, far)):
                rows = source[i].shape[0] // S
                spare_rows = rows - len(group) * cap
                for k in range(S):
                    columns = [as_column(gates[k][r : r + 1, :]) for r in group]
                    if spare_rows:
                        columns.append(jnp.zeros((spare_rows, 1), F32))
                    column = jnp.concatenate(columns, axis=0)
                    scaled[offset : offset + rows, :] = (
                        source[i][k * rows : (k + 1) * rows, :].astype(F32) * column
                    ).astype(BF)
                    offset += rows
            plain = rights if scale_left else lefts

            def tile(i, carry):
                cols = at(i * 512, 512)
                other = jnp.concatenate([p[:, cols] for p in plain], axis=0)
                if by_column:
                    out[:, cols] = dot_tn(scaled[...], other)
                else:
                    out[cols, :] = dot_tn(other, scaled[...])
                return carry

            lax.fori_loop(0, D // 512, tile, 0)

        total = sum(a.shape[0] for a in left)
        (result,) = run(
            body,
            [shaped(shape, F32)],
            slot_pieces + list(left) + list(right),
            [pltpu.VMEM((total, FF), BF)],
        )
        return result

    kept = list(zip(rest_kept, last_kept, far_kept))
    x_kept, y_kept, hid_kept, dg_kept, du_kept = kept

    back_parts = {}
    a, b, c = last_pair
    back_parts[a], back_parts[b], back_parts[c] = mix(last_pair, last_back)
    arrive(far_back)
    slot_gates[1:] = gate(*slot_gates[1:])
    far_top, far_bottom = mix(far[2:], far_back, split=True, first=2)
    back = Reduce(ring, chain, far_top, far_bottom)
    slot_pieces = [slot_gates[0]] + [swap(slot_gates[k], k, S) for k in range(1, S)]
    back_parts[far[0]], back_parts[far[1]] = mix(far[:2], far_back)

    def back_step():
        back.step(back_parts[back.left], back_parts[N - back.left])

    back_step()
    arrive(slot_pieces)
    grads = [
        lambda: row_grad(x_kept, dg_kept, False, (D, FF), False),
        lambda: row_grad(x_kept, du_kept, False, (D, FF), False),
    ]
    done_grads = []
    for i in range(len(near_pairs) - 1):
        near_back[i] = exchange(near_back[i])
        if grads:
            done_grads.append(grads.pop(0)())
        arrive(near_back[i])
        if i + 2 == len(near_pairs):
            far_front = exchange(far_front)
        mix_and_step(back, near_pairs[i], near_back[i])
    if grads:
        done_grads.append(grads.pop(0)())
    while back.left > 0:
        back_step()
    grad_gate, grad_up = done_grads
    arrive(far_front)
    y_parts = {}
    y_parts[far[0]], y_parts[far[1]], y_top, y_bottom = mix(far, far_front, split=True)
    back.ahead, back.behind, y_top, y_bottom = gate(back.ahead, back.behind, y_top, y_bottom)
    front = Reduce(ring, chain, y_top, y_bottom)

    extra_rows = -(-(E // 8 * slab + slab) // D) * 8

    def tokens_body(own, ahead, behind, x2, g2, router, gates, hidden, dy_, dx2, da, small):
        total = own[...] + ahead[...].astype(F32) + behind[...].astype(F32)
        gated = total[:, D:]
        dl = gated - gates[...] * jnp.sum(gated, axis=1, keepdims=True)
        grad = total[:, :D] + dot(dl[:, :E], router[...].astype(F32), EXACT)
        small[0:E, :] = dot_tn(dl, hidden[...].astype(F32), EXACT)[:E]
        scale = row_scale(x2[...])
        n2 = x2[...] * scale
        dn = grad * g2[...]
        small[E : E + 8, :] = jnp.broadcast_to(
            jnp.sum(grad * n2, axis=0, keepdims=True), (8, D)
        )
        out = dy_[...].astype(F32) + scale * (
            dn - n2 * jnp.mean(dn * n2, axis=-1, keepdims=True)
        )
        dx2[...] = out
        da[...] = out.astype(BF)

    grad_second, grad_attn, small_two = run(
        tokens_body,
        [shaped((T, D), F32), shaped((T, D), BF), shaped((E + 8, D), F32)],
        [
            back_parts[0],
            back.ahead,
            back.behind,
            x_second,
            gain_two,
            router_t,
            gate_own,
            h2,
            grad_low,
        ],
    )
    da_have = {0: grad_attn}
    bit = S // 2
    front_sent = False
    while bit:
        for k in sorted(da_have):
            if k:
                (da_have[k],) = gate(da_have[k])
            da_have[k ^ bit] = swap(da_have[k], bit, S)
        if bit == S // 2:
            front.step(y_parts[half - 1], y_parts[N - half + 1])
        elif not front_sent:
            (near_front,) = gate(jnp.concatenate(rest_front + last_front, axis=1))
            near_front = [all_to_all(near_front)]
            front_sent = True
        bit //= 2
    da_rows = [da_have[k] for k in range(S)]
    da_rows[1:] = gate(*da_rows[1:])

    def out_grad_body(*refs):
        m, os, rest = refs[0], refs[1 : 1 + calls], refs[1 + calls :]
        das, small, outs, full = rest[:S], rest[S], rest[S + 1 : S + N + 2], rest[S + N + 2]
        da = jnp.concatenate([a[...] for a in das], axis=0)
        if PR % 128:
            full[...] = dot_tn(jnp.concatenate([o[...] for o in os], axis=1), da)
        else:
            for i, o in enumerate(os):
                full[:, i * per_call * HD : (i + 1) * per_call * HD] = o[...]
        cut = halfway(PR + extra_rows)
        for r in range(N):
            if PR % 128:
                value = full[at(m[SPOT + r] * PR, PR), :]
            else:
                value = dot_tn(full[:, at(m[SPOT + r] * PR, PR)], da)
            place = at(m[r] * slab, slab)
            tail = [small[8 * g : 8 * (g + 1), place] for g in range(E // 8 + 1)]
            used = len(tail) * slab
            room = extra_rows // 8 * D
            if room > used:
                tail.append(jnp.zeros((8, room - used), F32))
            tail = jnp.concatenate(tail, axis=1)
            tail = [tail[:, g * D : (g + 1) * D] for g in range(extra_rows // 8)]
            if r == half:
                whole = jnp.concatenate([value] + tail, axis=0).astype(BF)
                outs[N - 1][...] = whole[:cut]
                outs[N][...] = whole[cut:]
            else:
                target = outs[r - (r > half)]
                target[0:PR, :] = value
                for g in range(extra_rows // 8):
                    target[PR + 8 * g : PR + 8 * (g + 1), :] = tail[g]

    out_cut = halfway(PR + extra_rows)
    *out_list, out_top, out_bottom = run(
        out_grad_body,
        [shaped((PR + extra_rows, D), F32)] * (N - 1)
        + [shaped((out_cut, D), BF), shaped((PR + extra_rows - out_cut, D), BF)],
        [meta_s] + attended + da_rows + [small_two],
        [pltpu.VMEM((QC, D), F32) if PR % 128 else pltpu.VMEM((L, QC), BF)],
    )
    out_parts = {r: out_list[r - (r > half)] for r in range(N) if r != half}
    out_walk = Reduce(ring, chain, out_top, out_bottom)

    def both_steps():
        if out_walk.left > 0:
            out_walk.step(out_parts[out_walk.left], out_parts[N - out_walk.left])

    def do_body(*refs):
        m, das, rest = refs[0], refs[1 : 1 + S], refs[1 + S :]
        parts = regroup(rest, out_blocks)
        do, full, sems = rest[sum(len(b) for b in out_blocks) :]
        for c in fetch_out(m, parts, full, sems):
            c.wait()
        da = jnp.concatenate([a[...] for a in das], axis=0)
        wide = 256 if QC % 256 == 0 else 128

        def tile(i, carry):
            do[:, at(i * wide, wide)] = dot_nt(da, full[at(i * wide, wide), :]).astype(BF)
            return carry

        lax.fori_loop(0, QC // wide, tile, 0)

    (grad_heads,) = run(
        do_body,
        [shaped((L, QC), BF)],
        [meta_s] + da_rows + [("a", b) for b in flat(out_blocks)],
        [pltpu.VMEM((QC, D), BF), pltpu.SemaphoreType.DMA((N, 2))],
    )
    front.ahead, front.behind = gate(front.ahead, front.behind)
    out_walk.step(out_parts[out_walk.left], out_parts[N - out_walk.left])

    def back_body(first_head, count):
        def body(raw_in, rot_in, do_in, krot, vlow, bias_, gq, cos, sin, dk0, dv0, gain0, *rest):
            dq, dk, dv, gain, raw, rot, do, sems = rest
            lanes_here = pl.ds(first_head * HD, count * HD)
            copies = [
                pltpu.make_async_copy(raw_in.at[:, lanes_here], raw, sems.at[0]),
                pltpu.make_async_copy(rot_in, rot, sems.at[1]),
                pltpu.make_async_copy(do_in.at[:, lanes_here], do, sems.at[2]),
            ]
            for c in copies:
                c.start()
            dk[...] = dk0[...]
            dv[...] = dv0[...]
            gain[...] = gain0[...]
            for c in copies:
                c.wait()

            def head(h, carry):
                lanes = at(h * HD, HD)
                q = rot[:, lanes]
                grad = do[:, lanes]
                p = weights_of(q, krot[...], bias_[...])
                dp = dot_nt(grad, vlow[...])
                centre = jnp.sum(p * dp, axis=-1, keepdims=True)
                ds = (p * (dp - centre)).astype(BF)
                scale = HD ** (-0.5)
                dk[...] += dot_tn(ds, q) * scale
                dv[...] += dot_tn(p.astype(BF), grad)
                dqr = (dot(ds, krot[...]) * scale).astype(BF).astype(F32)
                dqn = turn(dqr, cos[...], -sin[...])
                q_raw = raw[:, lanes]
                factor = row_scale(q_raw)
                nq = q_raw * factor
                gain[0:1, :] += jnp.sum(dqn * nq, axis=0, keepdims=True)
                dn = dqn * gq[0:1, :]
                dq[:, lanes] = (
                    factor * (dn - nq * jnp.mean(dn * nq, axis=-1, keepdims=True))
                ).astype(BF)
                return carry

            lax.fori_loop(0, count, head, 0)

        return body

    grad_k, grad_v = jnp.zeros((L, HD), F32), jnp.zeros((L, HD), F32)
    gain_sum = jnp.zeros((8, 128), F32)
    grad_q = []
    for i in range(calls):
        dq, grad_k, grad_v, gain_sum = run(
            back_body(i * per_call, per_call),
            [
                shaped((L, per_call * HD), BF),
                shaped((L, HD), F32),
                shaped((L, HD), F32),
                shaped((8, 128), F32),
            ],
            [("a", qkv), ("a", q_rot[i]), ("a", grad_heads)]
            + [k_rot, v_low, bias, gain_qk, cosines, sines, grad_k, grad_v, gain_sum],
            [
                pltpu.VMEM((L, per_call * HD), F32),
                pltpu.VMEM((L, per_call * HD), BF),
                pltpu.VMEM((L, per_call * HD), BF),
                pltpu.SemaphoreType.DMA((3,)),
            ],
        )
        grad_q.append(dq)
        both_steps()
    while out_walk.left > 0:
        both_steps()

    def final_y_body(x2, own, ahead, behind, out):
        out[...] = (
            x2[...] + own[...] + ahead[...].astype(F32) + behind[...].astype(F32)
        ).astype(BF)

    if replicas > 1:
        both = jnp.concatenate([grad_k, grad_v], axis=1).astype(BF).astype(F32)
        bit = 1
        while bit < replicas:
            both = both + swap(both.astype(BF), bit, S).astype(F32)
            bit *= 2
        grad_k, grad_v = both[:, :HD], both[:, HD:]

    def key_body(dk, dv, raw_in, gq, cos, sin, gain, dkv, gains, raw, sem):
        c = pltpu.make_async_copy(raw_in.at[:, pl.ds(QC, HD)], raw, sem)
        c.start()
        c.wait()
        k_raw = raw[...]
        factor = row_scale(k_raw)
        nk = k_raw * factor
        dkn = turn(dk[...].astype(BF).astype(F32), cos[...], -sin[...])
        k_part = jnp.sum(dkn * nk, axis=0, keepdims=True) * (1.0 / replicas)
        dn = dkn * gq[1:2, :]
        dk_raw = factor * (dn - nk * jnp.mean(dn * nk, axis=-1, keepdims=True))
        dkv[:, 0:HD] = dk_raw.astype(BF)
        dkv[:, HD:] = dv[...].astype(BF)
        line = iota((8, 128), 0)
        gains[...] = jnp.where(line == 0, gain[0:1, :], jnp.where(line == 1, k_part, 0.0))

    grad_kv, gain_lines = run(
        key_body,
        [shaped((L, 2 * HD), BF), shaped((8, 128), F32)],
        [grad_k, grad_v, ("a", qkv), gain_qk, cosines, sines, gain_sum],
        [pltpu.VMEM((L, HD), F32), pltpu.SemaphoreType.DMA],
    )

    block_rows = slab + 8
    block_cut = halfway(block_rows)

    def weight_grad(offsets, split=False):
        def body(m, h, *rest):
            dqs, rest = rest[:calls], rest[calls:]
            dkv, gains, outs = rest[0], rest[1], rest[2:]
            span = per_call * HD
            for j, r in enumerate(offsets):
                rows = h[:, at(m[r] * slab, slab)]
                pieces = [dot_tn(rows, dq[...]) for dq in dqs] + [dot_tn(rows, dkv[...])]
                spots = [slice(i * span, (i + 1) * span) for i in range(calls)]
                spots.append(slice(QC, C))
                tail = jnp.concatenate([gains[...], jnp.zeros((8, C - 128), F32)], axis=1)
                for spot_, piece_ in zip(spots, pieces):
                    if split:
                        outs[0][:, spot_] = piece_[:block_cut].astype(BF)
                        low = jnp.concatenate([piece_[block_cut:], tail[:, spot_]], axis=0)
                        outs[1][:, spot_] = low.astype(BF)
                    else:
                        outs[j][0:slab, spot_] = piece_
                if not split:
                    outs[j][slab:, :] = tail

        if split:
            shapes = [shaped((block_cut, C), BF), shaped((block_rows - block_cut, C), BF)]
        else:
            shapes = [shaped((block_rows, C), F32)] * len(offsets)
        return run(body, shapes, [meta_s, h1] + grad_q + [grad_kv, gain_lines])

    def total_body(own, ahead, behind, *outs):
        total = own[...] + ahead[...].astype(F32) + behind[...].astype(F32)
        start = 0
        for out in outs:
            out[...] = total[start : start + out.shape[0]].astype(BF)
            start += out.shape[0]

    out_piece, out_tail = run(
        total_body,
        [shaped((PR, D), BF), shaped((extra_rows, D), BF)],
        [out_parts[0], out_walk.ahead, out_walk.behind],
    )
    block_top, block_bottom = weight_grad([half], split=True)
    block_walk = Reduce(ring, chain, block_top, block_bottom)
    block_parts = {}

    def more_blocks(offsets):
        block_parts.update(zip(offsets, weight_grad(offsets)))

    def block_step():
        block_walk.step(block_parts[block_walk.left], block_parts[N - block_walk.left])

    more_blocks([half - 1, N - half + 1])
    block_step()
    more_blocks([r for r in range(N) if r not in block_parts and r != half])
    def make_first():
        def body(*refs):
            m, dqs, rest = refs[0], refs[1 : 1 + calls], refs[1 + calls :]
            dkv, rest = rest[0], rest[1:]
            blk = regroup(rest, blocks)
            rest = rest[sum(len(b) for b in blocks) :]
            outs, (full, sems) = rest[:S], rest[S:]
            copies = []
            for r in range(N):
                copies += fetch_block(m, blk[r], r, full, sems)
            share = (dkv[...].astype(F32) * (1.0 / replicas)).astype(BF)
            for c in copies:
                c.wait()
            span = per_call * HD

            def tile(i, carry):
                lanes = at(i * 512, 512)
                value = dot_nt(share, full[lanes, QC:])
                for j in range(calls):
                    value += dot_nt(dqs[j][...], full[lanes, j * span : (j + 1) * span])
                for j, k in enumerate(range(1, S, 2)):
                    outs[j][:, lanes] = value[k * T : (k + 1) * T].astype(BF)
                for j, k in enumerate(range(0, S, 2)):
                    outs[S // 2 + j][:, lanes] = value[k * T : (k + 1) * T]
                return carry

            lax.fori_loop(0, D // 512, tile, 0)

        result = run(
            body,
            reduce_shapes,
            [meta_s] + grad_q + [grad_kv] + [("a", b) for b in flat(blocks)],
            [pltpu.VMEM((D, C), BF), pltpu.SemaphoreType.DMA((N, 2))],
        )
        return result[: S // 2], result[S // 2 :]

    def send_pieces():
        (moved,) = gate(out_piece)
        return lax.ppermute(moved, ("seq", "shard"), [(b, a) for a, b in spread])

    one_own, one_got = seq_reduce(make_first, block_step)
    while block_walk.left > 0:
        block_step()
    near_front[:] = gate(*near_front)
    for r, part in zip(near, mix(near, near_front)):
        y_parts[r] = part
    front.step(y_parts[front.left], y_parts[N - front.left])

    def inputs_body(x_ref, own, got, g1, dx2, out):
        x = x_ref[...].astype(F32)
        grad = own[...] + got[...].astype(F32)
        scale = row_scale(x)
        n1 = x * scale
        dn = grad * g1[...]
        out[...] = dx2[...] + scale * (
            dn - n1 * jnp.mean(dn * n1, axis=-1, keepdims=True)
        )

    (grad_inputs,) = run(
        inputs_body,
        [shaped((T, D), F32)],
        [inputs[0], one_own, one_got, gain_one, grad_second],
    )

    (block_sum,) = run(
        total_body,
        [shaped((block_rows, C), BF)],
        [block_parts[0], block_walk.ahead, block_walk.behind],
    )
    bit = S // 2
    block_have = {0: block_sum, bit: swap(block_sum, bit, S)}
    out_piece = send_pieces()
    grad_down = row_grad(hid_kept, y_kept, True, (FF, D), True)
    while front.left > 0:
        front.step(y_parts[front.left], y_parts[N - front.left])
    tail_have = {0: out_tail, bit: swap(out_tail, bit, S)}
    while bit > 1:
        bit //= 2
        for have in (block_have, tail_have):
            for k in sorted(have):
                if k:
                    (have[k],) = gate(have[k])
                have[k ^ bit] = swap(have[k], bit, S)
    block_pieces = [block_have[k] for k in range(S)]
    tail_pieces = [tail_have[k] for k in range(S)]
    bit = S // 2
    (out_piece,) = gate(out_piece)
    out_have = {0: out_piece, bit: swap(out_piece, bit, S)}

    def join_body(*refs):
        m, pieces = refs[0], refs[1 : 1 + S]
        wq, wk, wv, oq, ok, ov, gains, rows = refs[1 + S :]
        for k in range(S):
            source = m[SRC + k]
            oq[:, at(source * QC, QC)] = pieces[k][0:slab, 0:QC].astype(F32)
            lanes = at(source // replicas * HD, HD)
            ok[:, lanes] = pieces[k][0:slab, QC : QC + HD].astype(F32)
            ov[:, lanes] = pieces[k][0:slab, QC + HD :].astype(F32)
        total = jnp.sum(oq[...] * wq[...].astype(F32), axis=1, keepdims=True)
        total += jnp.sum(ok[...] * wk[...].astype(F32), axis=1, keepdims=True)
        total += jnp.sum(ov[...] * wv[...].astype(F32), axis=1, keepdims=True)
        same = iota((slab, slab), 0) == iota((slab, slab), 1)
        rows[...] = jnp.broadcast_to(
            jnp.sum(jnp.where(same, total, 0.0), axis=0, keepdims=True), (8, slab)
        )
        gains[...] = tree_sum([p[slab:, 0:128].astype(F32) for p in pieces])

    grad_query, grad_key, grad_value, gain_rows, one_rows = run(
        join_body,
        [
            shaped((slab, S * QC), F32),
            shaped((slab, KEY_VALUE_HEADS * HD), F32),
            shaped((slab, KEY_VALUE_HEADS * HD), F32),
            shaped((8, 128), F32),
            shaped((8, slab), F32),
        ],
        [meta_s] + block_pieces + [w_query, key_weight, value_weight],
    )
    (result,) = run(
        final_y_body,
        [shaped((T, D), BF)],
        [x_second, y_parts[0], front.ahead, front.behind],
    )
    while bit > 1:
        bit //= 2
        for k in sorted(out_have):
            if k:
                (out_have[k],) = gate(out_have[k])
            out_have[k ^ bit] = swap(out_have[k], bit, S)
    out_pieces = [out_have[k] for k in range(S)]

    def out_join_body(*refs):
        m, pieces, tails = refs[0], refs[1 : 1 + S], refs[1 + S : 1 + 2 * S]
        out, small = refs[1 + 2 * S :]
        for k in range(S):
            out[at(m[QUA + k] * PR, PR), :] = pieces[k][...].astype(F32)
        small[...] = tree_sum([t_[...].astype(F32) for t_ in tails])

    grad_out_w, tail_two = run(
        out_join_body,
        [shaped((S * PR, D), F32), shaped((extra_rows, D), F32)],
        [meta_s] + out_pieces + tail_pieces,
    )

    grad_gain_one = one_rows[0] / norm1_gain.astype(F32)
    share = HD // N
    grad_qgain = lax.dynamic_slice(gain_rows[0], (d * share,), (share,))
    grad_kgain = lax.dynamic_slice(gain_rows[1], (d * share,), (share,))

    lines = [
        tail_two[8 * g : 8 * (g + 1), i * slab : (i + 1) * slab]
        for g in range(extra_rows // 8)
        for i in range(D // slab)
    ]
    grad_router = jnp.concatenate(lines[: E // 8], axis=0).T
    grad_gain_two = lines[E // 8][0]

    grad_gain_two = grad_gain_two + chain.token[0, 0]

    return (
        result[None],
        grad_inputs[None],
        grad_gain_one,
        grad_query,
        grad_key,
        grad_value,
        grad_qgain,
        grad_kgain,
        grad_out_w,
        grad_gain_two,
        grad_router,
        grad_gate[None],
        grad_up[None],
        grad_down[None],
    )


def solution(mesh):
    in_specs = (
        P("shard", "seq", None),
        P("shard", "seq"),
        P("shard", "seq", None),
        P("shard"),
        P("shard", None),
        P("shard", None),
        P("shard", None),
        P("shard"),
        P("shard"),
        P("shard", None),
        P("shard"),
        P("shard", None),
        P(("seq", "shard"), None, None),
        P(("seq", "shard"), None, None),
        P(("seq", "shard"), None, None),
        P("shard", "seq", None),
    )
    out_specs = (
        P("shard", "seq", None),
        P("shard", "seq", None),
        P("shard"),
        P("shard", None),
        P("shard", None),
        P("shard", None),
        P("shard"),
        P("shard"),
        P("shard", None),
        P("shard"),
        P("shard", None),
        P(("seq", "shard"), None, None),
        P(("seq", "shard"), None, None),
        P(("seq", "shard"), None, None),
    )
    return jax.shard_map(
        per_device, mesh=mesh, in_specs=in_specs, out_specs=out_specs, check_vma=False
    )
```
